256 devices in a mesh: dp: 64 (over y, z, core), rep: 4 (over x).
Axes of the slice: x: 4, y: 4, z: 8, core: 2. Of those that a mesh axis runs over, the one named last changes fastest.
Arguments:
- embeddings: bfloat16 [262144, 768], P(('dp', 'rep'))
- cluster_ids: int32 [262144], P(('dp', 'rep')), may hold values from 0 to 127, as said below
- member_order: int32 [262144], P(('dp', 'rep')), may hold values from 0 to 4095, as said below
Outputs:
- earlier_max: float32 [262144], P(('dp', 'rep'))
The draws below stay inside these ranges and needn't reach their ends.
Inputs may be any that keep to these rules, and one draw needn't show every extreme that they name: `cluster_ids`: clusters come in groups of 2 consecutive ids. In the rows of one device (aligned blocks of 1024 rows) at most 32 rows name clusters of one group; one group, the same in every block, is named by exactly 32 rows of every block. A cluster has at most 4096 rows, and the clusters of that group have exactly 4096; a cluster may have none. `member_order`: within every cluster the rows carry the orders 0 to its size - 1, each once.
All inputs are finite; a program needn't handle non-finite values.
Results may differ from the reference program's by a relative error of at most 0.00074.
Values may be sent and summed in bfloat16 or wider, within the bound.
No kernel may reach another device: no remote copies, remote signals or barrier semaphores. Data moves between devices by JAX's collectives and lax.ppermute only.
A program may use at most 128 MiB of HBM per device.

```python
import math
import jax
import jax.numpy as jnp
from jax import lax

D = 768
ROW_DEV = 1024
CL_OWN = 2
CLUSTERS = 128
SLOT = 4096
CAP = 32
ROWS = 262144


def layout(key):
    owners = CLUSTERS // CL_OWN
    sources = ROWS // ROW_DEV
    half_cap = CAP // 2
    subkeys = jax.random.split(key, 6)
    busiest = jax.random.randint(subkeys[0], (), 0, owners, dtype=jnp.int32)
    shuffled = jax.vmap(lambda one_key: jax.random.permutation(one_key, owners))(jax.random.split(subkeys[1], sources)).astype(jnp.int32)
    leading = shuffled[:, :1]
    owner_order = jnp.where(shuffled == busiest, leading, shuffled)
    owner_order = owner_order.at[:, 0].set(busiest)
    swing_size = jax.random.randint(subkeys[2], (sources, owners // 2), 0, half_cap + 1, dtype=jnp.int32)
    swing_size = swing_size.at[:, 0].set(half_cap)
    source_index = jnp.arange(sources, dtype=jnp.int32)[:, None]
    counts = jnp.zeros((sources, owners), jnp.int32)
    counts = counts.at[source_index, owner_order[:, 0::2]].set(half_cap + swing_size)
    counts = counts.at[source_index, owner_order[:, 1::2]].set(half_cap - swing_size)
    bounds = jnp.cumsum(counts, axis=1)
    within = jnp.arange(ROW_DEV, dtype=jnp.int32)
    sorted_owner = jnp.sum((within[None, :, None] >= bounds[:, None, :]).astype(jnp.int32), axis=2)
    mixing = jax.vmap(lambda one_key: jax.random.permutation(one_key, ROW_DEV))(jax.random.split(subkeys[3], sources)).astype(jnp.int32)
    row_owner = jnp.take_along_axis(sorted_owner, mixing, axis=1).reshape(ROWS).astype(jnp.int32)
    priority = jax.random.permutation(subkeys[4], ROWS).astype(jnp.int32)
    ranking = jnp.argsort(row_owner * ROWS + priority, stable=True).astype(jnp.int32)
    owner_load = jnp.sum(counts, axis=0).astype(jnp.int32)
    owner_start = jnp.cumsum(owner_load) - owner_load
    owner_rank = jnp.zeros((ROWS,), jnp.int32).at[ranking].set(jnp.arange(ROWS, dtype=jnp.int32) - owner_start[row_owner[ranking]])
    cut_low = jnp.maximum(owner_load - SLOT, 0)
    cut_high = jnp.minimum(owner_load, SLOT)
    cut_point = jax.random.randint(subkeys[5], (owners,), cut_low, cut_high + 1, dtype=jnp.int32)
    cut_here = cut_point[row_owner]
    second = (owner_rank >= cut_here).astype(jnp.int32)
    member = (owner_rank - second * cut_here).astype(jnp.int32)
    cluster = (row_owner * CL_OWN + second).astype(jnp.int32)
    return (cluster, member)


def draw_cluster_ids(key, part):
    cluster, member = layout(key)
    return cluster


def draw_member_order(key, part):
    cluster, member = layout(key)
    return member


def draw_embeddings(key, part):
    cluster, member = layout(key)
    key = jax.random.fold_in(key, 11)
    subkeys = jax.random.split(key, 4)
    base_rows = jax.random.normal(subkeys[0], (ROWS, D), jnp.float32)
    row_scale = jnp.exp(jax.random.uniform(subkeys[1], (ROWS, 1), jnp.float32, 0.0, math.log(10.0)))
    column_scale = jnp.exp(jax.random.uniform(subkeys[2], (1, D), jnp.float32, 0.0, math.log(10.0)))
    slot_table = jnp.zeros((CLUSTERS * SLOT,), jnp.int32).at[cluster * SLOT + member].set(jnp.arange(ROWS, dtype=jnp.int32))
    earlier_row = slot_table[cluster * SLOT + jnp.maximum(member - 1, 0)]
    copied = jax.random.bernoulli(subkeys[3], 0.25, (ROWS, 1)) & (member >= 1)[:, None]
    mixed_rows = base_rows + jnp.where(copied, 2.0 * base_rows[earlier_row], 0.0)
    return (mixed_rows * column_scale * row_scale).astype(jnp.bfloat16)


def setup_inputs(seed: int = 0) -> dict:
    seeds = jax.random.split(jax.random.key(seed), 4)
    embeddings = draw_embeddings(jax.random.fold_in(seeds[3], 71), 0)
    cluster_ids = draw_cluster_ids(jax.random.fold_in(seeds[3], 71), 0)
    member_order = draw_member_order(jax.random.fold_in(seeds[3], 71), 0)
    return dict(embeddings=embeddings, cluster_ids=cluster_ids, member_order=member_order)


def reference(embeddings, cluster_ids, member_order):
    wide_rows = embeddings.astype(jnp.float32)
    unit_rows = (wide_rows / jnp.sqrt(lax.optimization_barrier(jnp.sum(wide_rows * wide_rows, axis=1, keepdims=True)) + 1e-06)).astype(jnp.bfloat16)
    slot_of_row = (cluster_ids * SLOT + member_order).astype(jnp.int32)
    row_of_slot = jnp.full((CLUSTERS * SLOT,), -1, jnp.int32).at[slot_of_row].set(jnp.arange(ROWS, dtype=jnp.int32))
    slot_table = row_of_slot.reshape(CLUSTERS, SLOT)
    position = jnp.arange(SLOT, dtype=jnp.int32)
    earlier = position[None, :] < position[:, None]

    def one_cluster(slot_rows):
        members = unit_rows[jnp.maximum(slot_rows, 0)]
        members = jnp.where((slot_rows >= 0)[:, None], members, jnp.zeros_like(members))
        similar = jnp.dot(members, members.T, preferred_element_type=jnp.float32)
        return lax.optimization_barrier(jnp.max(jnp.where(earlier, similar, jnp.float32(-1.0)), axis=1))
    best_match = lax.map(one_cluster, slot_table)
    return best_match.reshape(-1)[slot_of_row]
```

```python
import functools

import jax
import jax.numpy as jnp
import numpy as np
from jax import lax
from jax.experimental import pallas as pl
from jax.experimental.pallas import tpu as pltpu
from jax.sharding import PartitionSpec as P

AXES = ("dp", "rep")
NX, NY, NZ = 4, 4, 8
CHIPS = NX * NY * NZ
GROUPS = 64
HALF = GROUPS // 2
SUB = 8
ROWS = 1024
D = 768
KEYS = 128
WIDE = D + KEYS
HALF_ROWS = 512
ORDERS = 4096
VMEM = 56 * 1024 * 1024


def device(x, y, z, core):
    return ((y * NZ + z) * 2 + core) * NX + x


SAME_CORE = [
    [device(x, y, z, core) for y in range(NY) for z in range(NZ) for x in range(NX)] for core in range(2)
]


def ring(step):
    pairs = []
    for y in range(NY):
        for z in range(NZ):
            for x in range(NX):
                pairs.append((device(x, y, z, 0), device((x + step) % NX, y, z, 0)))
                pairs.append((device(x, y, z, 1), device(x, (y + step) % NY, z, 1)))
    return pairs


SIBLING = [(dp * NX + x, (dp ^ 1) * NX + x) for dp in range(NY * NZ * 2) for x in range(NX)]


def exchange(rows):
    return lax.all_to_all(
        rows, AXES, split_axis=0, concat_axis=0, tiled=True, axis_index_groups=SAME_CORE
    )


def send(rows, pairs):
    return lax.ppermute(rows, AXES, pairs)


def cost(flops, size):
    return pl.CostEstimate(flops=flops, bytes_accessed=size, transcendentals=0)


def chip_of(group, place):
    core = (group >= HALF).astype(jnp.int32)
    inner = group - HALF * core
    on_x = inner * NX + place
    on_y = (place * NZ + (inner & (NZ - 1))) * NX + (inner >> 3)
    return jnp.where(core == 0, on_x, on_y), core


def key_rows(ids, order, first):
    key = (ids & 1) * ORDERS + order
    which = lax.broadcasted_iota(jnp.int32, (KEYS, ids.shape[1]), 0)
    high, low = (key >> 7) + 1, key & 127
    return jnp.where(which == first, high, jnp.where(which == first + 1, low, 0)).astype(jnp.float32).astype(
        jnp.bfloat16
    )


def slots_of(info, core, mine):
    group, rank = info[0:1], info[1:2]
    chip, serving = chip_of(group, rank & 3)
    slot = chip * SUB + (rank >> 2)
    return jnp.where((serving == core) if mine else (serving != core), slot, -1)


def onehot(slot):
    rows = lax.broadcasted_iota(jnp.int32, (ROWS, ROWS), 0)
    return jnp.where(rows == slot, 1.0, 0.0).astype(jnp.bfloat16)


def prep_kernel(place_ref, emb_ref, ids_ref, order_ref, unit_ref, box_ref, slab_ref, info_ref):
    ids, order = ids_ref[...], order_ref[...]
    group = ids >> 1
    member = (lax.broadcasted_iota(jnp.int32, (GROUPS, ROWS), 0) == group)
    hot = jnp.where(member, 1.0, 0.0)
    step = 256
    earlier = jnp.where(
        lax.broadcasted_iota(jnp.int32, (step, step), 0) < lax.broadcasted_iota(jnp.int32, (step, step), 1), 1.0, 0.0
    ).astype(jnp.bfloat16)
    before = jnp.zeros((GROUPS, 1), jnp.float32)
    ranks = []
    for part in range(ROWS // step):
        here = hot[:, part * step : (part + 1) * step]
        count = jnp.dot(here.astype(jnp.bfloat16), earlier, preferred_element_type=jnp.float32) + before
        ranks.append(jnp.sum(here * count, axis=0, keepdims=True))
        before = before + jnp.sum(here, axis=1, keepdims=True)
    rank = jnp.concatenate(ranks, axis=1).astype(jnp.int32)
    which = lax.broadcasted_iota(jnp.int32, (8, ROWS), 0)
    info = jnp.where(which == 0, group, jnp.where(which == 1, rank, 0))
    info_ref[...] = info

    wide = emb_ref[...].astype(jnp.float32)
    scale = 1.0 / jnp.sqrt(jnp.sum(wide * wide, axis=1, keepdims=True) + 1e-06)
    unit = (wide * scale).astype(jnp.bfloat16)
    unit_ref[...] = unit

    pick = onehot(slots_of(info, place_ref[0], True))
    box_ref[...] = jnp.dot(pick, unit, preferred_element_type=jnp.float32).astype(jnp.bfloat16)
    slab_ref[...] = lax.dot_general(
        pick, key_rows(ids, order, 2), (((1,), (1,)), ((), ())), preferred_element_type=jnp.float32
    ).astype(jnp.bfloat16)


def prep(place, embeddings, ids, order):
    return pl.pallas_call(
        prep_kernel,
        out_shape=(
            jax.ShapeDtypeStruct((ROWS, D), jnp.bfloat16),
            jax.ShapeDtypeStruct((ROWS, D), jnp.bfloat16),
            jax.ShapeDtypeStruct((ROWS, KEYS), jnp.bfloat16),
            jax.ShapeDtypeStruct((8, ROWS), jnp.int32),
        ),
        in_specs=[pl.BlockSpec(memory_space=pltpu.SMEM)] + [pl.BlockSpec(memory_space=pltpu.VMEM)] * 3,
        out_specs=tuple([pl.BlockSpec(memory_space=pltpu.VMEM)] * 4),
        compiler_params=pltpu.CompilerParams(vmem_limit_bytes=VMEM),
        cost_estimate=cost(2 * ROWS * ROWS * WIDE, 6 * ROWS * D),
        name="prep",
    )(place, embeddings, ids, order)


def hand_kernel(place_ref, unit_ref, info_ref, ids_ref, order_ref, box_ref):
    pick = onehot(slots_of(info_ref[...], place_ref[0], False))
    box_ref[:, :D] = jnp.dot(pick, unit_ref[...], preferred_element_type=jnp.float32).astype(jnp.bfloat16)
    box_ref[:, D:] = lax.dot_general(
        pick,
        key_rows(ids_ref[...], order_ref[...], 0),
        (((1,), (1,)), ((), ())),
        preferred_element_type=jnp.float32,
    ).astype(jnp.bfloat16)


def hand(place, unit, info, ids, order):
    return pl.pallas_call(
        hand_kernel,
        out_shape=jax.ShapeDtypeStruct((ROWS, WIDE), jnp.bfloat16),
        in_specs=[pl.BlockSpec(memory_space=pltpu.SMEM)] + [pl.BlockSpec(memory_space=pltpu.VMEM)] * 4,
        out_specs=pl.BlockSpec(memory_space=pltpu.VMEM),
        compiler_params=pltpu.CompilerParams(vmem_limit_bytes=VMEM),
        cost_estimate=cost(2 * ROWS * ROWS * WIDE, 4 * ROWS * D),
        name="hand",
    )(place, unit, info, ids, order)


def stamp_kernel(box_ref, slab_ref, out_ref):
    out_ref[...] = box_ref[...] + slab_ref[...]


def stamp(box, slab):
    return pl.pallas_call(
        stamp_kernel,
        grid=(1,),
        out_shape=jax.ShapeDtypeStruct(box.shape, box.dtype),
        in_specs=[
            pl.BlockSpec((ROWS, KEYS), lambda i: (0, D // KEYS)),
            pl.BlockSpec((ROWS, KEYS), lambda i: (0, 0)),
        ],
        out_specs=pl.BlockSpec((ROWS, KEYS), lambda i: (0, D // KEYS)),
        input_output_aliases={0: 0},
        compiler_params=pltpu.CompilerParams(vmem_limit_bytes=VMEM),
        cost_estimate=cost(0, 3 * 2 * ROWS * KEYS),
        name="stamp",
    )(box, slab)


BLOCKS = [(part, far, chunk) for far in range(3) for chunk in range(2) for part in "PM"]
SLOT = {block: number for number, block in enumerate(BLOCKS)}


def pair_lists():
    pairs, by_place = [], []

    def all_chunks(one, other):
        for c in range(2):
            for e in range(2):
                pairs.append((one + (c,), other + (e,)))

    for part in "PM":
        pairs.append(((part, 0, 0), (part, 0, 1)))
        all_chunks((part, 0), (part, 1))
        pairs.append(((part, 0, 1), (part, 2, 0)))
        early = ((part, 0, 0), (part, 2, 0))
        late = ((part, 0, 1), (part, 2, 1))
        by_place.append((early, late) if part == "P" else (late, early))
    all_chunks(("P", 0), ("M", 0))
    all_chunks(("P", 0), ("M", 1))
    all_chunks(("P", 1), ("M", 1))
    pairs.append((("P", 1, 0), ("M", 2, 0)))
    pairs.append((("P", 1, 1), ("M", 2, 0)))
    pairs.append((("P", 2, 0), ("M", 1, 1)))
    pairs.append((("P", 1, 1), ("M", 2, 1)))
    return pairs, by_place


def similar_kernel(loads, used, n_self, n_pairs, n_before, *refs):
    n_arrays = 1 + max(load[0] for load in loads)
    selfs_ref, pairs_ref = refs[:2]
    arrays = refs[2 : 2 + n_arrays]
    befores = refs[2 + n_arrays : 2 + n_arrays + n_before]
    out_ref = refs[2 + n_arrays + n_before]
    rows, slabs, kcol, ccol, krow, crow, best_row, best_col, sems = refs[3 + n_arrays + n_before :]

    copies = []
    for number, (array, first, columns, slot) in enumerate(loads):
        source = arrays[array].at[pl.ds(first, HALF_ROWS), pl.ds(columns, KEYS if columns else D)]
        target = slabs.at[slot] if columns else rows.at[slot]
        copy = pltpu.make_async_copy(source, target, sems.at[number])
        copy.start()
        copies.append((copy, bool(columns)))
    for slot in used:
        best_row[slot] = jnp.full((HALF_ROWS, 128), -1.0, jnp.float32)
        best_col[slot] = jnp.full((8, HALF_ROWS), -1.0, jnp.float32)
    for copy, is_key in copies:
        if is_key:
            copy.wait()

    lane_of = lax.broadcasted_iota(jnp.int32, (KEYS, 128), 0)
    row_of = lax.broadcasted_iota(jnp.int32, (8, KEYS), 1)
    for slot in used:
        part, far, chunk = BLOCKS[slot]
        first = 0 if chunk == 1 else 2
        slab = slabs[SLOT[(part, far, 1)]]
        weight = jnp.where(lane_of == first, 128.0, jnp.where(lane_of == first + 1, 1.0, 0.0)).astype(jnp.bfloat16)
        key = jnp.dot(slab, weight, preferred_element_type=jnp.float32)
        kcol[slot] = key
        ccol[slot] = jnp.where(key >= ORDERS + 128, 2.0, jnp.where(key > 0, 1.0, 0.0))
        weight = jnp.where(row_of == first, 128.0, jnp.where(row_of == first + 1, 1.0, 0.0)).astype(jnp.bfloat16)
        key = lax.dot_general(weight, slab, (((1,), (1,)), ((), ())), preferred_element_type=jnp.float32)
        krow[slot] = key
        crow[slot] = jnp.where(key >= ORDERS + 128, 2.0, jnp.where(key > 0, 1.0, 0.0))
    for copy, is_key in copies:
        if not is_key:
            copy.wait()

    width = 256

    def products(a, b, start):
        return lax.dot_general(
            rows[a], rows[b, start : start + width], (((1,), (1,)), ((), ())), preferred_element_type=jnp.float32
        )

    def one_self(number, carry):
        a = selfs_ref[number]
        ka, ca = kcol[a], ccol[a]
        best = best_row[a]
        for start in range(0, HALF_ROWS, width):
            s = products(a, a, start)
            for lane in range(0, width, 128):
                at = start + lane
                kb, cb = krow[a, 0:1, at : at + 128], crow[a, 0:1, at : at + 128]
                best = jnp.maximum(
                    best, jnp.where((ca == cb) & (kb < ka), s[:, lane : lane + 128], -1.0)
                )
        best_row[a] = best
        return carry

    def one_pair(number, carry):
        a, b = pairs_ref[2 * number], pairs_ref[2 * number + 1]
        ka, ca = kcol[a], ccol[a]
        best = best_row[a]
        for start in range(0, HALF_ROWS, width):
            s = products(a, b, start)
            for lane in range(0, width, 128):
                at = start + lane
                kb, cb = krow[b, 0:1, at : at + 128], crow[b, 0:1, at : at + 128]
                same = jnp.where(ca == cb, s[:, lane : lane + 128], -1.0)
                later = kb < ka
                best = jnp.maximum(best, jnp.where(later, same, -1.0))
                other = jnp.where(later, -1.0, same).reshape(HALF_ROWS // 8, 8, 128)
                best_col[b, :, at : at + 128] = jnp.maximum(
                    best_col[b, :, at : at + 128], jnp.max(other, axis=0)
                )
        best_row[a] = best
        return carry

    if n_self:
        lax.fori_loop(0, n_self, one_self, 0)
    lax.fori_loop(0, n_pairs, one_pair, 0)

    halves = {}
    sub = lax.broadcasted_iota(jnp.int32, (HALF_ROWS // SUB, SUB, 128), 1)
    lane = lax.broadcasted_iota(jnp.int32, (HALF_ROWS // SUB, SUB, 128), 2)
    for slot in used:
        part, far, chunk = BLOCKS[slot]
        by_row = jnp.max(best_row[slot], axis=1, keepdims=True)
        by_col = jnp.max(best_col[slot], axis=0, keepdims=True)
        by_col = jnp.transpose(jnp.broadcast_to(by_col, (128, HALF_ROWS)))
        value = jnp.maximum(by_col, by_row).reshape(HALF_ROWS // SUB, SUB, 128)
        value = jnp.max(jnp.where(lane == sub + (far * 16 + chunk * SUB), value, -1.0), axis=1)
        halves[part] = jnp.maximum(halves[part], value) if part in halves else value
    for number, part in enumerate("PM"):
        at = pl.ds(number * (CHIPS // 2), CHIPS // 2)
        value = halves[part]
        for before in befores:
            value = jnp.maximum(value, before[at, :])
        out_ref[at, :] = value


def similar(arrays, loads, selfs, pairs, n_pairs, slots, befores, name):
    n_blocks = len(BLOCKS)
    used = sorted(slots)
    kernel = functools.partial(similar_kernel, loads, used, len(selfs), n_pairs, len(befores))
    return pl.pallas_call(
        kernel,
        out_shape=jax.ShapeDtypeStruct((CHIPS, 128), jnp.float32),
        in_specs=[pl.BlockSpec(memory_space=pltpu.SMEM)] * 2
        + [pl.BlockSpec(memory_space=pl.ANY)] * len(arrays)
        + [pl.BlockSpec(memory_space=pltpu.VMEM)] * len(befores),
        out_specs=pl.BlockSpec(memory_space=pltpu.VMEM),
        scratch_shapes=[
            pltpu.VMEM((n_blocks, HALF_ROWS, D), jnp.bfloat16),
            pltpu.VMEM((n_blocks, HALF_ROWS, KEYS), jnp.bfloat16),
            pltpu.VMEM((n_blocks, HALF_ROWS, 128), jnp.float32),
            pltpu.VMEM((n_blocks, HALF_ROWS, 128), jnp.float32),
            pltpu.VMEM((n_blocks, 8, HALF_ROWS), jnp.float32),
            pltpu.VMEM((n_blocks, 8, HALF_ROWS), jnp.float32),
            pltpu.VMEM((n_blocks, HALF_ROWS, 128), jnp.float32),
            pltpu.VMEM((n_blocks, 8, HALF_ROWS), jnp.float32),
            pltpu.SemaphoreType.DMA((len(loads),)),
        ],
        compiler_params=pltpu.CompilerParams(vmem_limit_bytes=VMEM),
        cost_estimate=cost(
            2 * D * HALF_ROWS * HALF_ROWS * (n_pairs + len(selfs)), 2 * len(loads) * HALF_ROWS * D
        ),
        name=name,
    )(jnp.array(selfs or [0], jnp.int32), pairs, *arrays, *befores)


def answer_kernel(place_ref, info_ref, mine_ref, sibling_ref, out_ref):
    info = info_ref[...]
    group, rank = info[0:1], info[1:2]
    core, step = place_ref[0], place_ref[2]
    values = jnp.concatenate([mine_ref[...], sibling_ref[...]], axis=0)
    device_of = lax.broadcasted_iota(jnp.int32, (2 * CHIPS, ROWS), 0)
    lane_of = lax.broadcasted_iota(jnp.int32, (128, ROWS), 0)
    best = jnp.full((1, ROWS), -1.0, jnp.float32)
    for far in range(3):
        chip, serving = chip_of(group, (rank + far * step) & 3)
        away = (serving != core).astype(jnp.int32)
        pick = jnp.where(device_of == chip + CHIPS * away, 1.0, 0.0)
        found = lax.dot_general(
            values,
            pick,
            (((0,), (0,)), ((), ())),
            preferred_element_type=jnp.float32,
            precision=lax.Precision.HIGHEST,
        )
        wanted = far * 16 + away * SUB + (rank >> 2)
        found = jnp.max(jnp.where(lane_of == wanted, found, -1.0), axis=0, keepdims=True)
        best = jnp.maximum(best, found)
    out_ref[...] = best


def answer(place, info, mine, sibling):
    return pl.pallas_call(
        answer_kernel,
        out_shape=jax.ShapeDtypeStruct((1, ROWS), jnp.float32),
        in_specs=[pl.BlockSpec(memory_space=pltpu.SMEM)] + [pl.BlockSpec(memory_space=pltpu.VMEM)] * 3,
        out_specs=pl.BlockSpec(memory_space=pltpu.VMEM),
        compiler_params=pltpu.CompilerParams(vmem_limit_bytes=VMEM),
        cost_estimate=cost(2 * 3 * 6 * 128 * 256 * ROWS, 3 * 4 * 128 * 128),
        name="answer",
    )(place, info, mine, sibling)


def local(embeddings, cluster_ids, member_order):
    dp, x = lax.axis_index("dp"), lax.axis_index("rep")
    core, z, y = dp % 2, (dp // 2) % NZ, dp // (2 * NZ)
    ring_place = jnp.where(core == 0, x, y)
    step = jnp.where((y * NZ + z) * NX + x < CHIPS // 2, 1, -1)
    place = jnp.stack([core, ring_place, step]).astype(jnp.int32)
    ids, order = cluster_ids.reshape(1, ROWS), member_order.reshape(1, ROWS)

    unit, box, slab, info = prep(place, embeddings, ids, order)
    chunk1 = exchange(box.reshape(CHIPS, SUB, D)).reshape(ROWS, D)
    handed = stamp(send(hand(place, unit, info, ids, order), SIBLING), slab)
    chunk2 = exchange(handed.reshape(CHIPS, SUB, WIDE)).reshape(ROWS, WIDE)

    arrays = {(0, 0): chunk1, (0, 1): chunk2}
    hold = {}
    for chunk, rows in enumerate((chunk1, chunk2)):
        hold["P", 0, chunk], hold["M", 0, chunk] = (rows, 0), (rows, HALF_ROWS)
        near = send(rows[:HALF_ROWS], ring(1)), send(rows[HALF_ROWS:], ring(-1))
        far = send(near[0], ring(1)), send(near[1], ring(-1))
        for part, one, two in zip("PM", near, far):
            hold[part, 1, chunk], hold[part, 2, chunk] = (one, 0), (two, 0)

    pairs, by_place = pair_lists()
    answers = []
    for stage in range(3):
        mine = [pair for pair in pairs if max(pair[0][1], pair[1][1]) == stage]
        table = [jnp.array([SLOT[a], SLOT[b]], jnp.int32) for a, b in mine]
        slots = {SLOT[block] for pair in mine for block in pair}
        if stage == 2:
            for low, high in by_place:
                table.append(
                    jnp.where(
                        ring_place < 2,
                        jnp.array([SLOT[block] for block in low], jnp.int32),
                        jnp.array([SLOT[block] for block in high], jnp.int32),
                    )
                )
                slots |= {SLOT[block] for block in low + high}
        arrays, loads = [], []

        def number_of(array):
            for number, known in enumerate(arrays):
                if known is array:
                    return number
            arrays.append(array)
            return len(arrays) - 1

        for slot in sorted(slots):
            part, far, chunk = BLOCKS[slot]
            array, first = hold[part, far, 1]
            load = (number_of(array), first, D, SLOT[part, far, 1])
            if load not in loads:
                loads.append(load)
        for slot in sorted(slots):
            array, first = hold[BLOCKS[slot]]
            loads.append((number_of(array), first, 0, slot))
        selfs = [SLOT[part, 0, chunk] for part in "PM" for chunk in range(2)] if stage == 0 else []
        answers.append(
            similar(
                arrays,
                loads,
                selfs,
                jnp.concatenate(table),
                len(table),
                slots,
                answers if stage == 2 else [],
                ("own", "near", "far")[stage],
            )
        )
    mine = exchange(answers[2].reshape(CHIPS, 1, 128)).reshape(CHIPS, 128)
    return answer(place, info, mine, send(mine, SIBLING)).reshape(ROWS)


def solution(mesh):
    return jax.shard_map(
        local,
        mesh=mesh,
        in_specs=(P(AXES, None), P(AXES), P(AXES)),
        out_specs=P(AXES),
        check_vma=False,
    )
```

```python
import functools

import jax
import jax.numpy as jnp
import numpy as np
from jax import lax
from jax.experimental import pallas as pl
from jax.experimental.pallas import tpu as pltpu
from jax.sharding import PartitionSpec as P

AXES = ("dp", "rep")
NX, NY, NZ = 4, 4, 8
CHIPS = NX * NY * NZ
GROUPS = 64
HALF = GROUPS // 2
SUB = 8
ROWS = 1024
D = 768
KEYS = 128
WIDE = D + KEYS
HALF_ROWS = 512
ORDERS = 4096
VMEM = 24 * 1024 * 1024
FULL = 56 * 1024 * 1024


def device(x, y, z, core):
    return ((y * NZ + z) * 2 + core) * NX + x


SAME_CORE = [
    [device(x, y, z, core) for y in range(NY) for z in range(NZ) for x in range(NX)] for core in range(2)
]


def ring(step):
    pairs = []
    for y in range(NY):
        for z in range(NZ):
            for x in range(NX):
                pairs.append((device(x, y, z, 0), device((x + step) % NX, y, z, 0)))
                pairs.append((device(x, y, z, 1), device(x, (y + step) % NY, z, 1)))
    return pairs


SIBLING = [(dp * NX + x, (dp ^ 1) * NX + x) for dp in range(NY * NZ * 2) for x in range(NX)]


def exchange(rows):
    return lax.all_to_all(
        rows, AXES, split_axis=0, concat_axis=0, tiled=True, axis_index_groups=SAME_CORE
    )


def send(rows, pairs):
    return lax.ppermute(rows, AXES, pairs)


def cost(flops, size):
    return pl.CostEstimate(flops=flops, bytes_accessed=size, transcendentals=0)


def chip_of(group, place):
    core = (group >= HALF).astype(jnp.int32)
    inner = group - HALF * core
    on_x = inner * NX + place
    on_y = (place * NZ + (inner & (NZ - 1))) * NX + (inner >> 3)
    return jnp.where(core == 0, on_x, on_y), core


def key_rows(ids, order, first):
    key = (ids & 1) * ORDERS + order
    which = lax.broadcasted_iota(jnp.int32, (KEYS, ids.shape[1]), 0)
    high, low = (key >> 7) + 1, key & 127
    return jnp.where(which == first, high, jnp.where(which == first + 1, low, 0)).astype(jnp.float32).astype(
        jnp.bfloat16
    )


def slots_of(info, core, mine):
    group, rank = info[0:1], info[1:2]
    chip, serving = chip_of(group, rank & 3)
    slot = chip * SUB + (rank >> 2)
    return jnp.where((serving == core) if mine else (serving != core), slot, -1)


def onehot(slot):
    rows = lax.broadcasted_iota(jnp.int32, (ROWS, ROWS), 0)
    return jnp.where(rows == slot, 1.0, 0.0).astype(jnp.bfloat16)


def prep_kernel(place_ref, emb_ref, ids_ref, order_ref, unit_ref, box_ref, slab_ref, info_ref):
    ids, order = ids_ref[...], order_ref[...]
    group = ids >> 1
    member = (lax.broadcasted_iota(jnp.int32, (GROUPS, ROWS), 0) == group)
    hot = jnp.where(member, 1.0, 0.0)
    step = 256
    earlier = jnp.where(
        lax.broadcasted_iota(jnp.int32, (step, step), 0) < lax.broadcasted_iota(jnp.int32, (step, step), 1), 1.0, 0.0
    ).astype(jnp.bfloat16)
    before = jnp.zeros((GROUPS, 1), jnp.float32)
    ranks = []
    for part in range(ROWS // step):
        here = hot[:, part * step : (part + 1) * step]
        count = jnp.dot(here.astype(jnp.bfloat16), earlier, preferred_element_type=jnp.float32) + before
        ranks.append(jnp.sum(here * count, axis=0, keepdims=True))
        before = before + jnp.sum(here, axis=1, keepdims=True)
    rank = jnp.concatenate(ranks, axis=1).astype(jnp.int32)
    which = lax.broadcasted_iota(jnp.int32, (8, ROWS), 0)
    info = jnp.where(which == 0, group, jnp.where(which == 1, rank, 0))
    info_ref[...] = info

    wide = emb_ref[...].astype(jnp.float32)
    scale = 1.0 / jnp.sqrt(jnp.sum(wide * wide, axis=1, keepdims=True) + 1e-06)
    unit = (wide * scale).astype(jnp.bfloat16)
    unit_ref[...] = unit

    pick = onehot(slots_of(info, place_ref[0], True))
    box_ref[...] = jnp.dot(pick, unit, preferred_element_type=jnp.float32).astype(jnp.bfloat16)
    slab_ref[...] = lax.dot_general(
        pick, key_rows(ids, order, 2), (((1,), (1,)), ((), ())), preferred_element_type=jnp.float32
    ).astype(jnp.bfloat16)


def prep(place, embeddings, ids, order):
    return pl.pallas_call(
        prep_kernel,
        out_shape=(
            jax.ShapeDtypeStruct((ROWS, D), jnp.bfloat16),
            jax.ShapeDtypeStruct((ROWS, D), jnp.bfloat16),
            jax.ShapeDtypeStruct((ROWS, KEYS), jnp.bfloat16),
            jax.ShapeDtypeStruct((8, ROWS), jnp.int32),
        ),
        in_specs=[pl.BlockSpec(memory_space=pltpu.SMEM)] + [pl.BlockSpec(memory_space=pltpu.VMEM)] * 3,
        out_specs=tuple([pl.BlockSpec(memory_space=pltpu.VMEM)] * 4),
        compiler_params=pltpu.CompilerParams(vmem_limit_bytes=FULL),
        cost_estimate=cost(2 * ROWS * ROWS * WIDE, 6 * ROWS * D),
        name="prep",
    )(place, embeddings, ids, order)


def hand_kernel(place_ref, unit_ref, info_ref, ids_ref, order_ref, box_ref):
    pick = onehot(slots_of(info_ref[...], place_ref[0], False))
    box_ref[:, :D] = jnp.dot(pick, unit_ref[...], preferred_element_type=jnp.float32).astype(jnp.bfloat16)
    box_ref[:, D:] = lax.dot_general(
        pick,
        key_rows(ids_ref[...], order_ref[...], 0),
        (((1,), (1,)), ((), ())),
        preferred_element_type=jnp.float32,
    ).astype(jnp.bfloat16)


def hand(place, unit, info, ids, order):
    return pl.pallas_call(
        hand_kernel,
        out_shape=jax.ShapeDtypeStruct((ROWS, WIDE), jnp.bfloat16),
        in_specs=[pl.BlockSpec(memory_space=pltpu.SMEM)] + [pl.BlockSpec(memory_space=pltpu.VMEM)] * 4,
        out_specs=pl.BlockSpec(memory_space=pltpu.VMEM),
        compiler_params=pltpu.CompilerParams(vmem_limit_bytes=VMEM),
        cost_estimate=cost(2 * ROWS * ROWS * WIDE, 4 * ROWS * D),
        name="hand",
    )(place, unit, info, ids, order)


def stamp_kernel(box_ref, slab_ref, out_ref):
    out_ref[...] = box_ref[...] + slab_ref[...]


def stamp(box, slab):
    return pl.pallas_call(
        stamp_kernel,
        grid=(1,),
        out_shape=jax.ShapeDtypeStruct(box.shape, box.dtype),
        in_specs=[
            pl.BlockSpec((ROWS, KEYS), lambda i: (0, D // KEYS)),
            pl.BlockSpec((ROWS, KEYS), lambda i: (0, 0)),
        ],
        out_specs=pl.BlockSpec((ROWS, KEYS), lambda i: (0, D // KEYS)),
        input_output_aliases={0: 0},
        compiler_params=pltpu.CompilerParams(vmem_limit_bytes=VMEM),
        cost_estimate=cost(0, 3 * 2 * ROWS * KEYS),
        name="stamp",
    )(box, slab)


BLOCKS = [(part, far, chunk) for far in range(3) for chunk in range(2) for part in "PM"]


def pair_lists():
    pairs = []

    def all_chunks(one, other):
        for c in range(2):
            for e in range(2):
                pairs.append((one + (c,), other + (e,)))

    for part in "PM":
        pairs.append(((part, 0, 0), (part, 0, 1)))
        all_chunks((part, 0), (part, 1))
        pairs.append(((part, 0, 1), (part, 2, 0)))
    all_chunks(("P", 0), ("M", 0))
    all_chunks(("P", 0), ("M", 1))
    all_chunks(("P", 1), ("M", 1))
    pairs.append((("P", 1, 0), ("M", 2, 0)))
    pairs.append((("P", 1, 1), ("M", 2, 0)))
    pairs.append((("P", 2, 0), ("M", 1, 1)))
    pairs.append((("P", 1, 1), ("M", 2, 1)))
    by_place = [
        ((("P", 0, 0), ("P", 2, 0)), (("M", 0, 0), ("M", 2, 0))),
        ((("M", 0, 1), ("M", 2, 1)), (("P", 0, 1), ("P", 2, 1))),
    ]
    return pairs, by_place


def stage_of(pair):
    if all(far == 0 for part, far, chunk in pair):
        return 0
    return 2 if any(far == 2 and chunk == 1 for part, far, chunk in pair) else 1


def similar_kernel(blocks, loads, n_tasks, n_before, *refs):
    n_arrays = 1 + max(load[0] for load in loads)
    tasks_ref = refs[0]
    arrays = refs[1 : 1 + n_arrays]
    befores = refs[1 + n_arrays : 1 + n_arrays + n_before]
    out_ref = refs[1 + n_arrays + n_before]
    rows, slabs, kcol, ccol, krow, crow, best_row, best_col, s0, s1, sems = refs[2 + n_arrays + n_before :]
    n_blocks = len(blocks)

    copies = []
    for number, (array, first, columns, is_key, slot) in enumerate(loads):
        source = arrays[array].at[pl.ds(first, HALF_ROWS), pl.ds(columns, KEYS if is_key else D)]
        target = slabs.at[slot] if is_key else rows.at[slot]
        copy = pltpu.make_async_copy(source, target, sems.at[number])
        copy.start()
        copies.append((copy, is_key))
    for slot in range(n_blocks):
        best_row[slot] = jnp.full((HALF_ROWS, 128), -1.0, jnp.float32)
        best_col[slot] = jnp.full((8, HALF_ROWS), -1.0, jnp.float32)
    for copy, is_key in copies:
        if is_key:
            copy.wait()

    lane_of = lax.broadcasted_iota(jnp.int32, (KEYS, 128), 0)
    row_of = lax.broadcasted_iota(jnp.int32, (8, KEYS), 1)
    for slot, (part, far, chunk) in enumerate(blocks):
        first = 0 if chunk == 1 else 2
        slab = slabs[slot]
        weight = jnp.where(lane_of == first, 128.0, jnp.where(lane_of == first + 1, 1.0, 0.0)).astype(jnp.bfloat16)
        key = jnp.dot(slab, weight, preferred_element_type=jnp.float32)
        kcol[slot] = key
        ccol[slot] = jnp.where(key >= ORDERS + 128, 2.0, jnp.where(key > 0, 1.0, 0.0))
        weight = jnp.where(row_of == first, 128.0, jnp.where(row_of == first + 1, 1.0, 0.0)).astype(jnp.bfloat16)
        key = lax.dot_general(weight, slab, (((1,), (1,)), ((), ())), preferred_element_type=jnp.float32)
        krow[slot] = key
        crow[slot] = jnp.where(key >= ORDERS + 128, 2.0, jnp.where(key > 0, 1.0, 0.0))
    for copy, is_key in copies:
        if not is_key:
            copy.wait()

    def multiply(task, s):
        a, b = tasks_ref[3 * task], tasks_ref[3 * task + 1]
        s[...] = lax.dot_general(rows[a], rows[b], (((1,), (1,)), ((), ())), preferred_element_type=jnp.float32)

    step = 16

    def reduce(task, s):
        a, b, sink = tasks_ref[3 * task], tasks_ref[3 * task + 1], tasks_ref[3 * task + 2]
        kb, cb = krow[b], crow[b]
        for row in range(0, HALF_ROWS, step):
            ka = kcol[a, row : row + step].reshape(step // 8, 8, 128)
            ca = ccol[a, row : row + step].reshape(step // 8, 8, 128)
            best = best_row[a, row : row + step]
            for at in range(0, HALF_ROWS, 128):
                found = s[row : row + step, at : at + 128].reshape(step // 8, 8, 128)
                same = jnp.where(ca == cb[None, :, at : at + 128], found, -1.0)
                later = kb[None, :, at : at + 128] < ka
                best = jnp.maximum(best, jnp.where(later, same, -1.0).reshape(step, 128))
                other = jnp.max(jnp.where(later, -1.0, same), axis=0)
                best_col[sink, :, at : at + 128] = jnp.maximum(best_col[sink, :, at : at + 128], other)
            best_row[a, row : row + step] = best

    def two(turn, carry):
        multiply(2 * turn + 1, s1)
        reduce(2 * turn, s0)
        multiply(2 * turn + 2, s0)
        reduce(2 * turn + 1, s1)
        return carry

    multiply(0, s0)
    if n_tasks > 2:
        lax.fori_loop(0, n_tasks // 2 - 1, two, 0)
    multiply(n_tasks - 1, s1)
    reduce(n_tasks - 2, s0)
    reduce(n_tasks - 1, s1)

    empty = jnp.full((8, HALF_ROWS), -1.0, jnp.float32)
    diagonal = lax.broadcasted_iota(jnp.int32, (8, HALF_ROWS), 0) == (
        lax.broadcasted_iota(jnp.int32, (8, HALF_ROWS), 1) & (SUB - 1)
    )
    for number, part in enumerate("PM"):
        tiles = [empty] * 16
        for slot, (its, far, chunk) in enumerate(blocks):
            if its == part:
                by_row = jnp.max(jnp.transpose(best_row[slot]), axis=0, keepdims=True)
                by_col = jnp.max(best_col[slot], axis=0, keepdims=True)
                tiles[2 * far + chunk] = jnp.where(diagonal, jnp.maximum(by_row, by_col), -1.0)
        value = jnp.transpose(jnp.concatenate(tiles, axis=0)).reshape(HALF_ROWS // SUB, SUB, 128)
        value = jnp.max(value, axis=1)
        at = pl.ds(number * (CHIPS // 2), CHIPS // 2)
        for before in befores:
            value = jnp.maximum(value, before[at, :])
        out_ref[at, :] = value


def similar(hold, keys, low, high, ring_place, befores, name):
    blocks = [block for block in BLOCKS if any(block in pair for pair in low + high)]
    place = {block: number for number, block in enumerate(blocks)}
    spare = len(blocks)

    def table(pairs):
        return np.array(
            [(place[a], place[b], spare if a == b else place[b]) for a, b in pairs], np.int32
        ).reshape(-1)

    tasks = jnp.asarray(table(low))
    if low != high:
        tasks = jnp.where(ring_place < 2, tasks, jnp.asarray(table(high)))
    arrays, loads = [], []

    def number_of(array):
        for number, known in enumerate(arrays):
            if known is array:
                return number
        arrays.append(array)
        return len(arrays) - 1

    for block in blocks:
        array, first, column = keys[block[:2]]
        loads.append((number_of(array), first, column, True, place[block]))
    for block in blocks:
        array, first = hold[block]
        loads.append((number_of(array), first, 0, False, place[block]))
    n = len(blocks)
    kernel = functools.partial(similar_kernel, blocks, loads, len(low), len(befores))
    return pl.pallas_call(
        kernel,
        out_shape=jax.ShapeDtypeStruct((CHIPS, 128), jnp.float32),
        in_specs=[pl.BlockSpec(memory_space=pltpu.SMEM)]
        + [pl.BlockSpec(memory_space=pl.ANY)] * len(arrays)
        + [pl.BlockSpec(memory_space=pltpu.VMEM)] * len(befores),
        out_specs=pl.BlockSpec(memory_space=pltpu.VMEM),
        scratch_shapes=[
            pltpu.VMEM((n, HALF_ROWS, D), jnp.bfloat16),
            pltpu.VMEM((n, HALF_ROWS, KEYS), jnp.bfloat16),
            pltpu.VMEM((n, HALF_ROWS, 128), jnp.float32),
            pltpu.VMEM((n, HALF_ROWS, 128), jnp.float32),
            pltpu.VMEM((n, 8, HALF_ROWS), jnp.float32),
            pltpu.VMEM((n, 8, HALF_ROWS), jnp.float32),
            pltpu.VMEM((n, HALF_ROWS, 128), jnp.float32),
            pltpu.VMEM((n + 1, 8, HALF_ROWS), jnp.float32),
            pltpu.VMEM((HALF_ROWS, HALF_ROWS), jnp.float32),
            pltpu.VMEM((HALF_ROWS, HALF_ROWS), jnp.float32),
            pltpu.SemaphoreType.DMA((len(loads),)),
        ],
        compiler_params=pltpu.CompilerParams(vmem_limit_bytes=32 * 1024 * 1024),
        cost_estimate=cost(2 * D * HALF_ROWS * HALF_ROWS * len(low), 2 * len(loads) * HALF_ROWS * D),
        name=name,
    )(tasks, *arrays, *befores)


def answer_kernel(place_ref, info_ref, mine_ref, sibling_ref, out_ref):
    info = info_ref[...]
    group, rank = info[0:1], info[1:2]
    core, step = place_ref[0], place_ref[2]
    values = jnp.concatenate([mine_ref[...], sibling_ref[...]], axis=0)
    device_of = lax.broadcasted_iota(jnp.int32, (2 * CHIPS, ROWS), 0)
    lane_of = lax.broadcasted_iota(jnp.int32, (128, ROWS), 0)
    best = jnp.full((1, ROWS), -1.0, jnp.float32)
    parts = []
    rest = values
    for piece in range(3):
        parts.append(rest.astype(jnp.bfloat16))
        rest = rest - parts[-1].astype(jnp.float32)
    parts = jnp.concatenate(parts, axis=0)
    for far in range(3):
        chip, serving = chip_of(group, (rank + far * step) & 3)
        away = (serving != core).astype(jnp.int32)
        pick = jnp.where(device_of == chip + CHIPS * away, 1.0, 0.0).astype(jnp.bfloat16)
        found = lax.dot_general(
            parts,
            jnp.concatenate([pick] * 3, axis=0),
            (((0,), (0,)), ((), ())),
            preferred_element_type=jnp.float32,
        )
        wanted = far * 16 + away * SUB + (rank >> 2)
        found = jnp.max(jnp.where(lane_of == wanted, found, -1.0), axis=0, keepdims=True)
        best = jnp.maximum(best, found)
    out_ref[...] = best


def answer(place, info, mine, sibling):
    return pl.pallas_call(
        answer_kernel,
        out_shape=jax.ShapeDtypeStruct((1, ROWS), jnp.float32),
        in_specs=[pl.BlockSpec(memory_space=pltpu.SMEM)] + [pl.BlockSpec(memory_space=pltpu.VMEM)] * 3,
        out_specs=pl.BlockSpec(memory_space=pltpu.VMEM),
        compiler_params=pltpu.CompilerParams(vmem_limit_bytes=VMEM),
        cost_estimate=cost(2 * 3 * 6 * 128 * 256 * ROWS, 3 * 4 * 128 * 128),
        name="answer",
    )(place, info, mine, sibling)


def local(embeddings, cluster_ids, member_order):
    dp, x = lax.axis_index("dp"), lax.axis_index("rep")
    core, z, y = dp % 2, (dp // 2) % NZ, dp // (2 * NZ)
    ring_place = jnp.where(core == 0, x, y)
    step = jnp.where((y * NZ + z) * NX + x < CHIPS // 2, 1, -1)
    place = jnp.stack([core, ring_place, step]).astype(jnp.int32)
    ids, order = cluster_ids.reshape(1, ROWS), member_order.reshape(1, ROWS)

    unit, box, slab, info = prep(place, embeddings, ids, order)
    chunk1 = exchange(box.reshape(CHIPS, SUB, D)).reshape(ROWS, D)
    handed = stamp(send(hand(place, unit, info, ids, order), SIBLING), slab)
    chunk1, handed = lax.optimization_barrier((chunk1, handed))
    chunk2 = exchange(handed.reshape(CHIPS, SUB, WIDE)).reshape(ROWS, WIDE)
    near1 = send(chunk1[:HALF_ROWS], ring(1)), send(chunk1[HALF_ROWS:], ring(-1))
    far1 = send(near1[0], ring(1)), send(near1[1], ring(-1))
    chunk2, near1, far1 = lax.optimization_barrier((chunk2, near1, far1))
    near2 = send(chunk2[:HALF_ROWS], ring(1)), send(chunk2[HALF_ROWS:], ring(-1))
    far_keys = send(chunk2[:, D:], ring(2))

    hold, keys = {}, {}
    for half, part in enumerate("PM"):
        first = half * HALF_ROWS
        hold[part, 0, 0], hold[part, 0, 1] = (chunk1, first), (chunk2, first)
        hold[part, 1, 0], hold[part, 2, 0] = (near1[half], 0), (far1[half], 0)
        keys[part, 0], keys[part, 2] = (chunk2, first, D), (far_keys, first, 0)

    pairs, by_place = pair_lists()
    answers = []
    for stage in range(3):
        low = [pair for pair in pairs if stage_of(pair) == stage]
        if stage == 0:
            low += [((part, 0, chunk),) * 2 for part in "PM" for chunk in range(2)]
        high = list(low)
        for one, other in by_place:
            if stage_of(one) == stage:
                low.append(one)
                high.append(other)
        answers.append(
            similar(hold, keys, low, high, ring_place, answers if stage == 2 else [], ("own", "near", "far")[stage])
        )
        if stage == 0:
            near2, answers[0] = lax.optimization_barrier((near2, answers[0]))
            far2 = send(near2[0], ring(1)), send(near2[1], ring(-1))
            for half, part in enumerate("PM"):
                hold[part, 1, 1], hold[part, 2, 1] = (near2[half], 0), (far2[half], 0)
                keys[part, 1] = (near2[half], 0, D)
    mine = exchange(answers[2].reshape(CHIPS, 1, 128)).reshape(CHIPS, 128)
    return answer(place, info, mine, send(mine, SIBLING)).reshape(ROWS)


def solution(mesh):
    return jax.shard_map(
        local,
        mesh=mesh,
        in_specs=(P(AXES, None), P(AXES), P(AXES)),
        out_specs=P(AXES),
        check_vma=False,
    )
```

```python
import functools

import jax
import jax.numpy as jnp
import numpy as np
from jax import lax
from jax.experimental import pallas as pl
from jax.experimental.pallas import tpu as pltpu
from jax.sharding import PartitionSpec as P

AXES = ("dp", "rep")
NX, NY, NZ = 4, 4, 8
CHIPS = NX * NY * NZ
GROUPS = 64
HALF = GROUPS // 2
SUB = 8
ROWS = 1024
D = 768
KEYS = 128
WIDE = D + KEYS
HALF_ROWS = 512
ORDERS = 4096
VMEM = 24 * 1024 * 1024
FULL = 56 * 1024 * 1024


def device(x, y, z, core):
    return ((y * NZ + z) * 2 + core) * NX + x


SAME_CORE = [
    [device(x, y, z, core) for y in range(NY) for z in range(NZ) for x in range(NX)] for core in range(2)
]


def ring(step):
    pairs = []
    for y in range(NY):
        for z in range(NZ):
            for x in range(NX):
                pairs.append((device(x, y, z, 0), device((x + step) % NX, y, z, 0)))
                pairs.append((device(x, y, z, 1), device(x, (y + step) % NY, z, 1)))
    return pairs


SIBLING = [(dp * NX + x, (dp ^ 1) * NX + x) for dp in range(NY * NZ * 2) for x in range(NX)]


def exchange(rows):
    return lax.all_to_all(
        rows, AXES, split_axis=0, concat_axis=0, tiled=True, axis_index_groups=SAME_CORE
    )


def send(rows, pairs):
    return lax.ppermute(rows, AXES, pairs)


def cost(flops, size):
    return pl.CostEstimate(flops=flops, bytes_accessed=size, transcendentals=0)


def chip_of(group, place):
    core = (group >= HALF).astype(jnp.int32)
    inner = group - HALF * core
    on_x = inner * NX + place
    on_y = (place * NZ + (inner & (NZ - 1))) * NX + (inner >> 3)
    return jnp.where(core == 0, on_x, on_y), core


def key_rows(ids, order, first):
    key = (ids & 1) * ORDERS + order
    which = lax.broadcasted_iota(jnp.int32, (KEYS, ids.shape[1]), 0)
    high, low = (key >> 7) + 1, key & 127
    return jnp.where(which == first, high, jnp.where(which == first + 1, low, 0)).astype(jnp.float32).astype(
        jnp.bfloat16
    )


def where_am_i():
    dp = lax.axis_index("dp")
    return lax.axis_index("rep"), dp >> 4, (dp >> 1) & (NZ - 1), dp & 1


def slots_of(info, core, mine):
    group, rank = info[0:1], info[1:2]
    chip, serving = chip_of(group, rank & 3)
    slot = chip * SUB + (rank >> 2)
    return jnp.where((serving == core) if mine else (serving != core), slot, -1)


def onehot(slot, first, count):
    rows = lax.broadcasted_iota(jnp.int32, (count, ROWS), 0) + first
    return jnp.where(rows == slot, 1.0, 0.0).astype(jnp.bfloat16)


def normalize(rows):
    wide = rows.astype(jnp.float32)
    scale = 1.0 / jnp.sqrt(jnp.sum(wide * wide, axis=1, keepdims=True) + 1e-06)
    return (wide * scale).astype(jnp.bfloat16)


PIECE = 256
PIECES = ROWS // PIECE


def prep_kernel(emb_ref, ids_ref, box_ref, info_ref, rows, unit, out, in_sems, out_sems):
    def piece(number):
        return pl.ds(number * PIECE, PIECE)

    loads = [
        pltpu.make_async_copy(emb_ref.at[piece(n)], rows.at[piece(n)], in_sems.at[n]) for n in range(PIECES)
    ]
    for load in loads:
        load.start()
    group = ids_ref[...] >> 1
    member = lax.broadcasted_iota(jnp.int32, (GROUPS, ROWS), 0) == group
    hot = jnp.where(member, 1.0, 0.0)
    earlier = jnp.where(
        lax.broadcasted_iota(jnp.int32, (PIECE, PIECE), 0) < lax.broadcasted_iota(jnp.int32, (PIECE, PIECE), 1),
        1.0,
        0.0,
    ).astype(jnp.bfloat16)
    before = jnp.zeros((GROUPS, 1), jnp.float32)
    ranks = []
    for n in range(PIECES):
        here = hot[:, n * PIECE : (n + 1) * PIECE]
        count = jnp.dot(here.astype(jnp.bfloat16), earlier, preferred_element_type=jnp.float32) + before
        ranks.append(jnp.sum(here * count, axis=0, keepdims=True))
        before = before + jnp.sum(here, axis=1, keepdims=True)
    rank = jnp.concatenate(ranks, axis=1).astype(jnp.int32)
    which = lax.broadcasted_iota(jnp.int32, (8, ROWS), 0)
    info = jnp.where(which == 0, group, jnp.where(which == 1, rank, 0))
    info_ref[...] = info
    slot = slots_of(info, where_am_i()[3], True)

    for n in range(PIECES):
        loads[n].wait()
        unit[piece(n)] = normalize(rows[piece(n)])
    stores = []
    for n in range(PIECES):
        pick = onehot(slot, n * PIECE, PIECE)
        out[piece(n)] = jnp.dot(pick, unit[...], preferred_element_type=jnp.float32).astype(jnp.bfloat16)
        stores.append(pltpu.make_async_copy(out.at[piece(n)], box_ref.at[piece(n)], out_sems.at[n]))
        stores[-1].start()
    for store in stores:
        store.wait()


def prep(embeddings, ids):
    return pl.pallas_call(
        prep_kernel,
        out_shape=(
            jax.ShapeDtypeStruct((ROWS, D), jnp.bfloat16),
            jax.ShapeDtypeStruct((8, ROWS), jnp.int32),
        ),
        in_specs=[pl.BlockSpec(memory_space=pl.ANY), pl.BlockSpec(memory_space=pltpu.VMEM)],
        out_specs=(pl.BlockSpec(memory_space=pl.ANY), pl.BlockSpec(memory_space=pltpu.VMEM)),
        scratch_shapes=[
            pltpu.VMEM((ROWS, D), jnp.bfloat16),
            pltpu.VMEM((ROWS, D), jnp.bfloat16),
            pltpu.VMEM((ROWS, D), jnp.bfloat16),
            pltpu.SemaphoreType.DMA((PIECES,)),
            pltpu.SemaphoreType.DMA((PIECES,)),
        ],
        compiler_params=pltpu.CompilerParams(vmem_limit_bytes=FULL),
        cost_estimate=cost(2 * ROWS * ROWS * D, 4 * ROWS * D),
        name="prep",
    )(embeddings, ids)


def hand_kernel(emb_ref, info_ref, ids_ref, order_ref, box_ref, slab_ref):
    info, core = info_ref[...], where_am_i()[3]
    ids, order = ids_ref[...], order_ref[...]

    def keys(pick, first):
        return lax.dot_general(
            pick, key_rows(ids, order, first), (((1,), (1,)), ((), ())), preferred_element_type=jnp.float32
        ).astype(jnp.bfloat16)

    pick = onehot(slots_of(info, core, False), 0, ROWS)
    box_ref[:, :D] = jnp.dot(pick, normalize(emb_ref[...]), preferred_element_type=jnp.float32).astype(jnp.bfloat16)
    box_ref[:, D:] = keys(pick, 0)
    slab_ref[...] = keys(onehot(slots_of(info, core, True), 0, ROWS), 2)


def hand(embeddings, info, ids, order):
    return pl.pallas_call(
        hand_kernel,
        out_shape=(
            jax.ShapeDtypeStruct((ROWS, WIDE), jnp.bfloat16),
            jax.ShapeDtypeStruct((ROWS, KEYS), jnp.bfloat16),
        ),
        in_specs=[pl.BlockSpec(memory_space=pltpu.VMEM)] * 4,
        out_specs=tuple([pl.BlockSpec(memory_space=pltpu.VMEM)] * 2),
        compiler_params=pltpu.CompilerParams(vmem_limit_bytes=VMEM),
        cost_estimate=cost(2 * ROWS * ROWS * WIDE, 4 * ROWS * D),
        name="hand",
    )(embeddings, info, ids, order)


def stamp_kernel(box_ref, slab_ref, out_ref):
    out_ref[...] = box_ref[...] + slab_ref[...]


def stamp(box, slab):
    return pl.pallas_call(
        stamp_kernel,
        grid=(1,),
        out_shape=jax.ShapeDtypeStruct(box.shape, box.dtype),
        in_specs=[
            pl.BlockSpec((ROWS, KEYS), lambda i: (0, D // KEYS)),
            pl.BlockSpec((ROWS, KEYS), lambda i: (0, 0)),
        ],
        out_specs=pl.BlockSpec((ROWS, KEYS), lambda i: (0, D // KEYS)),
        input_output_aliases={0: 0},
        compiler_params=pltpu.CompilerParams(vmem_limit_bytes=VMEM),
        cost_estimate=cost(0, 3 * 2 * ROWS * KEYS),
        name="stamp",
    )(box, slab)


def split_kernel(both_ref, p_ref, m_ref, key_ref):
    p_ref[...] = both_ref[:HALF_ROWS, :D]
    m_ref[...] = both_ref[HALF_ROWS:, :D]
    row = lax.broadcasted_iota(jnp.int32, (8, KEYS), 0)
    lane = lax.broadcasted_iota(jnp.int32, (8, KEYS), 1)
    first = jnp.where(row == 0, 2, jnp.where(row == 1, 0, KEYS))
    weight = jnp.where(lane == first, 128.0, jnp.where(lane == first + 1, 1.0, 0.0)).astype(jnp.bfloat16)
    key_ref[...] = lax.dot_general(
        weight, both_ref[:, D:], (((1,), (1,)), ((), ())), preferred_element_type=jnp.float32
    )


def split(both):
    return pl.pallas_call(
        split_kernel,
        out_shape=(
            jax.ShapeDtypeStruct((HALF_ROWS, D), jnp.bfloat16),
            jax.ShapeDtypeStruct((HALF_ROWS, D), jnp.bfloat16),
            jax.ShapeDtypeStruct((8, ROWS), jnp.float32),
        ),
        in_specs=[pl.BlockSpec(memory_space=pltpu.VMEM)],
        out_specs=tuple([pl.BlockSpec(memory_space=pltpu.VMEM)] * 3),
        compiler_params=pltpu.CompilerParams(vmem_limit_bytes=VMEM),
        cost_estimate=cost(0, 4 * ROWS * WIDE),
        name="split",
    )(both)


BLOCKS = [(part, far, chunk) for far in range(3) for chunk in range(2) for part in "PM"]


def pair_lists():
    pairs = []

    def all_chunks(one, other):
        for c in range(2):
            for e in range(2):
                pairs.append((one + (c,), other + (e,)))

    for part in "PM":
        pairs.append(((part, 0, 0), (part, 0, 1)))
        all_chunks((part, 0), (part, 1))
        pairs.append(((part, 0, 1), (part, 2, 0)))
    all_chunks(("P", 0), ("M", 0))
    all_chunks(("P", 0), ("M", 1))
    all_chunks(("P", 1), ("M", 1))
    pairs.append((("P", 1, 0), ("M", 2, 0)))
    pairs.append((("P", 1, 1), ("M", 2, 0)))
    pairs.append((("P", 2, 0), ("M", 1, 1)))
    pairs.append((("P", 1, 1), ("M", 2, 1)))
    by_place = [
        ((("P", 0, 0), ("P", 2, 0)), (("M", 0, 0), ("M", 2, 0))),
        ((("M", 0, 1), ("M", 2, 1)), (("P", 0, 1), ("P", 2, 1))),
    ]
    return pairs, by_place


def stage_of(pair):
    if all(far == 0 for part, far, chunk in pair):
        return 0
    return 2 if any(far == 2 and chunk == 1 for part, far, chunk in pair) else 1


def similar_kernel(blocks, loads, n_tasks, n_keys, n_before, *refs):
    n_arrays = 1 + max(load[0] for load in loads)
    tasks_ref, refs = refs[0], refs[1:]
    arrays, refs = refs[:n_arrays], refs[n_arrays:]
    key_refs, refs = refs[:n_keys], refs[n_keys:]
    befores, refs = refs[:n_before], refs[n_before:]
    out_ref, rows, kcol, ccol, krow, crow, best_row, best_col, s0, s1, sems = refs
    n_blocks = len(blocks)

    copies = []
    for number, (array, first, slot, task) in enumerate(loads):
        copy = pltpu.make_async_copy(arrays[array].at[pl.ds(first, HALF_ROWS)], rows.at[slot], sems.at[number])
        copy.start()
        copies.append((copy, task))
    for slot in range(n_blocks):
        best_row[slot] = jnp.full((HALF_ROWS, 128), -1.0, jnp.float32)
        best_col[slot] = jnp.full((8, HALF_ROWS), -1.0, jnp.float32)

    def cluster(key):
        return jnp.where(key >= ORDERS + 128, 2.0, jnp.where(key > 0, 1.0, 0.0))

    for slot, (part, far, chunk, source) in enumerate(blocks):
        first = 0 if part == "P" else HALF_ROWS
        key = key_refs[source][chunk : chunk + 1, first : first + HALF_ROWS]
        krow[slot] = jnp.broadcast_to(key, (8, HALF_ROWS))
        crow[slot] = cluster(krow[slot])
        key = jnp.transpose(jnp.broadcast_to(key, (128, HALF_ROWS)))
        kcol[slot] = key
        ccol[slot] = cluster(key)

    def arrive(low, high):
        for copy, task in copies:
            if low <= task < high:
                copy.wait()

    def multiply(task, s):
        a, b = tasks_ref[3 * task], tasks_ref[3 * task + 1]
        s[...] = lax.dot_general(rows[a], rows[b], (((1,), (1,)), ((), ())), preferred_element_type=jnp.float32)

    step = 16

    def reduce(task, s):
        a, b, sink = tasks_ref[3 * task], tasks_ref[3 * task + 1], tasks_ref[3 * task + 2]
        kb, cb = krow[b], crow[b]
        for row in range(0, HALF_ROWS, step):
            ka = kcol[a, row : row + step].reshape(step // 8, 8, 128)
            ca = ccol[a, row : row + step].reshape(step // 8, 8, 128)
            best = best_row[a, row : row + step]
            for at in range(0, HALF_ROWS, 128):
                found = s[row : row + step, at : at + 128].reshape(step // 8, 8, 128)
                same = jnp.where(ca == cb[None, :, at : at + 128], found, -1.0)
                later = kb[None, :, at : at + 128] < ka
                best = jnp.maximum(best, jnp.where(later, same, -1.0).reshape(step, 128))
                other = jnp.max(jnp.where(later, -1.0, same), axis=0)
                best_col[sink, :, at : at + 128] = jnp.maximum(best_col[sink, :, at : at + 128], other)
            best_row[a, row : row + step] = best

    def two(turn, carry):
        for t in range(n_tasks // 2 - 1):
            if any(2 * t + 1 <= task < 2 * t + 3 for copy, task in copies):

                @pl.when(turn == t)
                def _():
                    arrive(2 * t + 1, 2 * t + 3)

        multiply(2 * turn + 1, s1)
        reduce(2 * turn, s0)
        multiply(2 * turn + 2, s0)
        reduce(2 * turn + 1, s1)
        return carry

    arrive(0, 1)
    multiply(0, s0)
    if n_tasks > 2:
        lax.fori_loop(0, n_tasks // 2 - 1, two, 0)
    arrive(n_tasks - 1, n_tasks)
    multiply(n_tasks - 1, s1)
    reduce(n_tasks - 2, s0)
    reduce(n_tasks - 1, s1)

    empty = jnp.full((8, HALF_ROWS), -1.0, jnp.float32)
    diagonal = lax.broadcasted_iota(jnp.int32, (8, HALF_ROWS), 0) == (
        lax.broadcasted_iota(jnp.int32, (8, HALF_ROWS), 1) & (SUB - 1)
    )
    for number, part in enumerate("PM"):
        tiles = [empty] * 16
        for slot, (its, far, chunk, source) in enumerate(blocks):
            if its == part:
                by_row = jnp.max(jnp.transpose(best_row[slot]), axis=0, keepdims=True)
                by_col = jnp.max(best_col[slot], axis=0, keepdims=True)
                tiles[2 * far + chunk] = jnp.where(diagonal, jnp.maximum(by_row, by_col), -1.0)
        value = jnp.transpose(jnp.concatenate(tiles, axis=0)).reshape(HALF_ROWS // SUB, SUB, 128)
        value = jnp.max(value, axis=1)
        at = pl.ds(number * (CHIPS // 2), CHIPS // 2)
        for before in befores:
            value = jnp.maximum(value, before[at, :])
        out_ref[at, :] = value


def similar(hold, keys, low, high, ring_place, befores, name):
    blocks = [block for block in BLOCKS if any(block in pair for pair in low + high)]
    place = {block: number for number, block in enumerate(blocks)}
    spare = len(blocks)

    def table(pairs):
        return np.array(
            [(place[a], place[b], spare if a == b else place[b]) for a, b in pairs], np.int32
        ).reshape(-1)

    tasks = jnp.asarray(table(low))
    if low != high:
        tasks = jnp.where(ring_place < 2, tasks, jnp.asarray(table(high)))

    def number_of(array, arrays):
        for number, known in enumerate(arrays):
            if known is array:
                return number
        arrays.append(array)
        return len(arrays) - 1

    arrays, key_arrays, loads, full = [], [], [], []
    for block in blocks:
        array, first = hold[block]
        task = min(n for n, pairs in enumerate(zip(low, high)) if any(block in pair for pair in pairs))
        loads.append((number_of(array, arrays), first, place[block], task))
        full.append(block + (number_of(keys[block[:2]], key_arrays),))
    loads.sort(key=lambda load: load[3])
    n = len(blocks)
    kernel = functools.partial(similar_kernel, full, loads, len(low), len(key_arrays), len(befores))
    return pl.pallas_call(
        kernel,
        out_shape=jax.ShapeDtypeStruct((CHIPS, 128), jnp.float32),
        in_specs=[pl.BlockSpec(memory_space=pltpu.SMEM)]
        + [pl.BlockSpec(memory_space=pl.ANY)] * len(arrays)
        + [pl.BlockSpec(memory_space=pltpu.VMEM)] * (len(key_arrays) + len(befores)),
        out_specs=pl.BlockSpec(memory_space=pltpu.VMEM),
        scratch_shapes=[
            pltpu.VMEM((n, HALF_ROWS, D), jnp.bfloat16),
            pltpu.VMEM((n, HALF_ROWS, 128), jnp.float32),
            pltpu.VMEM((n, HALF_ROWS, 128), jnp.float32),
            pltpu.VMEM((n, 8, HALF_ROWS), jnp.float32),
            pltpu.VMEM((n, 8, HALF_ROWS), jnp.float32),
            pltpu.VMEM((n, HALF_ROWS, 128), jnp.float32),
            pltpu.VMEM((n + 1, 8, HALF_ROWS), jnp.float32),
            pltpu.VMEM((HALF_ROWS, HALF_ROWS), jnp.float32),
            pltpu.VMEM((HALF_ROWS, HALF_ROWS), jnp.float32),
            pltpu.SemaphoreType.DMA((len(loads),)),
        ],
        compiler_params=pltpu.CompilerParams(vmem_limit_bytes=32 * 1024 * 1024),
        cost_estimate=cost(2 * D * HALF_ROWS * HALF_ROWS * len(low), 2 * len(loads) * HALF_ROWS * D),
        name=name,
    )(tasks, *arrays, *key_arrays, *befores)


def answer_kernel(info_ref, mine_ref, sibling_ref, out_ref):
    info = info_ref[...]
    group, rank = info[0:1], info[1:2]
    x, y, z, core = where_am_i()
    step = jnp.where((y * NZ + z) * NX + x < CHIPS // 2, 1, -1)
    values = jnp.concatenate([mine_ref[...], sibling_ref[...]], axis=0)
    device_of = lax.broadcasted_iota(jnp.int32, (2 * CHIPS, ROWS), 0)
    lane_of = lax.broadcasted_iota(jnp.int32, (128, ROWS), 0)
    best = jnp.full((1, ROWS), -1.0, jnp.float32)
    parts = []
    rest = values
    for piece in range(3):
        parts.append(rest.astype(jnp.bfloat16))
        rest = rest - parts[-1].astype(jnp.float32)
    parts = jnp.concatenate(parts, axis=0)
    for far in range(3):
        chip, serving = chip_of(group, (rank + far * step) & 3)
        away = (serving != core).astype(jnp.int32)
        pick = jnp.where(device_of == chip + CHIPS * away, 1.0, 0.0).astype(jnp.bfloat16)
        found = lax.dot_general(
            parts,
            jnp.concatenate([pick] * 3, axis=0),
            (((0,), (0,)), ((), ())),
            preferred_element_type=jnp.float32,
        )
        wanted = far * 16 + away * SUB + (rank >> 2)
        found = jnp.max(jnp.where(lane_of == wanted, found, -1.0), axis=0, keepdims=True)
        best = jnp.maximum(best, found)
    out_ref[...] = best


def answer(info, mine, sibling):
    return pl.pallas_call(
        answer_kernel,
        out_shape=jax.ShapeDtypeStruct((1, ROWS), jnp.float32),
        in_specs=[pl.BlockSpec(memory_space=pltpu.VMEM)] * 3,
        out_specs=pl.BlockSpec(memory_space=pltpu.VMEM),
        compiler_params=pltpu.CompilerParams(vmem_limit_bytes=VMEM),
        cost_estimate=cost(2 * 3 * 6 * 128 * 256 * ROWS, 3 * 4 * 128 * 128),
        name="answer",
    )(info, mine, sibling)


def local(embeddings, cluster_ids, member_order):
    x, y, z, core = where_am_i()
    ring_place = jnp.where(core == 0, x, y)
    ids, order = cluster_ids.reshape(1, ROWS), member_order.reshape(1, ROWS)

    box, info = prep(embeddings, ids)
    chunk1 = exchange(box.reshape(CHIPS, SUB, D)).reshape(ROWS, D)
    handed, slab = hand(embeddings, info, ids, order)
    handed = stamp(send(handed, SIBLING), slab)
    chunk1, handed = lax.optimization_barrier((chunk1, handed))
    chunk2 = exchange(handed.reshape(CHIPS, SUB, WIDE)).reshape(ROWS, WIDE)
    near1 = send(chunk1[:HALF_ROWS], ring(1)), send(chunk1[HALF_ROWS:], ring(-1))
    far1 = send(near1[0], ring(1)), send(near1[1], ring(-1))
    chunk2, near1, far1 = lax.optimization_barrier((chunk2, near1, far1))
    own2_p, own2_m, key = split(chunk2)
    own2 = own2_p, own2_m
    near2 = send(own2_p, ring(1)), send(own2_m, ring(-1))
    keys = {("P", 0): key, ("M", 0): key, ("P", 1): send(key, ring(1)), ("M", 1): send(key, ring(-1))}
    keys["P", 2] = keys["M", 2] = send(key, ring(2))

    hold = {}
    for half, part in enumerate("PM"):
        hold[part, 0, 0], hold[part, 0, 1] = (chunk1, half * HALF_ROWS), (own2[half], 0)
        hold[part, 1, 0], hold[part, 2, 0] = (near1[half], 0), (far1[half], 0)

    pairs, by_place = pair_lists()
    answers = []
    for stage in range(3):
        low = [pair for pair in pairs if stage_of(pair) == stage]
        if stage == 0:
            low += [((part, 0, chunk),) * 2 for part in "PM" for chunk in range(2)]
        high = list(low)
        for one, other in by_place:
            if stage_of(one) == stage:
                low.append(one)
                high.append(other)
        answers.append(
            similar(hold, keys, low, high, ring_place, answers if stage == 2 else [], ("own", "near", "far")[stage])
        )
        if stage == 0:
            near2, answers[0] = lax.optimization_barrier((near2, answers[0]))
            far2 = send(near2[0], ring(1)), send(near2[1], ring(-1))
            for half, part in enumerate("PM"):
                hold[part, 1, 1], hold[part, 2, 1] = (near2[half], 0), (far2[half], 0)
    mine = exchange(answers[2].reshape(CHIPS, 1, 128)).reshape(CHIPS, 128)
    return answer(info, mine, send(mine, SIBLING)).reshape(ROWS)


def solution(mesh):
    return jax.shard_map(
        local,
        mesh=mesh,
        in_specs=(P(AXES, None), P(AXES), P(AXES)),
        out_specs=P(AXES),
        check_vma=False,
    )
```

```python
import functools

import jax
import jax.numpy as jnp
import numpy as np
from jax import lax
from jax.experimental import pallas as pl
from jax.experimental.pallas import tpu as pltpu
from jax.sharding import PartitionSpec as P

AXES = ("dp", "rep")
NX, NY, NZ = 4, 4, 8
CHIPS = NX * NY * NZ
GROUPS = 64
HALF = GROUPS // 2
SUB = 8
ROWS = 1024
D = 768
CAP = 32
HALF_ROWS = 512
ORDERS = 4096
VMEM = 24 * 1024 * 1024
FULL = 56 * 1024 * 1024


def device(x, y, z, core):
    return ((y * NZ + z) * 2 + core) * NX + x


SAME_CORE = [
    [device(x, y, z, core) for y in range(NY) for z in range(NZ) for x in range(NX)] for core in range(2)
]


def ring(step):
    pairs = []
    for y in range(NY):
        for z in range(NZ):
            for x in range(NX):
                pairs.append((device(x, y, z, 0), device((x + step) % NX, y, z, 0)))
                pairs.append((device(x, y, z, 1), device(x, (y + step) % NY, z, 1)))
    return pairs


def shift(axis, step):
    pairs = []
    for y in range(NY):
        for z in range(NZ):
            for x in range(NX):
                to = [x, y, z]
                to[axis] = (to[axis] + step) % (NX, NY, NZ)[axis]
                pairs += [(device(x, y, z, core), device(*to, core)) for core in range(2)]
    return pairs


SIBLING = [(dp * NX + x, (dp ^ 1) * NX + x) for dp in range(NY * NZ * 2) for x in range(NX)]


def exchange(rows):
    return lax.all_to_all(
        rows, AXES, split_axis=0, concat_axis=0, tiled=True, axis_index_groups=SAME_CORE
    )


def send(rows, pairs):
    return lax.ppermute(rows, AXES, pairs)


def cost(flops, size):
    return pl.CostEstimate(flops=flops, bytes_accessed=size, transcendentals=0)


def chip_of(group, place):
    core = (group >= HALF).astype(jnp.int32)
    inner = group - HALF * core
    on_x = inner * NX + place
    on_y = (place * NZ + (inner & (NZ - 1))) * NX + (inner >> 3)
    return jnp.where(core == 0, on_x, on_y), core


def where_am_i():
    dp = lax.axis_index("dp")
    return lax.axis_index("rep"), dp >> 4, (dp >> 1) & (NZ - 1), dp & 1


def slots_of(info, core, mine):
    group, rank = info[0:1], info[1:2]
    chip, serving = chip_of(group, rank & 3)
    slot = chip * SUB + (rank >> 2)
    return jnp.where((serving == core) if mine else (serving != core), slot, -1)


def onehot(slot, first, count):
    rows = lax.broadcasted_iota(jnp.int32, (count, ROWS), 0) + first
    return jnp.where(rows == slot, 1.0, 0.0).astype(jnp.bfloat16)


def normalize(rows):
    wide = rows.astype(jnp.float32)
    scale = 1.0 / jnp.sqrt(jnp.sum(wide * wide, axis=1, keepdims=True) + 1e-06)
    return (wide * scale).astype(jnp.bfloat16)


PIECE = 256
PIECES = ROWS // PIECE


def prep_kernel(emb_ref, ids_ref, box_ref, info_ref, rows, unit, out, in_sems, out_sems):
    def piece(number):
        return pl.ds(number * PIECE, PIECE)

    loads = [
        pltpu.make_async_copy(emb_ref.at[piece(n)], rows.at[piece(n)], in_sems.at[n]) for n in range(PIECES)
    ]
    for load in loads:
        load.start()
    group = ids_ref[...] >> 1
    member = lax.broadcasted_iota(jnp.int32, (GROUPS, ROWS), 0) == group
    hot = jnp.where(member, 1.0, 0.0)
    earlier = jnp.where(
        lax.broadcasted_iota(jnp.int32, (PIECE, PIECE), 0) < lax.broadcasted_iota(jnp.int32, (PIECE, PIECE), 1),
        1.0,
        0.0,
    ).astype(jnp.bfloat16)
    before = jnp.zeros((GROUPS, 1), jnp.float32)
    ranks = []
    for n in range(PIECES):
        here = hot[:, n * PIECE : (n + 1) * PIECE]
        count = jnp.dot(here.astype(jnp.bfloat16), earlier, preferred_element_type=jnp.float32) + before
        ranks.append(jnp.sum(here * count, axis=0, keepdims=True))
        before = before + jnp.sum(here, axis=1, keepdims=True)
    rank = jnp.concatenate(ranks, axis=1).astype(jnp.int32)
    which = lax.broadcasted_iota(jnp.int32, (8, ROWS), 0)
    info = jnp.where(which == 0, group, jnp.where(which == 1, rank, 0))
    info_ref[...] = info
    slot = slots_of(info, where_am_i()[3], True)

    for n in range(PIECES):
        loads[n].wait()
        unit[piece(n)] = normalize(rows[piece(n)])
    stores = []
    for n in range(PIECES):
        pick = onehot(slot, n * PIECE, PIECE)
        out[piece(n)] = jnp.dot(pick, unit[...], preferred_element_type=jnp.float32).astype(jnp.bfloat16)
        stores.append(pltpu.make_async_copy(out.at[piece(n)], box_ref.at[piece(n)], out_sems.at[n]))
        stores[-1].start()
    for store in stores:
        store.wait()


def prep(embeddings, ids):
    return pl.pallas_call(
        prep_kernel,
        out_shape=(
            jax.ShapeDtypeStruct((ROWS, D), jnp.bfloat16),
            jax.ShapeDtypeStruct((8, ROWS), jnp.int32),
        ),
        in_specs=[pl.BlockSpec(memory_space=pl.ANY), pl.BlockSpec(memory_space=pltpu.VMEM)],
        out_specs=(pl.BlockSpec(memory_space=pl.ANY), pl.BlockSpec(memory_space=pltpu.VMEM)),
        scratch_shapes=[
            pltpu.VMEM((ROWS, D), jnp.bfloat16),
            pltpu.VMEM((ROWS, D), jnp.bfloat16),
            pltpu.VMEM((ROWS, D), jnp.bfloat16),
            pltpu.SemaphoreType.DMA((PIECES,)),
            pltpu.SemaphoreType.DMA((PIECES,)),
        ],
        compiler_params=pltpu.CompilerParams(vmem_limit_bytes=FULL),
        cost_estimate=cost(2 * ROWS * ROWS * D, 4 * ROWS * D),
        name="prep",
    )(embeddings, ids)


def across(one, other):
    return lax.dot_general(one, other, (((1,), (1,)), ((), ())), preferred_element_type=jnp.float32)


def two_parts(key):
    high = jnp.floor(key * (1.0 / 128.0)) * 128.0
    return high.astype(jnp.bfloat16), (key - high).astype(jnp.bfloat16)


def hand_kernel(emb_ref, info_ref, ids_ref, order_ref, box_ref, mine_ref, theirs_ref):
    info = info_ref[...]
    x, y, z, core = where_am_i()
    pick = onehot(slots_of(info, core, False), 0, ROWS)
    box_ref[...] = jnp.dot(pick, normalize(emb_ref[...]), preferred_element_type=jnp.float32).astype(jnp.bfloat16)

    group, rank = info[0:1], info[1:2]
    inner = group & (HALF - 1)
    key = (ids_ref[...] & 1) * ORDERS + order_ref[...] + 128
    column = lax.broadcasted_iota(jnp.int32, (128, ROWS), 0) == (inner >> 3) * CAP + rank
    column = jnp.where(column, 1.0, 0.0).astype(jnp.bfloat16)
    row = (((inner & (NZ - 1)) - z) & (NZ - 1)) * 8
    number = lax.broadcasted_iota(jnp.int32, (8 * NZ, ROWS), 0)
    for out_ref, mine in ((mine_ref, True), (theirs_ref, False)):
        serving = (group >= HALF).astype(jnp.int32)
        here = jnp.where((serving == core) if mine else (serving != core), row + (0 if mine else 1), -1)
        high, low = two_parts(jnp.where(number == here, key.astype(jnp.float32), 0.0))
        out_ref[...] = across(high, column) + across(low, column)


def hand(embeddings, info, ids, order):
    return pl.pallas_call(
        hand_kernel,
        out_shape=(
            jax.ShapeDtypeStruct((ROWS, D), jnp.bfloat16),
            jax.ShapeDtypeStruct((8 * NZ, 128), jnp.float32),
            jax.ShapeDtypeStruct((8 * NZ, 128), jnp.float32),
        ),
        in_specs=[pl.BlockSpec(memory_space=pltpu.VMEM)] * 4,
        out_specs=tuple([pl.BlockSpec(memory_space=pltpu.VMEM)] * 3),
        compiler_params=pltpu.CompilerParams(vmem_limit_bytes=VMEM),
        cost_estimate=cost(2 * ROWS * ROWS * D, 4 * ROWS * D),
        name="hand",
    )(embeddings, info, ids, order)


def choose(wanted, table):
    wanted = jnp.where(wanted, 1.0, 0.0).astype(jnp.bfloat16)
    high, low = two_parts(table)
    return jnp.dot(wanted, high, preferred_element_type=jnp.float32) + jnp.dot(
        wanted, low, preferred_element_type=jnp.float32
    )


def pack_kernel(*refs):
    tables, out_ref = refs[:NZ], refs[NZ]
    z = where_am_i()[2]
    table = jnp.concatenate([ref[...] for ref in tables], axis=0)
    row = lax.broadcasted_iota(jnp.int32, (2 * NZ, 8 * NZ), 0)
    source = lax.broadcasted_iota(jnp.int32, (2 * NZ, 8 * NZ), 1)
    out_ref[...] = choose(source == ((z - (row >> 1)) & (NZ - 1)) * 8 + (row & 1), table)


def pack(tables):
    return pl.pallas_call(
        pack_kernel,
        out_shape=jax.ShapeDtypeStruct((2 * NZ, 128), jnp.float32),
        in_specs=[pl.BlockSpec(memory_space=pltpu.VMEM)] * NZ,
        out_specs=pl.BlockSpec(memory_space=pltpu.VMEM),
        compiler_params=pltpu.CompilerParams(vmem_limit_bytes=VMEM),
        cost_estimate=cost(0, 8 * NZ * 512),
        name="pack",
    )(*tables)


def keys_kernel(*refs):
    tables, outs = refs[:NY], refs[NY:]
    x, y, z, core = where_am_i()
    place, unit = jnp.where(core == 0, x, y), jnp.where(core == 0, y, x)
    table = jnp.concatenate([ref[...] for ref in tables], axis=0)
    chip = lax.broadcasted_iota(jnp.int32, (CHIPS, table.shape[0]), 0)
    source = lax.broadcasted_iota(jnp.int32, (CHIPS, table.shape[0]), 1)
    of_y, of_z, of_x = chip >> 5, (chip >> 2) & (NZ - 1), chip & (NX - 1)
    source_row = ((y - of_y) & (NY - 1)) * 64 + ((x - of_x) & (NX - 1)) * 16 + of_z * 2
    half = lax.broadcasted_iota(jnp.int32, (CHIPS, SUB, 128), 0) >> 6
    sub = lax.broadcasted_iota(jnp.int32, (CHIPS, SUB, 128), 1)
    lane = lax.broadcasted_iota(jnp.int32, (CHIPS, SUB, 128), 2)
    ones = jnp.ones((8, 128), jnp.bfloat16)
    found = []
    for chunk in range(2):
        rows = choose(source == source_row + chunk, table)
        rows = jnp.broadcast_to(rows[:, None, :], (CHIPS, SUB, 128))
        for far in range(3):
            at = jnp.where(half == 0, place - far, place + far) & 3
            its = jnp.where(lane == unit * CAP + sub * 4 + at, rows, 0.0).reshape(ROWS, 128)
            high, low = two_parts(its)
            found.append(across(ones, high) + across(ones, low))
    which = lax.broadcasted_iota(jnp.int32, (8, ROWS), 0)
    for far in range(3):
        outs[far][...] = jnp.where(which == 0, found[far], found[3 + far])


def ring_keys(tables):
    return pl.pallas_call(
        keys_kernel,
        out_shape=tuple([jax.ShapeDtypeStruct((8, ROWS), jnp.float32)] * 3),
        in_specs=[pl.BlockSpec(memory_space=pltpu.VMEM)] * NY,
        out_specs=tuple([pl.BlockSpec(memory_space=pltpu.VMEM)] * 3),
        compiler_params=pltpu.CompilerParams(vmem_limit_bytes=VMEM),
        cost_estimate=cost(0, 4 * 8 * NZ * 512),
        name="keys",
    )(*tables)


def split_kernel(both_ref, p_ref, m_ref):
    p_ref[...] = both_ref[:HALF_ROWS]
    m_ref[...] = both_ref[HALF_ROWS:]


def split(both):
    return pl.pallas_call(
        split_kernel,
        out_shape=tuple([jax.ShapeDtypeStruct((HALF_ROWS, D), jnp.bfloat16)] * 2),
        in_specs=[pl.BlockSpec(memory_space=pltpu.VMEM)],
        out_specs=tuple([pl.BlockSpec(memory_space=pltpu.VMEM)] * 2),
        compiler_params=pltpu.CompilerParams(vmem_limit_bytes=VMEM),
        cost_estimate=cost(0, 4 * ROWS * D),
        name="split",
    )(both)


BLOCKS = [(part, far, chunk) for far in range(3) for chunk in range(2) for part in "PM"]


def pair_lists():
    pairs = []

    def all_chunks(one, other):
        for c in range(2):
            for e in range(2):
                pairs.append((one + (c,), other + (e,)))

    for part in "PM":
        pairs.append(((part, 0, 0), (part, 0, 1)))
        all_chunks((part, 0), (part, 1))
        pairs.append(((part, 0, 1), (part, 2, 0)))
    all_chunks(("P", 0), ("M", 0))
    all_chunks(("P", 0), ("M", 1))
    all_chunks(("P", 1), ("M", 1))
    pairs.append((("P", 1, 0), ("M", 2, 0)))
    pairs.append((("P", 1, 1), ("M", 2, 0)))
    pairs.append((("P", 2, 0), ("M", 1, 1)))
    pairs.append((("P", 1, 1), ("M", 2, 1)))
    by_place = [
        ((("P", 0, 0), ("P", 2, 0)), (("M", 0, 0), ("M", 2, 0))),
        ((("M", 0, 1), ("M", 2, 1)), (("P", 0, 1), ("P", 2, 1))),
    ]
    return pairs, by_place


def stage_of(pair):
    if all(chunk == 0 for part, far, chunk in pair):
        return 0
    return 1 + max(far for part, far, chunk in pair if chunk == 1)


def similar_kernel(blocks, loads, n_tasks, n_keys, n_before, *refs):
    n_arrays = 1 + max(load[0] for load in loads)
    tasks_ref, refs = refs[0], refs[1:]
    arrays, refs = refs[:n_arrays], refs[n_arrays:]
    key_refs, refs = refs[:n_keys], refs[n_keys:]
    befores, refs = refs[:n_before], refs[n_before:]
    out_ref, rows, kcol, ccol, krow, crow, best_row, best_col, s0, s1, sems = refs
    n_blocks = len(blocks)

    copies = []
    for number, (array, first, slot, task) in enumerate(loads):
        copy = pltpu.make_async_copy(arrays[array].at[pl.ds(first, HALF_ROWS)], rows.at[slot], sems.at[number])
        copy.start()
        copies.append((copy, task))
    for slot in range(n_blocks):
        best_row[slot] = jnp.full((HALF_ROWS, 128), -1.0, jnp.float32)
        best_col[slot] = jnp.full((8, HALF_ROWS), -1.0, jnp.float32)

    def cluster(key):
        return jnp.where(key >= ORDERS + 128, 2.0, jnp.where(key > 0, 1.0, 0.0))

    for slot, (part, far, chunk, source) in enumerate(blocks):
        first = 0 if part == "P" else HALF_ROWS
        key = key_refs[source][chunk : chunk + 1, first : first + HALF_ROWS]
        krow[slot] = jnp.broadcast_to(key, (8, HALF_ROWS))
        crow[slot] = cluster(krow[slot])
        key = jnp.transpose(jnp.broadcast_to(key, (128, HALF_ROWS)))
        kcol[slot] = key
        ccol[slot] = cluster(key)

    def arrive(low, high):
        for copy, task in copies:
            if low <= task < high:
                copy.wait()

    def multiply(task, s):
        a, b = tasks_ref[3 * task], tasks_ref[3 * task + 1]
        s[...] = lax.dot_general(rows[a], rows[b], (((1,), (1,)), ((), ())), preferred_element_type=jnp.float32)

    step = 16

    def reduce(task, s):
        a, b, sink = tasks_ref[3 * task], tasks_ref[3 * task + 1], tasks_ref[3 * task + 2]
        kb, cb = krow[b], crow[b]
        for row in range(0, HALF_ROWS, step):
            ka = kcol[a, row : row + step].reshape(step // 8, 8, 128)
            ca = ccol[a, row : row + step].reshape(step // 8, 8, 128)
            best = best_row[a, row : row + step]
            for at in range(0, HALF_ROWS, 128):
                found = s[row : row + step, at : at + 128].reshape(step // 8, 8, 128)
                same = jnp.where(ca == cb[None, :, at : at + 128], found, -1.0)
                later = kb[None, :, at : at + 128] < ka
                best = jnp.maximum(best, jnp.where(later, same, -1.0).reshape(step, 128))
                other = jnp.max(jnp.where(later, -1.0, same), axis=0)
                best_col[sink, :, at : at + 128] = jnp.maximum(best_col[sink, :, at : at + 128], other)
            best_row[a, row : row + step] = best

    turns = (n_tasks - 1) // 2

    def two(turn, carry):
        for t in range(turns):
            if any(2 * t + 1 <= task < 2 * t + 3 for copy, task in copies):

                @pl.when(turn == t)
                def _():
                    arrive(2 * t + 1, 2 * t + 3)

        multiply(2 * turn + 1, s1)
        reduce(2 * turn, s0)
        multiply(2 * turn + 2, s0)
        reduce(2 * turn + 1, s1)
        return carry

    arrive(0, 1)
    multiply(0, s0)
    if turns:
        lax.fori_loop(0, turns, two, 0)
    if n_tasks % 2 == 0:
        arrive(n_tasks - 1, n_tasks)
        multiply(n_tasks - 1, s1)
    reduce(2 * turns, s0)
    if n_tasks % 2 == 0:
        reduce(n_tasks - 1, s1)

    empty = jnp.full((8, HALF_ROWS), -1.0, jnp.float32)
    diagonal = lax.broadcasted_iota(jnp.int32, (8, HALF_ROWS), 0) == (
        lax.broadcasted_iota(jnp.int32, (8, HALF_ROWS), 1) & (SUB - 1)
    )
    for number, part in enumerate("PM"):
        tiles = [empty] * 16
        for slot, (its, far, chunk, source) in enumerate(blocks):
            if its == part:
                by_row = jnp.max(jnp.transpose(best_row[slot]), axis=0, keepdims=True)
                by_col = jnp.max(best_col[slot], axis=0, keepdims=True)
                tiles[2 * far + chunk] = jnp.where(diagonal, jnp.maximum(by_row, by_col), -1.0)
        value = jnp.transpose(jnp.concatenate(tiles, axis=0)).reshape(HALF_ROWS // SUB, SUB, 128)
        value = jnp.max(value, axis=1)
        at = pl.ds(number * (CHIPS // 2), CHIPS // 2)
        for before in befores:
            value = jnp.maximum(value, before[at, :])
        out_ref[at, :] = value


def similar(hold, keys, low, high, ring_place, befores, name):
    blocks = [block for block in BLOCKS if any(block in pair for pair in low + high)]
    place = {block: number for number, block in enumerate(blocks)}
    spare = len(blocks)

    def table(pairs):
        return np.array(
            [(place[a], place[b], spare if a == b else place[b]) for a, b in pairs], np.int32
        ).reshape(-1)

    tasks = jnp.asarray(table(low))
    if low != high:
        tasks = jnp.where(ring_place < 2, tasks, jnp.asarray(table(high)))

    def number_of(array, arrays):
        for number, known in enumerate(arrays):
            if known is array:
                return number
        arrays.append(array)
        return len(arrays) - 1

    arrays, key_arrays, loads, full = [], [], [], []
    for block in blocks:
        array, first = hold[block]
        task = min(n for n, pairs in enumerate(zip(low, high)) if any(block in pair for pair in pairs))
        loads.append((number_of(array, arrays), first, place[block], task))
        full.append(block + (number_of(keys[block[1]], key_arrays),))
    loads.sort(key=lambda load: load[3])
    n = len(blocks)
    kernel = functools.partial(similar_kernel, full, loads, len(low), len(key_arrays), len(befores))
    return pl.pallas_call(
        kernel,
        out_shape=jax.ShapeDtypeStruct((CHIPS, 128), jnp.float32),
        in_specs=[pl.BlockSpec(memory_space=pltpu.SMEM)]
        + [pl.BlockSpec(memory_space=pl.ANY)] * len(arrays)
        + [pl.BlockSpec(memory_space=pltpu.VMEM)] * (len(key_arrays) + len(befores)),
        out_specs=pl.BlockSpec(memory_space=pltpu.VMEM),
        scratch_shapes=[
            pltpu.VMEM((n, HALF_ROWS, D), jnp.bfloat16),
            pltpu.VMEM((n, HALF_ROWS, 128), jnp.float32),
            pltpu.VMEM((n, HALF_ROWS, 128), jnp.float32),
            pltpu.VMEM((n, 8, HALF_ROWS), jnp.float32),
            pltpu.VMEM((n, 8, HALF_ROWS), jnp.float32),
            pltpu.VMEM((n, HALF_ROWS, 128), jnp.float32),
            pltpu.VMEM((n + 1, 8, HALF_ROWS), jnp.float32),
            pltpu.VMEM((HALF_ROWS, HALF_ROWS), jnp.float32),
            pltpu.VMEM((HALF_ROWS, HALF_ROWS), jnp.float32),
            pltpu.SemaphoreType.DMA((len(loads),)),
        ],
        compiler_params=pltpu.CompilerParams(vmem_limit_bytes=32 * 1024 * 1024),
        cost_estimate=cost(2 * D * HALF_ROWS * HALF_ROWS * len(low), 2 * len(loads) * HALF_ROWS * D),
        name=name,
    )(tasks, *arrays, *key_arrays, *befores)


def answer_kernel(info_ref, mine_ref, sibling_ref, out_ref):
    info = info_ref[...]
    group, rank = info[0:1], info[1:2]
    x, y, z, core = where_am_i()
    step = jnp.where((y * NZ + z) * NX + x < CHIPS // 2, 1, -1)
    values = jnp.concatenate([mine_ref[...], sibling_ref[...]], axis=0)
    device_of = lax.broadcasted_iota(jnp.int32, (2 * CHIPS, ROWS), 0)
    lane_of = lax.broadcasted_iota(jnp.int32, (128, ROWS), 0)
    best = jnp.full((1, ROWS), -1.0, jnp.float32)
    parts = []
    rest = values
    for piece in range(3):
        parts.append(rest.astype(jnp.bfloat16))
        rest = rest - parts[-1].astype(jnp.float32)
    parts = jnp.concatenate(parts, axis=0)
    for far in range(3):
        chip, serving = chip_of(group, (rank + far * step) & 3)
        away = (serving != core).astype(jnp.int32)
        pick = jnp.where(device_of == chip + CHIPS * away, 1.0, 0.0).astype(jnp.bfloat16)
        found = lax.dot_general(
            parts,
            jnp.concatenate([pick] * 3, axis=0),
            (((0,), (0,)), ((), ())),
            preferred_element_type=jnp.float32,
        )
        wanted = far * 16 + away * SUB + (rank >> 2)
        found = jnp.max(jnp.where(lane_of == wanted, found, -1.0), axis=0, keepdims=True)
        best = jnp.maximum(best, found)
    out_ref[...] = best


def answer(info, mine, sibling):
    return pl.pallas_call(
        answer_kernel,
        out_shape=jax.ShapeDtypeStruct((1, ROWS), jnp.float32),
        in_specs=[pl.BlockSpec(memory_space=pltpu.VMEM)] * 3,
        out_specs=pl.BlockSpec(memory_space=pltpu.VMEM),
        compiler_params=pltpu.CompilerParams(vmem_limit_bytes=VMEM),
        cost_estimate=cost(2 * 3 * 6 * 128 * 256 * ROWS, 3 * 4 * 128 * 128),
        name="answer",
    )(info, mine, sibling)


def local(embeddings, cluster_ids, member_order):
    x, y, z, core = where_am_i()
    ring_place = jnp.where(core == 0, x, y)
    ids, order = cluster_ids.reshape(1, ROWS), member_order.reshape(1, ROWS)

    box, info = prep(embeddings, ids)
    chunk1 = exchange(box.reshape(CHIPS, SUB, D)).reshape(ROWS, D)
    handed, table, theirs = hand(embeddings, info, ids, order)
    handed = send(handed, SIBLING)
    table = table + send(theirs, SIBLING)
    tables = [table[:8]] + [send(table[8 * n : 8 * n + 8], shift(2, n)) for n in range(1, NZ)]
    chunk1, handed, tables = lax.optimization_barrier((chunk1, handed, tables))

    chunk2 = exchange(handed.reshape(CHIPS, SUB, D)).reshape(ROWS, D)
    near1 = send(chunk1[:HALF_ROWS], ring(1)), send(chunk1[HALF_ROWS:], ring(-1))
    far1 = send(near1[0], ring(1)), send(near1[1], ring(-1))
    packed = pack(tables)
    line = jnp.concatenate([packed] + [send(packed, shift(0, n)) for n in range(1, NX)], axis=0)
    keys = ring_keys([line] + [send(line, shift(1, n)) for n in range(1, NY)])

    hold = {}
    for half, part in enumerate("PM"):
        hold[part, 0, 0] = (chunk1, half * HALF_ROWS)
        hold[part, 1, 0], hold[part, 2, 0] = (near1[half], 0), (far1[half], 0)
    pairs, by_place = pair_lists()
    pairs += [((part, 0, chunk),) * 2 for part in "PM" for chunk in range(2)]

    def run(stage, name, befores=()):
        low = [pair for pair in pairs if stage_of(pair) == stage]
        high = list(low)
        for one, other in by_place:
            if stage_of(one) == stage:
                low.append(one)
                high.append(other)
        return similar(hold, keys, low, high, ring_place, befores, name)

    first = run(0, "first")
    chunk2, near1, far1, keys, first = lax.optimization_barrier((chunk2, near1, far1, keys, first))
    own2 = split(chunk2)
    near2 = send(own2[0], ring(1)), send(own2[1], ring(-1))
    for half, part in enumerate("PM"):
        hold[part, 0, 1] = (own2[half], 0)
        hold[part, 1, 0], hold[part, 2, 0] = (near1[half], 0), (far1[half], 0)
    own = run(1, "own")
    near2, own = lax.optimization_barrier((near2, own))
    far2 = send(near2[0], ring(1)), send(near2[1], ring(-1))
    for half, part in enumerate("PM"):
        hold[part, 1, 1], hold[part, 2, 1] = (near2[half], 0), (far2[half], 0)
    near = run(2, "near")
    last = run(3, "far", (first, own, near))
    mine = exchange(last.reshape(CHIPS, 1, 128)).reshape(CHIPS, 128)
    return answer(info, mine, send(mine, SIBLING)).reshape(ROWS)


def solution(mesh):
    return jax.shard_map(
        local,
        mesh=mesh,
        in_specs=(P(AXES, None), P(AXES), P(AXES)),
        out_specs=P(AXES),
        check_vma=False,
    )
```

```python
import functools

import jax
import jax.numpy as jnp
import numpy as np
from jax import lax
from jax.experimental import pallas as pl
from jax.experimental.pallas import tpu as pltpu
from jax.sharding import PartitionSpec as P

AXES = ("dp", "rep")
NX, NY, NZ = 4, 4, 8
CHIPS = NX * NY * NZ
GROUPS = 64
HALF = GROUPS // 2
SUB = 8
ROWS = 1024
D = 768
KEYS = 128
WIDE = D + KEYS
EXTRA = 16
HALF_ROWS = 512
ORDERS = 4096
VMEM = 24 * 1024 * 1024
FULL = 56 * 1024 * 1024


def device(x, y, z, core):
    return ((y * NZ + z) * 2 + core) * NX + x


SAME_CORE = [
    [device(x, y, z, core) for y in range(NY) for z in range(NZ) for x in range(NX)] for core in range(2)
]


def ring(step):
    pairs = []
    for y in range(NY):
        for z in range(NZ):
            for x in range(NX):
                pairs.append((device(x, y, z, 0), device((x + step) % NX, y, z, 0)))
                pairs.append((device(x, y, z, 1), device(x, (y + step) % NY, z, 1)))
    return pairs


SIBLING = [(dp * NX + x, (dp ^ 1) * NX + x) for dp in range(NY * NZ * 2) for x in range(NX)]


def exchange(rows):
    return lax.all_to_all(
        rows, AXES, split_axis=0, concat_axis=0, tiled=True, axis_index_groups=SAME_CORE
    )


def send(rows, pairs):
    return lax.ppermute(rows, AXES, pairs)


def cost(flops, size):
    return pl.CostEstimate(flops=flops, bytes_accessed=size, transcendentals=0)


def chip_of(group, place):
    core = (group >= HALF).astype(jnp.int32)
    inner = group - HALF * core
    on_x = inner * NX + place
    on_y = (place * NZ + (inner & (NZ - 1))) * NX + (inner >> 3)
    return jnp.where(core == 0, on_x, on_y), core


def key_rows(ids, order, first):
    key = (ids & 1) * ORDERS + order
    which = lax.broadcasted_iota(jnp.int32, (KEYS, ids.shape[1]), 0)
    high, low = (key >> 7) + 1, key & 127
    return jnp.where(which == first, high, jnp.where(which == first + 1, low, 0)).astype(jnp.float32).astype(
        jnp.bfloat16
    )


def where_am_i():
    dp = lax.axis_index("dp")
    return lax.axis_index("rep"), dp >> 4, (dp >> 1) & (NZ - 1), dp & 1


def slots_of(info, core, mine):
    group, rank = info[0:1], info[1:2]
    chip, serving = chip_of(group, rank & 3)
    slot = chip * SUB + (rank >> 2)
    return jnp.where((serving == core) if mine else (serving != core), slot, -1)


def onehot(slot, first, count):
    rows = lax.broadcasted_iota(jnp.int32, (count, ROWS), 0) + first
    return jnp.where(rows == slot, 1.0, 0.0).astype(jnp.bfloat16)


def normalize(rows):
    wide = rows.astype(jnp.float32)
    scale = 1.0 / jnp.sqrt(jnp.sum(wide * wide, axis=1, keepdims=True) + 1e-06)
    return (wide * scale).astype(jnp.bfloat16)


PIECE = 512
PIECES = ROWS // PIECE
SPAN = 256


def prep_kernel(emb_ref, ids_ref, box_ref, info_ref, rows, out, in_sem, out_sems):
    load = pltpu.make_async_copy(emb_ref, rows, in_sem)
    load.start()
    group = ids_ref[...] >> 1
    member = lax.broadcasted_iota(jnp.int32, (GROUPS, ROWS), 0) == group
    hot = jnp.where(member, 1.0, 0.0)
    earlier = jnp.where(
        lax.broadcasted_iota(jnp.int32, (SPAN, SPAN), 0) < lax.broadcasted_iota(jnp.int32, (SPAN, SPAN), 1), 1.0, 0.0
    ).astype(jnp.bfloat16)
    before = jnp.zeros((GROUPS, 1), jnp.float32)
    ranks = []
    for n in range(ROWS // SPAN):
        here = hot[:, n * SPAN : (n + 1) * SPAN]
        count = jnp.dot(here.astype(jnp.bfloat16), earlier, preferred_element_type=jnp.float32) + before
        ranks.append(jnp.sum(here * count, axis=0, keepdims=True))
        before = before + jnp.sum(here, axis=1, keepdims=True)
    rank = jnp.concatenate(ranks, axis=1).astype(jnp.int32)
    which = lax.broadcasted_iota(jnp.int32, (8, ROWS), 0)
    info = jnp.where(which == 0, group, jnp.where(which == 1, rank, 0))
    info_ref[...] = info
    slot = slots_of(info, where_am_i()[3], True)
    load.wait()
    stores = []
    for n in range(PIECES):
        piece = pl.ds(n * PIECE, PIECE)
        pick = onehot(slot, n * PIECE, PIECE)
        out[piece] = jnp.dot(pick, rows[...], preferred_element_type=jnp.float32).astype(jnp.bfloat16)
        stores.append(pltpu.make_async_copy(out.at[piece], box_ref.at[piece], out_sems.at[n]))
        stores[-1].start()
    for store in stores:
        store.wait()


def prep(embeddings, ids):
    return pl.pallas_call(
        prep_kernel,
        out_shape=(
            jax.ShapeDtypeStruct((ROWS, D), jnp.bfloat16),
            jax.ShapeDtypeStruct((8, ROWS), jnp.int32),
        ),
        in_specs=[pl.BlockSpec(memory_space=pl.ANY), pl.BlockSpec(memory_space=pltpu.VMEM)],
        out_specs=(pl.BlockSpec(memory_space=pl.ANY), pl.BlockSpec(memory_space=pltpu.VMEM)),
        scratch_shapes=[
            pltpu.VMEM((ROWS, D), jnp.bfloat16),
            pltpu.VMEM((ROWS, D), jnp.bfloat16),
            pltpu.SemaphoreType.DMA,
            pltpu.SemaphoreType.DMA((PIECES,)),
        ],
        compiler_params=pltpu.CompilerParams(vmem_limit_bytes=FULL),
        cost_estimate=cost(2 * ROWS * ROWS * D, 4 * ROWS * D),
        name="prep",
    )(embeddings, ids)


def hand_kernel(emb_ref, info_ref, ids_ref, order_ref, box_ref, slab_ref):
    info, core = info_ref[...], where_am_i()[3]
    ids, order = ids_ref[...], order_ref[...]

    def keys(pick, first):
        return lax.dot_general(
            pick, key_rows(ids, order, first), (((1,), (1,)), ((), ())), preferred_element_type=jnp.float32
        ).astype(jnp.bfloat16)

    pick = onehot(slots_of(info, core, False), 0, ROWS)
    box_ref[:, :D] = jnp.dot(pick, normalize(emb_ref[...]), preferred_element_type=jnp.float32).astype(jnp.bfloat16)
    box_ref[:, D:] = keys(pick, 0)
    slab_ref[...] = keys(onehot(slots_of(info, core, True), 0, ROWS), 2)


def hand(embeddings, info, ids, order):
    return pl.pallas_call(
        hand_kernel,
        out_shape=(
            jax.ShapeDtypeStruct((ROWS, WIDE), jnp.bfloat16),
            jax.ShapeDtypeStruct((ROWS, KEYS), jnp.bfloat16),
        ),
        in_specs=[pl.BlockSpec(memory_space=pltpu.VMEM)] * 4,
        out_specs=tuple([pl.BlockSpec(memory_space=pltpu.VMEM)] * 2),
        compiler_params=pltpu.CompilerParams(vmem_limit_bytes=VMEM),
        cost_estimate=cost(2 * ROWS * ROWS * WIDE, 4 * ROWS * D),
        name="hand",
    )(embeddings, info, ids, order)


def stamp_kernel(box_ref, slab_ref, out_ref):
    out_ref[...] = box_ref[...] + slab_ref[...]


def stamp(box, slab):
    return pl.pallas_call(
        stamp_kernel,
        grid=(1,),
        out_shape=jax.ShapeDtypeStruct(box.shape, box.dtype),
        in_specs=[
            pl.BlockSpec((ROWS, KEYS), lambda i: (0, D // KEYS)),
            pl.BlockSpec((ROWS, KEYS), lambda i: (0, 0)),
        ],
        out_specs=pl.BlockSpec((ROWS, KEYS), lambda i: (0, D // KEYS)),
        input_output_aliases={0: 0},
        compiler_params=pltpu.CompilerParams(vmem_limit_bytes=VMEM),
        cost_estimate=cost(0, 3 * 2 * ROWS * KEYS),
        name="stamp",
    )(box, slab)


def settle_kernel(rows_ref, p_ref, m_ref):
    p_ref[...] = normalize(rows_ref[:HALF_ROWS])
    m_ref[...] = normalize(rows_ref[HALF_ROWS:])


def settle(rows):
    return pl.pallas_call(
        settle_kernel,
        out_shape=tuple([jax.ShapeDtypeStruct((HALF_ROWS, D), jnp.bfloat16)] * 2),
        in_specs=[pl.BlockSpec(memory_space=pltpu.VMEM)],
        out_specs=tuple([pl.BlockSpec(memory_space=pltpu.VMEM)] * 2),
        compiler_params=pltpu.CompilerParams(vmem_limit_bytes=VMEM),
        cost_estimate=cost(0, 4 * ROWS * D),
        name="settle",
    )(rows)


def split_kernel(both_ref, p_ref, m_ref, key_ref):
    row = lax.broadcasted_iota(jnp.int32, (EXTRA, KEYS), 0)
    lane = lax.broadcasted_iota(jnp.int32, (EXTRA, KEYS), 1)
    source = jnp.where(row < 2, row + 2, jnp.where(row < 4, row - 2, KEYS))
    weight = jnp.where(lane == source, 1.0, 0.0).astype(jnp.bfloat16)
    parts = lax.dot_general(weight, both_ref[:, D:], (((1,), (1,)), ((), ())), preferred_element_type=jnp.float32)
    key_ref[...] = parts
    for out_ref, first in ((p_ref, 0), (m_ref, HALF_ROWS)):
        out_ref[:HALF_ROWS] = both_ref[first : first + HALF_ROWS, :D]
        its = parts[:, first : first + HALF_ROWS]
        out_ref[HALF_ROWS:] = jnp.concatenate([its, jnp.zeros((EXTRA, D - HALF_ROWS), jnp.float32)], axis=1).astype(
            jnp.bfloat16
        )


def split(both):
    return pl.pallas_call(
        split_kernel,
        out_shape=(
            jax.ShapeDtypeStruct((HALF_ROWS + EXTRA, D), jnp.bfloat16),
            jax.ShapeDtypeStruct((HALF_ROWS + EXTRA, D), jnp.bfloat16),
            jax.ShapeDtypeStruct((EXTRA, ROWS), jnp.float32),
        ),
        in_specs=[pl.BlockSpec(memory_space=pltpu.VMEM)],
        out_specs=tuple([pl.BlockSpec(memory_space=pltpu.VMEM)] * 3),
        compiler_params=pltpu.CompilerParams(vmem_limit_bytes=VMEM),
        cost_estimate=cost(0, 4 * ROWS * WIDE),
        name="split",
    )(both)


BLOCKS = [(part, far, chunk) for far in range(3) for chunk in range(2) for part in "PM"]


def pair_lists():
    pairs = []

    def all_chunks(one, other):
        for c in range(2):
            for e in range(2):
                pairs.append((one + (c,), other + (e,)))

    for part in "PM":
        pairs.append(((part, 0, 0), (part, 0, 1)))
        all_chunks((part, 0), (part, 1))
        pairs.append(((part, 0, 1), (part, 2, 0)))
    all_chunks(("P", 0), ("M", 0))
    all_chunks(("P", 0), ("M", 1))
    all_chunks(("P", 1), ("M", 1))
    pairs.append((("P", 1, 0), ("M", 2, 0)))
    pairs.append((("P", 1, 1), ("M", 2, 0)))
    pairs.append((("P", 2, 0), ("M", 1, 1)))
    pairs.append((("P", 1, 1), ("M", 2, 1)))
    by_place = [
        ((("P", 0, 0), ("P", 2, 0)), (("M", 0, 0), ("M", 2, 0))),
        ((("M", 0, 1), ("M", 2, 1)), (("P", 0, 1), ("P", 2, 1))),
    ]
    return pairs, by_place


def stage_of(pair):
    if all(far == 0 for part, far, chunk in pair):
        return 0
    return 2 if any(far == 2 and chunk == 1 for part, far, chunk in pair) else 1


def similar_kernel(blocks, loads, n_tasks, n_keys, n_before, *refs):
    n_arrays = 1 + max(load[0] for load in loads)
    tasks_ref, refs = refs[0], refs[1:]
    arrays, refs = refs[:n_arrays], refs[n_arrays:]
    key_refs, refs = refs[:n_keys], refs[n_keys:]
    befores, refs = refs[:n_before], refs[n_before:]
    out_ref, rows, extra, kcol, ccol, krow, crow, best_row, best_col, s0, s1, sems, key_sems = refs
    n_blocks = len(blocks)

    copies, key_copies = [], []
    for slot, (part, far, chunk, source, rides) in enumerate(blocks):
        if rides:
            key_copies.append(
                pltpu.make_async_copy(arrays[source].at[pl.ds(HALF_ROWS, EXTRA)], extra.at[slot], key_sems.at[slot])
            )
            key_copies[-1].start()
    for number, (array, first, slot) in enumerate(loads):
        copies.append(
            pltpu.make_async_copy(arrays[array].at[pl.ds(first, HALF_ROWS)], rows.at[slot], sems.at[number])
        )
        copies[-1].start()
    for slot in range(n_blocks):
        best_row[slot] = jnp.full((HALF_ROWS, 128), -1.0, jnp.float32)
        best_col[slot] = jnp.full((8, HALF_ROWS), -1.0, jnp.float32)

    def cluster(key):
        return jnp.where(key >= ORDERS + 128, 2.0, jnp.where(key > 0, 1.0, 0.0))

    for copy in key_copies:
        copy.wait()
    for slot, (part, far, chunk, source, rides) in enumerate(blocks):
        if rides:
            parts = extra[slot].astype(jnp.float32)[:, :HALF_ROWS]
        else:
            first = 0 if part == "P" else HALF_ROWS
            parts = key_refs[source][:, first : first + HALF_ROWS]
        key = 128.0 * parts[2 * chunk : 2 * chunk + 1] + parts[2 * chunk + 1 : 2 * chunk + 2]
        krow[slot] = jnp.broadcast_to(key, (8, HALF_ROWS))
        crow[slot] = cluster(krow[slot])
        key = jnp.transpose(jnp.broadcast_to(key, (128, HALF_ROWS)))
        kcol[slot] = key
        ccol[slot] = cluster(key)
    for copy in copies:
        copy.wait()

    def multiply(task, s):
        a, b = tasks_ref[3 * task], tasks_ref[3 * task + 1]
        s[...] = lax.dot_general(rows[a], rows[b], (((1,), (1,)), ((), ())), preferred_element_type=jnp.float32)

    step = 16

    def reduce(task, s):
        a, b, sink = tasks_ref[3 * task], tasks_ref[3 * task + 1], tasks_ref[3 * task + 2]
        kb, cb = krow[b], crow[b]
        for row in range(0, HALF_ROWS, step):
            ka = kcol[a, row : row + step].reshape(step // 8, 8, 128)
            ca = ccol[a, row : row + step].reshape(step // 8, 8, 128)
            best = best_row[a, row : row + step]
            for at in range(0, HALF_ROWS, 128):
                found = s[row : row + step, at : at + 128].reshape(step // 8, 8, 128)
                same = jnp.where(ca == cb[None, :, at : at + 128], found, -1.0)
                later = kb[None, :, at : at + 128] < ka
                best = jnp.maximum(best, jnp.where(later, same, -1.0).reshape(step, 128))
                other = jnp.max(jnp.where(later, -1.0, same), axis=0)
                best_col[sink, :, at : at + 128] = jnp.maximum(best_col[sink, :, at : at + 128], other)
            best_row[a, row : row + step] = best

    def two(turn, carry):
        multiply(2 * turn + 1, s1)
        reduce(2 * turn, s0)
        multiply(2 * turn + 2, s0)
        reduce(2 * turn + 1, s1)
        return carry

    multiply(0, s0)
    if n_tasks > 2:
        lax.fori_loop(0, n_tasks // 2 - 1, two, 0)
    multiply(n_tasks - 1, s1)
    reduce(n_tasks - 2, s0)
    reduce(n_tasks - 1, s1)

    empty = jnp.full((8, HALF_ROWS), -1.0, jnp.float32)
    diagonal = lax.broadcasted_iota(jnp.int32, (8, HALF_ROWS), 0) == (
        lax.broadcasted_iota(jnp.int32, (8, HALF_ROWS), 1) & (SUB - 1)
    )
    for number, part in enumerate("PM"):
        tiles = [empty] * 16
        for slot, (its, far, chunk, source, rides) in enumerate(blocks):
            if its == part:
                by_row = jnp.max(jnp.transpose(best_row[slot]), axis=0, keepdims=True)
                by_col = jnp.max(best_col[slot], axis=0, keepdims=True)
                tiles[2 * far + chunk] = jnp.where(diagonal, jnp.maximum(by_row, by_col), -1.0)
        value = jnp.transpose(jnp.concatenate(tiles, axis=0)).reshape(HALF_ROWS // SUB, SUB, 128)
        value = jnp.max(value, axis=1)
        at = pl.ds(number * (CHIPS // 2), CHIPS // 2)
        for before in befores:
            value = jnp.maximum(value, before[at, :])
        out_ref[at, :] = value


def similar(hold, keys, low, high, ring_place, befores, name):
    blocks = [block for block in BLOCKS if any(block in pair for pair in low + high)]
    place = {block: number for number, block in enumerate(blocks)}
    spare = len(blocks)

    def table(pairs):
        return np.array(
            [(place[a], place[b], spare if a == b else place[b]) for a, b in pairs], np.int32
        ).reshape(-1)

    tasks = jnp.asarray(table(low))
    if low != high:
        tasks = jnp.where(ring_place < 2, tasks, jnp.asarray(table(high)))

    def number_of(array, arrays):
        for number, known in enumerate(arrays):
            if known is array:
                return number
        arrays.append(array)
        return len(arrays) - 1

    arrays, key_arrays, loads, full = [], [], [], []
    for block in blocks:
        array, first = hold[block]
        loads.append((number_of(array, arrays), first, place[block]))
    for block in blocks:
        source, rides = keys[block[:2]]
        full.append(block + (number_of(source, arrays if rides else key_arrays), rides))
    n = len(blocks)
    kernel = functools.partial(similar_kernel, full, loads, len(low), len(key_arrays), len(befores))
    return pl.pallas_call(
        kernel,
        out_shape=jax.ShapeDtypeStruct((CHIPS, 128), jnp.float32),
        in_specs=[pl.BlockSpec(memory_space=pltpu.SMEM)]
        + [pl.BlockSpec(memory_space=pl.ANY)] * len(arrays)
        + [pl.BlockSpec(memory_space=pltpu.VMEM)] * (len(key_arrays) + len(befores)),
        out_specs=pl.BlockSpec(memory_space=pltpu.VMEM),
        scratch_shapes=[
            pltpu.VMEM((n, HALF_ROWS, D), jnp.bfloat16),
            pltpu.VMEM((n, EXTRA, D), jnp.bfloat16),
            pltpu.VMEM((n, HALF_ROWS, 128), jnp.float32),
            pltpu.VMEM((n, HALF_ROWS, 128), jnp.float32),
            pltpu.VMEM((n, 8, HALF_ROWS), jnp.float32),
            pltpu.VMEM((n, 8, HALF_ROWS), jnp.float32),
            pltpu.VMEM((n, HALF_ROWS, 128), jnp.float32),
            pltpu.VMEM((n + 1, 8, HALF_ROWS), jnp.float32),
            pltpu.VMEM((HALF_ROWS, HALF_ROWS), jnp.float32),
            pltpu.VMEM((HALF_ROWS, HALF_ROWS), jnp.float32),
            pltpu.SemaphoreType.DMA((n,)),
            pltpu.SemaphoreType.DMA((n,)),
        ],
        compiler_params=pltpu.CompilerParams(vmem_limit_bytes=32 * 1024 * 1024),
        cost_estimate=cost(2 * D * HALF_ROWS * HALF_ROWS * len(low), 2 * len(loads) * HALF_ROWS * D),
        name=name,
    )(tasks, *arrays, *key_arrays, *befores)


def answer_kernel(away, info_ref, values_ref, *refs):
    info, out_ref = info_ref[...], refs[-1]
    group, rank = info[0:1], info[1:2]
    x, y, z, core = where_am_i()
    step = jnp.where((y * NZ + z) * NX + x < CHIPS // 2, 1, -1)
    device_of = lax.broadcasted_iota(jnp.int32, (CHIPS, ROWS), 0)
    lane_of = lax.broadcasted_iota(jnp.int32, (128, ROWS), 0)
    parts = []
    rest = values_ref[...]
    for piece in range(3):
        parts.append(rest.astype(jnp.bfloat16))
        rest = rest - parts[-1].astype(jnp.float32)
    parts = jnp.concatenate(parts, axis=0)
    best = refs[0][...] if away else jnp.full((1, ROWS), -1.0, jnp.float32)
    for far in range(3):
        chip, serving = chip_of(group, (rank + far * step) & 3)
        here = (serving != core) if away else (serving == core)
        pick = jnp.where(device_of == jnp.where(here, chip, -1), 1.0, 0.0).astype(jnp.bfloat16)
        found = lax.dot_general(
            parts,
            jnp.concatenate([pick] * 3, axis=0),
            (((0,), (0,)), ((), ())),
            preferred_element_type=jnp.float32,
        )
        wanted = jnp.where(here, far * 16 + away * SUB + (rank >> 2), -1)
        found = jnp.max(jnp.where(lane_of == wanted, found, -1.0), axis=0, keepdims=True)
        best = jnp.maximum(best, found)
    out_ref[...] = best


def answer(away, info, values, *before):
    return pl.pallas_call(
        functools.partial(answer_kernel, away),
        out_shape=jax.ShapeDtypeStruct((1, ROWS), jnp.float32),
        in_specs=[pl.BlockSpec(memory_space=pltpu.VMEM)] * (2 + len(before)),
        out_specs=pl.BlockSpec(memory_space=pltpu.VMEM),
        compiler_params=pltpu.CompilerParams(vmem_limit_bytes=VMEM),
        cost_estimate=cost(2 * 3 * 3 * 128 * 128 * ROWS, 4 * 128 * 128),
        name="answer",
    )(info, values, *before)


def local(embeddings, cluster_ids, member_order):
    x, y, z, core = where_am_i()
    ring_place = jnp.where(core == 0, x, y)
    ids, order = cluster_ids.reshape(1, ROWS), member_order.reshape(1, ROWS)

    box, info = prep(embeddings, ids)
    chunk1 = exchange(box.reshape(CHIPS, SUB, D)).reshape(ROWS, D)
    handed, slab = hand(embeddings, info, ids, order)
    handed = stamp(send(handed, SIBLING), slab)
    chunk1, handed = lax.optimization_barrier((chunk1, handed))
    chunk2 = exchange(handed.reshape(CHIPS, SUB, WIDE)).reshape(ROWS, WIDE)
    own1 = settle(chunk1)
    near1 = send(own1[0], ring(1)), send(own1[1], ring(-1))
    far1 = send(near1[0], ring(1)), send(near1[1], ring(-1))
    chunk2, own1, near1, far1 = lax.optimization_barrier((chunk2, own1, near1, far1))
    *own2, key = split(chunk2)
    near2 = send(own2[0], ring(1)), send(own2[1], ring(-1))
    far_key = send(key, ring(2))

    hold, keys = {}, {}
    for half, part in enumerate("PM"):
        hold[part, 0, 0], hold[part, 0, 1] = (own1[half], 0), (own2[half], 0)
        hold[part, 1, 0], hold[part, 2, 0] = (near1[half], 0), (far1[half], 0)
        keys[part, 0], keys[part, 2] = (key, False), (far_key, False)

    pairs, by_place = pair_lists()
    answers = []
    for stage in range(3):
        low = [pair for pair in pairs if stage_of(pair) == stage]
        if stage == 0:
            low += [((part, 0, chunk),) * 2 for part in "PM" for chunk in range(2)]
        high = list(low)
        for one, other in by_place:
            if stage_of(one) == stage:
                low.append(one)
                high.append(other)
        answers.append(
            similar(hold, keys, low, high, ring_place, answers if stage == 2 else [], ("own", "near", "far")[stage])
        )
        if stage == 0:
            near2, answers[0] = lax.optimization_barrier((near2, answers[0]))
            far2 = send(near2[0], ring(1)), send(near2[1], ring(-1))
            for half, part in enumerate("PM"):
                hold[part, 1, 1], hold[part, 2, 1] = (near2[half], 0), (far2[half], 0)
                keys[part, 1] = (near2[half], True)
    mine = exchange(answers[2].reshape(CHIPS, 1, 128)).reshape(CHIPS, 128)
    best = answer(0, info, mine)
    return answer(1, info, send(mine, SIBLING), best).reshape(ROWS)


def solution(mesh):
    return jax.shard_map(
        local,
        mesh=mesh,
        in_specs=(P(AXES, None), P(AXES), P(AXES)),
        out_specs=P(AXES),
        check_vma=False,
    )
```

```python
import functools

import jax
import jax.numpy as jnp
import numpy as np
from jax import lax
from jax.experimental import pallas as pl
from jax.experimental.pallas import tpu as pltpu
from jax.sharding import PartitionSpec as P

AXES = ("dp", "rep")
NX, NY, NZ = 4, 4, 8
CHIPS = NX * NY * NZ
GROUPS = 64
HALF = GROUPS // 2
SOURCES = 32
CAP = 32
ROWS = 1024
D = 768
KEYS = 128
WIDE = D + KEYS
EXTRA = 16
HALF_ROWS = 512
ORDERS = 4096
VMEM = 24 * 1024 * 1024
FULL = 56 * 1024 * 1024


def device(x, y, z, core):
    return ((y * NZ + z) * 2 + core) * NX + x


ROUTES = [[device(x, y, z, 0) for y in range(NY) for z in range(NZ)] for x in range(NX)] + [
    [device(x, y, z, 1) for x in range(NX) for z in range(NZ)] for y in range(NY)
]
RETURNS = [
    [device(x, y, z, 0) for y in range(NY) for z in range(NZ) for x in range(NX)],
    [device(x, y, z, 1) for x in range(NX) for z in range(NZ) for y in range(NY)],
]


def ring(step):
    pairs = []
    for y in range(NY):
        for z in range(NZ):
            for x in range(NX):
                pairs.append((device(x, y, z, 0), device((x + step) % NX, y, z, 0)))
                pairs.append((device(x, y, z, 1), device(x, (y + step) % NY, z, 1)))
    return pairs


SIBLING = [(dp * NX + x, (dp ^ 1) * NX + x) for dp in range(NY * NZ * 2) for x in range(NX)]


def exchange(rows, groups):
    return lax.all_to_all(rows, AXES, split_axis=0, concat_axis=0, tiled=True, axis_index_groups=groups)


def send(rows, pairs):
    return lax.ppermute(rows, AXES, pairs)


def cost(flops, size):
    return pl.CostEstimate(flops=flops, bytes_accessed=size, transcendentals=0)


def key_rows(ids, order, first):
    key = (ids & 1) * ORDERS + order
    which = lax.broadcasted_iota(jnp.int32, (KEYS, ids.shape[1]), 0)
    high, low = (key >> 7) + 1, key & 127
    return jnp.where(which == first, high, jnp.where(which == first + 1, low, 0)).astype(jnp.float32).astype(
        jnp.bfloat16
    )


def where_am_i():
    dp = lax.axis_index("dp")
    return lax.axis_index("rep"), dp >> 4, (dp >> 1) & (NZ - 1), dp & 1


def slots_of(info, core, mine):
    group, rank = info[0:1], info[1:2]
    serving = group >> 5
    slot = (group & (HALF - 1)) * CAP + rank
    return jnp.where((serving == core) if mine else (serving != core), slot, -1)


def onehot(slot, first, count):
    rows = lax.broadcasted_iota(jnp.int32, (count, ROWS), 0) + first
    return jnp.where(rows == slot, 1.0, 0.0).astype(jnp.bfloat16)


def normalize(rows):
    wide = rows.astype(jnp.float32)
    scale = 1.0 / jnp.sqrt(jnp.sum(wide * wide, axis=1, keepdims=True) + 1e-06)
    return (wide * scale).astype(jnp.bfloat16)


PIECE = 512
PIECES = ROWS // PIECE
SPAN = 256


def prep_kernel(emb_ref, ids_ref, box_ref, info_ref, rows, out, in_sem, out_sems):
    load = pltpu.make_async_copy(emb_ref, rows, in_sem)
    load.start()
    group = ids_ref[...] >> 1
    member = lax.broadcasted_iota(jnp.int32, (GROUPS, ROWS), 0) == group
    hot = jnp.where(member, 1.0, 0.0)
    earlier = jnp.where(
        lax.broadcasted_iota(jnp.int32, (SPAN, SPAN), 0) < lax.broadcasted_iota(jnp.int32, (SPAN, SPAN), 1), 1.0, 0.0
    ).astype(jnp.bfloat16)
    before = jnp.zeros((GROUPS, 1), jnp.float32)
    ranks = []
    for n in range(ROWS // SPAN):
        here = hot[:, n * SPAN : (n + 1) * SPAN]
        count = jnp.dot(here.astype(jnp.bfloat16), earlier, preferred_element_type=jnp.float32) + before
        ranks.append(jnp.sum(here * count, axis=0, keepdims=True))
        before = before + jnp.sum(here, axis=1, keepdims=True)
    rank = jnp.concatenate(ranks, axis=1).astype(jnp.int32)
    which = lax.broadcasted_iota(jnp.int32, (8, ROWS), 0)
    info = jnp.where(which == 0, group, jnp.where(which == 1, rank, 0))
    info_ref[...] = info
    slot = slots_of(info, where_am_i()[3], True)
    load.wait()
    stores = []
    for n in range(PIECES):
        piece = pl.ds(n * PIECE, PIECE)
        pick = onehot(slot, n * PIECE, PIECE)
        out[piece] = jnp.dot(pick, rows[...], preferred_element_type=jnp.float32).astype(jnp.bfloat16)
        stores.append(pltpu.make_async_copy(out.at[piece], box_ref.at[piece], out_sems.at[n]))
        stores[-1].start()
    for store in stores:
        store.wait()


def prep(embeddings, ids):
    return pl.pallas_call(
        prep_kernel,
        out_shape=(
            jax.ShapeDtypeStruct((ROWS, D), jnp.bfloat16),
            jax.ShapeDtypeStruct((8, ROWS), jnp.int32),
        ),
        in_specs=[pl.BlockSpec(memory_space=pl.ANY), pl.BlockSpec(memory_space=pltpu.VMEM)],
        out_specs=(pl.BlockSpec(memory_space=pl.ANY), pl.BlockSpec(memory_space=pltpu.VMEM)),
        scratch_shapes=[
            pltpu.VMEM((ROWS, D), jnp.bfloat16),
            pltpu.VMEM((ROWS, D), jnp.bfloat16),
            pltpu.SemaphoreType.DMA,
            pltpu.SemaphoreType.DMA((PIECES,)),
        ],
        compiler_params=pltpu.CompilerParams(vmem_limit_bytes=FULL),
        cost_estimate=cost(2 * ROWS * ROWS * D, 4 * ROWS * D),
        name="prep",
    )(embeddings, ids)


def hand_kernel(emb_ref, info_ref, ids_ref, order_ref, box_ref, slab_ref):
    info, core = info_ref[...], where_am_i()[3]
    ids, order = ids_ref[...], order_ref[...]

    def keys(pick, first):
        return lax.dot_general(
            pick, key_rows(ids, order, first), (((1,), (1,)), ((), ())), preferred_element_type=jnp.float32
        ).astype(jnp.bfloat16)

    pick = onehot(slots_of(info, core, False), 0, ROWS)
    box_ref[:, :D] = jnp.dot(pick, normalize(emb_ref[...]), preferred_element_type=jnp.float32).astype(jnp.bfloat16)
    box_ref[:, D:] = keys(pick, 0)
    slab_ref[...] = keys(onehot(slots_of(info, core, True), 0, ROWS), 2)


def hand(embeddings, info, ids, order):
    return pl.pallas_call(
        hand_kernel,
        out_shape=(
            jax.ShapeDtypeStruct((ROWS, WIDE), jnp.bfloat16),
            jax.ShapeDtypeStruct((ROWS, KEYS), jnp.bfloat16),
        ),
        in_specs=[pl.BlockSpec(memory_space=pltpu.VMEM)] * 4,
        out_specs=tuple([pl.BlockSpec(memory_space=pltpu.VMEM)] * 2),
        compiler_params=pltpu.CompilerParams(vmem_limit_bytes=VMEM),
        cost_estimate=cost(2 * ROWS * ROWS * WIDE, 4 * ROWS * D),
        name="hand",
    )(embeddings, info, ids, order)


def stamp_kernel(box_ref, slab_ref, out_ref):
    out_ref[...] = box_ref[...] + slab_ref[...]


def stamp(box, slab):
    return pl.pallas_call(
        stamp_kernel,
        grid=(1,),
        out_shape=jax.ShapeDtypeStruct(box.shape, box.dtype),
        in_specs=[
            pl.BlockSpec((ROWS, KEYS), lambda i: (0, D // KEYS)),
            pl.BlockSpec((ROWS, KEYS), lambda i: (0, 0)),
        ],
        out_specs=pl.BlockSpec((ROWS, KEYS), lambda i: (0, D // KEYS)),
        input_output_aliases={0: 0},
        compiler_params=pltpu.CompilerParams(vmem_limit_bytes=VMEM),
        cost_estimate=cost(0, 3 * 2 * ROWS * KEYS),
        name="stamp",
    )(box, slab)


def settle_kernel(rows_ref, p_ref, m_ref):
    p_ref[...] = normalize(rows_ref[:HALF_ROWS])
    m_ref[...] = normalize(rows_ref[HALF_ROWS:])


def settle(rows):
    return pl.pallas_call(
        settle_kernel,
        out_shape=tuple([jax.ShapeDtypeStruct((HALF_ROWS, D), jnp.bfloat16)] * 2),
        in_specs=[pl.BlockSpec(memory_space=pltpu.VMEM)],
        out_specs=tuple([pl.BlockSpec(memory_space=pltpu.VMEM)] * 2),
        compiler_params=pltpu.CompilerParams(vmem_limit_bytes=VMEM),
        cost_estimate=cost(0, 4 * ROWS * D),
        name="settle",
    )(rows)


def split_kernel(both_ref, p_ref, m_ref, key_ref):
    row = lax.broadcasted_iota(jnp.int32, (EXTRA, KEYS), 0)
    lane = lax.broadcasted_iota(jnp.int32, (EXTRA, KEYS), 1)
    source = jnp.where(row < 2, row + 2, jnp.where(row < 4, row - 2, KEYS))
    weight = jnp.where(lane == source, 1.0, 0.0).astype(jnp.bfloat16)
    parts = lax.dot_general(weight, both_ref[:, D:], (((1,), (1,)), ((), ())), preferred_element_type=jnp.float32)
    key_ref[...] = parts
    for out_ref, first in ((p_ref, 0), (m_ref, HALF_ROWS)):
        out_ref[:HALF_ROWS] = both_ref[first : first + HALF_ROWS, :D]
        its = parts[:, first : first + HALF_ROWS]
        out_ref[HALF_ROWS:] = jnp.concatenate([its, jnp.zeros((EXTRA, D - HALF_ROWS), jnp.float32)], axis=1).astype(
            jnp.bfloat16
        )


def split(both):
    return pl.pallas_call(
        split_kernel,
        out_shape=(
            jax.ShapeDtypeStruct((HALF_ROWS + EXTRA, D), jnp.bfloat16),
            jax.ShapeDtypeStruct((HALF_ROWS + EXTRA, D), jnp.bfloat16),
            jax.ShapeDtypeStruct((EXTRA, ROWS), jnp.float32),
        ),
        in_specs=[pl.BlockSpec(memory_space=pltpu.VMEM)],
        out_specs=tuple([pl.BlockSpec(memory_space=pltpu.VMEM)] * 3),
        compiler_params=pltpu.CompilerParams(vmem_limit_bytes=VMEM),
        cost_estimate=cost(0, 4 * ROWS * WIDE),
        name="split",
    )(both)


BLOCKS = [(part, far, chunk) for far in range(3) for chunk in range(2) for part in "PM"]


def pair_lists():
    pairs = []

    def all_chunks(one, other):
        for c in range(2):
            for e in range(2):
                pairs.append((one + (c,), other + (e,)))

    for part in "PM":
        pairs.append(((part, 0, 0), (part, 0, 1)))
        all_chunks((part, 0), (part, 1))
        pairs.append(((part, 0, 1), (part, 2, 0)))
    all_chunks(("P", 0), ("M", 0))
    all_chunks(("P", 0), ("M", 1))
    all_chunks(("P", 1), ("M", 1))
    pairs.append((("P", 1, 0), ("M", 2, 0)))
    pairs.append((("P", 1, 1), ("M", 2, 0)))
    pairs.append((("P", 2, 0), ("M", 1, 1)))
    pairs.append((("P", 1, 1), ("M", 2, 1)))
    by_place = [
        ((("P", 0, 0), ("P", 2, 0)), (("M", 0, 0), ("M", 2, 0))),
        ((("M", 0, 1), ("M", 2, 1)), (("P", 0, 1), ("P", 2, 1))),
    ]
    return pairs, by_place


def stage_of(pair):
    if all(far == 0 for part, far, chunk in pair):
        return 0
    return 2 if any(far == 2 and chunk == 1 for part, far, chunk in pair) else 1


def three_parts(values):
    parts = []
    for piece in range(3):
        parts.append(values.astype(jnp.bfloat16))
        values = values - parts[-1].astype(jnp.float32)
    return parts


def similar_kernel(blocks, loads, n_tasks, n_keys, n_before, *refs):
    n_arrays = 1 + max(load[0] for load in loads)
    tasks_ref, refs = refs[0], refs[1:]
    arrays, refs = refs[:n_arrays], refs[n_arrays:]
    key_refs, refs = refs[:n_keys], refs[n_keys:]
    befores, refs = refs[:n_before], refs[n_before:]
    out_ref, rows, extra, kcol, ccol, krow, crow, best_row, best_col, s0, s1, sems, key_sems = refs
    n_blocks = len(blocks)

    copies, key_copies = [], []
    for slot, (part, far, chunk, source, rides) in enumerate(blocks):
        if rides:
            key_copies.append(
                pltpu.make_async_copy(arrays[source].at[pl.ds(HALF_ROWS, EXTRA)], extra.at[slot], key_sems.at[slot])
            )
            key_copies[-1].start()
    for number, (array, first, slot) in enumerate(loads):
        copies.append(
            pltpu.make_async_copy(arrays[array].at[pl.ds(first, HALF_ROWS)], rows.at[slot], sems.at[number])
        )
        copies[-1].start()
    for slot in range(n_blocks):
        best_row[slot] = jnp.full((HALF_ROWS, 128), -1.0, jnp.float32)
        best_col[slot] = jnp.full((8, HALF_ROWS), -1.0, jnp.float32)

    def cluster(key):
        return jnp.where(key >= ORDERS + 128, 2.0, jnp.where(key > 0, 1.0, 0.0))

    for copy in key_copies:
        copy.wait()
    for slot, (part, far, chunk, source, rides) in enumerate(blocks):
        if rides:
            parts = extra[slot].astype(jnp.float32)[:, :HALF_ROWS]
        else:
            first = 0 if part == "P" else HALF_ROWS
            parts = key_refs[source][:, first : first + HALF_ROWS]
        key = 128.0 * parts[2 * chunk : 2 * chunk + 1] + parts[2 * chunk + 1 : 2 * chunk + 2]
        krow[slot] = jnp.broadcast_to(key, (8, HALF_ROWS))
        crow[slot] = cluster(krow[slot])
        key = jnp.transpose(jnp.broadcast_to(key, (128, HALF_ROWS)))
        kcol[slot] = key
        ccol[slot] = cluster(key)
    for copy in copies:
        copy.wait()

    def multiply(task, s):
        a, b = tasks_ref[3 * task], tasks_ref[3 * task + 1]
        s[...] = lax.dot_general(rows[a], rows[b], (((1,), (1,)), ((), ())), preferred_element_type=jnp.float32)

    step = 16

    def reduce(task, s):
        a, b, sink = tasks_ref[3 * task], tasks_ref[3 * task + 1], tasks_ref[3 * task + 2]
        kb, cb = krow[b], crow[b]
        for row in range(0, HALF_ROWS, step):
            ka = kcol[a, row : row + step].reshape(step // 8, 8, 128)
            ca = ccol[a, row : row + step].reshape(step // 8, 8, 128)
            best = best_row[a, row : row + step]
            for at in range(0, HALF_ROWS, 128):
                found = s[row : row + step, at : at + 128].reshape(step // 8, 8, 128)
                same = jnp.where(ca == cb[None, :, at : at + 128], found, -1.0)
                later = kb[None, :, at : at + 128] < ka
                best = jnp.maximum(best, jnp.where(later, same, -1.0).reshape(step, 128))
                other = jnp.max(jnp.where(later, -1.0, same), axis=0)
                best_col[sink, :, at : at + 128] = jnp.maximum(best_col[sink, :, at : at + 128], other)
            best_row[a, row : row + step] = best

    def two(turn, carry):
        multiply(2 * turn + 1, s1)
        reduce(2 * turn, s0)
        multiply(2 * turn + 2, s0)
        reduce(2 * turn + 1, s1)
        return carry

    multiply(0, s0)
    if n_tasks > 2:
        lax.fori_loop(0, n_tasks // 2 - 1, two, 0)
    multiply(n_tasks - 1, s1)
    reduce(n_tasks - 2, s0)
    reduce(n_tasks - 1, s1)

    empty = jnp.full((CAP, HALF_ROWS), -1.0, jnp.float32)
    diagonal = lax.broadcasted_iota(jnp.int32, (CAP, HALF_ROWS), 0) == (
        lax.broadcasted_iota(jnp.int32, (CAP, HALF_ROWS), 1) & (CAP - 1)
    )
    values = {}
    for number, part in enumerate("PM"):
        for level in range(2):
            tiles = [empty] * 4
            for slot, (its, far, chunk, source, rides) in enumerate(blocks):
                if its == part and far // 2 == level:
                    by_row = jnp.max(jnp.transpose(best_row[slot]), axis=0, keepdims=True)
                    by_col = jnp.max(best_col[slot], axis=0, keepdims=True)
                    tiles[2 * (far & 1) + chunk] = jnp.where(diagonal, jnp.maximum(by_row, by_col), -1.0)
            if all(tile is empty for tile in tiles):
                value = jnp.full((HALF_ROWS // CAP, 128), -1.0, jnp.float32)
            else:
                value = jnp.transpose(jnp.concatenate(tiles, axis=0)).reshape(HALF_ROWS // CAP, CAP, 128)
                value = jnp.max(value, axis=1)
            at = pl.ds(level * SOURCES + number * (SOURCES // 2), SOURCES // 2)
            for before in befores:
                value = jnp.maximum(value, before[at, :])
            values[level, number] = value
    values = jnp.concatenate([values[level, number] for level in range(2) for number in range(2)], axis=0)
    if not befores:
        out_ref[...] = values
        return
    x, y, z, core = where_am_i()
    here = jnp.where(core == 0, x, y)
    row = lax.broadcasted_iota(jnp.int32, (CHIPS, 2 * SOURCES), 0)
    column = lax.broadcasted_iota(jnp.int32, (CHIPS, 2 * SOURCES), 1)
    source, step = row >> 2, jnp.where(row < CHIPS // 2, 1, -1)
    far = ((here - (row & 3)) * step) & 3
    wanted = (column == source) & (far < 2) | (column == source + SOURCES) & (far == 2)
    pick = jnp.where(wanted, 1.0, 0.0).astype(jnp.bfloat16)
    out_ref[...] = jnp.dot(
        jnp.concatenate([pick] * 3, axis=1),
        jnp.concatenate(three_parts(values), axis=0),
        preferred_element_type=jnp.float32,
    )


def similar(hold, keys, low, high, ring_place, befores, name):
    blocks = [block for block in BLOCKS if any(block in pair for pair in low + high)]
    place = {block: number for number, block in enumerate(blocks)}
    spare = len(blocks)

    def table(pairs):
        return np.array(
            [(place[a], place[b], spare if a == b else place[b]) for a, b in pairs], np.int32
        ).reshape(-1)

    tasks = jnp.asarray(table(low))
    if low != high:
        tasks = jnp.where(ring_place < 2, tasks, jnp.asarray(table(high)))

    def number_of(array, arrays):
        for number, known in enumerate(arrays):
            if known is array:
                return number
        arrays.append(array)
        return len(arrays) - 1

    arrays, key_arrays, loads, full = [], [], [], []
    for block in blocks:
        array, first = hold[block]
        loads.append((number_of(array, arrays), first, place[block]))
    for block in blocks:
        source, rides = keys[block[:2]]
        full.append(block + (number_of(source, arrays if rides else key_arrays), rides))
    n = len(blocks)
    kernel = functools.partial(similar_kernel, full, loads, len(low), len(key_arrays), len(befores))
    return pl.pallas_call(
        kernel,
        out_shape=jax.ShapeDtypeStruct((CHIPS if befores else 2 * SOURCES, 128), jnp.float32),
        in_specs=[pl.BlockSpec(memory_space=pltpu.SMEM)]
        + [pl.BlockSpec(memory_space=pl.ANY)] * len(arrays)
        + [pl.BlockSpec(memory_space=pltpu.VMEM)] * (len(key_arrays) + len(befores)),
        out_specs=pl.BlockSpec(memory_space=pltpu.VMEM),
        scratch_shapes=[
            pltpu.VMEM((n, HALF_ROWS, D), jnp.bfloat16),
            pltpu.VMEM((n, EXTRA, D), jnp.bfloat16),
            pltpu.VMEM((n, HALF_ROWS, 128), jnp.float32),
            pltpu.VMEM((n, HALF_ROWS, 128), jnp.float32),
            pltpu.VMEM((n, 8, HALF_ROWS), jnp.float32),
            pltpu.VMEM((n, 8, HALF_ROWS), jnp.float32),
            pltpu.VMEM((n, HALF_ROWS, 128), jnp.float32),
            pltpu.VMEM((n + 1, 8, HALF_ROWS), jnp.float32),
            pltpu.VMEM((HALF_ROWS, HALF_ROWS), jnp.float32),
            pltpu.VMEM((HALF_ROWS, HALF_ROWS), jnp.float32),
            pltpu.SemaphoreType.DMA((n,)),
            pltpu.SemaphoreType.DMA((n,)),
        ],
        compiler_params=pltpu.CompilerParams(vmem_limit_bytes=32 * 1024 * 1024),
        cost_estimate=cost(2 * D * HALF_ROWS * HALF_ROWS * len(low), 2 * len(loads) * HALF_ROWS * D),
        name=name,
    )(tasks, *arrays, *key_arrays, *befores)


def answer_kernel(away, info_ref, values_ref, *refs):
    info, out_ref = info_ref[...], refs[-1]
    group, rank = info[0:1], info[1:2]
    x, y, z, core = where_am_i()
    serving = (core + away) & 1
    here = (group >> 5) == serving
    ring_place, source = jnp.where(serving == 0, x, y), jnp.where(serving == 0, y, x)
    step = jnp.where(source < 2, 1, -1)
    device_of = lax.broadcasted_iota(jnp.int32, (CHIPS, ROWS), 0)
    lane_of = lax.broadcasted_iota(jnp.int32, (128, ROWS), 0)
    parts = jnp.concatenate(three_parts(values_ref[...]), axis=0)
    best = refs[0][...] if away else jnp.full((1, ROWS), -1.0, jnp.float32)
    for far in range(3):
        holder = (group & (HALF - 1)) * 4 + ((ring_place + far * step) & 3)
        pick = jnp.where(device_of == jnp.where(here, holder, -1), 1.0, 0.0).astype(jnp.bfloat16)
        found = lax.dot_general(
            parts,
            jnp.concatenate([pick] * 3, axis=0),
            (((0,), (0,)), ((), ())),
            preferred_element_type=jnp.float32,
        )
        wanted = jnp.where(here, (far & 1) * 64 + away * CAP + rank, -1)
        found = jnp.max(jnp.where(lane_of == wanted, found, -1.0), axis=0, keepdims=True)
        best = jnp.maximum(best, found)
    out_ref[...] = best


def answer(away, info, values, *before):
    return pl.pallas_call(
        functools.partial(answer_kernel, away),
        out_shape=jax.ShapeDtypeStruct((1, ROWS), jnp.float32),
        in_specs=[pl.BlockSpec(memory_space=pltpu.VMEM)] * (2 + len(before)),
        out_specs=pl.BlockSpec(memory_space=pltpu.VMEM),
        compiler_params=pltpu.CompilerParams(vmem_limit_bytes=VMEM),
        cost_estimate=cost(2 * 3 * 3 * 128 * 128 * ROWS, 4 * 128 * 128),
        name="answer",
    )(info, values, *before)


def local(embeddings, cluster_ids, member_order):
    x, y, z, core = where_am_i()
    ring_place = jnp.where(core == 0, x, y)
    ids, order = cluster_ids.reshape(1, ROWS), member_order.reshape(1, ROWS)

    box, info = prep(embeddings, ids)
    chunk1 = exchange(box.reshape(SOURCES, CAP, D), ROUTES).reshape(ROWS, D)
    handed, slab = hand(embeddings, info, ids, order)
    handed = stamp(send(handed, SIBLING), slab)
    chunk1, handed = lax.optimization_barrier((chunk1, handed))
    chunk2 = exchange(handed.reshape(SOURCES, CAP, WIDE), ROUTES).reshape(ROWS, WIDE)
    own1 = settle(chunk1)
    near1 = send(own1[0], ring(1)), send(own1[1], ring(-1))
    far1 = send(near1[0], ring(1)), send(near1[1], ring(-1))
    chunk2, own1, near1, far1 = lax.optimization_barrier((chunk2, own1, near1, far1))
    *own2, key = split(chunk2)
    near2 = send(own2[0], ring(1)), send(own2[1], ring(-1))
    far_key = send(key, ring(2))

    hold, keys = {}, {}
    for half, part in enumerate("PM"):
        hold[part, 0, 0], hold[part, 0, 1] = (own1[half], 0), (own2[half], 0)
        hold[part, 1, 0], hold[part, 2, 0] = (near1[half], 0), (far1[half], 0)
        keys[part, 0], keys[part, 2] = (key, False), (far_key, False)

    pairs, by_place = pair_lists()
    answers = []
    for stage in range(3):
        low = [pair for pair in pairs if stage_of(pair) == stage]
        if stage == 0:
            low += [((part, 0, chunk),) * 2 for part in "PM" for chunk in range(2)]
        high = list(low)
        for one, other in by_place:
            if stage_of(one) == stage:
                low.append(one)
                high.append(other)
        answers.append(
            similar(hold, keys, low, high, ring_place, answers if stage == 2 else [], ("own", "near", "far")[stage])
        )
        if stage == 0:
            near2, answers[0] = lax.optimization_barrier((near2, answers[0]))
            far2 = send(near2[0], ring(1)), send(near2[1], ring(-1))
            for half, part in enumerate("PM"):
                hold[part, 1, 1], hold[part, 2, 1] = (near2[half], 0), (far2[half], 0)
                keys[part, 1] = (near2[half], True)
    mine = exchange(answers[2].reshape(CHIPS, 1, 128), RETURNS).reshape(CHIPS, 128)
    best = answer(0, info, mine)
    return answer(1, info, send(mine, SIBLING), best).reshape(ROWS)


def solution(mesh):
    return jax.shard_map(
        local,
        mesh=mesh,
        in_specs=(P(AXES, None), P(AXES), P(AXES)),
        out_specs=P(AXES),
        check_vma=False,
    )
```

```python
import functools

import jax
import jax.numpy as jnp
import numpy as np
from jax import lax
from jax.experimental import pallas as pl
from jax.experimental.pallas import tpu as pltpu
from jax.sharding import PartitionSpec as P

AXES = ("dp", "rep")
NX, NY, NZ = 4, 4, 8
CHIPS = NX * NY * NZ
GROUPS = 64
HALF = GROUPS // 2
SOURCES = 32
CAP = 32
ROWS = 1024
D = 768
EXTRA = 16
COLUMNS = D // 128
CELL = COLUMNS * 32 + 8
HALF_ROWS = 512
ORDERS = 4096
VMEM = 24 * 1024 * 1024
FULL = 56 * 1024 * 1024


def device(x, y, z, core):
    return ((y * NZ + z) * 2 + core) * NX + x


ROUTES = [[device(x, y, z, 0) for y in range(NY) for z in range(NZ)] for x in range(NX)] + [
    [device(x, y, z, 1) for x in range(NX) for z in range(NZ)] for y in range(NY)
]
RETURNS = [
    [device(x, y, z, 0) for x in range(NX) for y in range(NY) for z in range(NZ)],
    [device(x, y, z, 1) for y in range(NY) for x in range(NX) for z in range(NZ)],
]


def ring(step):
    pairs = []
    for y in range(NY):
        for z in range(NZ):
            for x in range(NX):
                pairs.append((device(x, y, z, 0), device((x + step) % NX, y, z, 0)))
                pairs.append((device(x, y, z, 1), device(x, (y + step) % NY, z, 1)))
    return pairs


SIBLING = [(dp * NX + x, (dp ^ 1) * NX + x) for dp in range(NY * NZ * 2) for x in range(NX)]


def exchange(rows, groups):
    return lax.all_to_all(rows, AXES, split_axis=0, concat_axis=0, tiled=True, axis_index_groups=groups)


def send(rows, pairs):
    return lax.ppermute(rows, AXES, pairs)


def cost(flops, size):
    return pl.CostEstimate(flops=flops, bytes_accessed=size, transcendentals=0)


def across(one, other):
    return lax.dot_general(one, other, (((1,), (1,)), ((), ())), preferred_element_type=jnp.float32)


def key_tables(info, ids, order, core, mine):
    group, rank = info[0:1], info[1:2]
    key = (ids & 1) * ORDERS + order
    serving = group >> 5
    here = jnp.where((serving == core) if mine else (serving != core), group & (HALF - 1), -1)
    here = lax.broadcasted_iota(jnp.int32, (SOURCES, ROWS), 0) == here
    lanes = lax.broadcasted_iota(jnp.int32, (128, ROWS), 0) == rank
    lanes = jnp.where(lanes, 1.0, 0.0).astype(jnp.bfloat16)
    parts = ((key >> 7) + 1).astype(jnp.float32), (key & 127).astype(jnp.float32)
    return [across(jnp.where(here, part, 0.0).astype(jnp.bfloat16), lanes) for part in parts]


def fill_cells(out, first, count, rows, high, low):
    for column in range(COLUMNS):
        out[first : first + count, column * CAP : (column + 1) * CAP, :] = (
            rows[:, column * 128 : (column + 1) * 128].reshape(count, CAP, 128).astype(jnp.bfloat16)
        )
    sub = lax.broadcasted_iota(jnp.int32, (count, 8, 128), 1)
    high, low = high[first : first + count][:, None, :], low[first : first + count][:, None, :]
    tile = jnp.where(sub == 0, high, jnp.where(sub == 1, low, 0.0))
    out[first : first + count, COLUMNS * CAP :, :] = tile.astype(jnp.bfloat16)


def where_am_i():
    dp = lax.axis_index("dp")
    return lax.axis_index("rep"), dp >> 4, (dp >> 1) & (NZ - 1), dp & 1


def slots_of(info, core, mine):
    group, rank = info[0:1], info[1:2]
    serving = group >> 5
    slot = (group & (HALF - 1)) * CAP + rank
    return jnp.where((serving == core) if mine else (serving != core), slot, -1)


def onehot(slot, first, count):
    rows = lax.broadcasted_iota(jnp.int32, (count, ROWS), 0) + first
    return jnp.where(rows == slot, 1.0, 0.0).astype(jnp.bfloat16)


def normalize(rows):
    wide = rows.astype(jnp.float32)
    scale = 1.0 / jnp.sqrt(jnp.sum(wide * wide, axis=1, keepdims=True) + 1e-06)
    return (wide * scale).astype(jnp.bfloat16)


PIECE = 512
PIECES = ROWS // PIECE
SPAN = 256


def prep_kernel(emb_ref, ids_ref, order_ref, box_ref, info_ref, rows, out, in_sem, out_sems):
    load = pltpu.make_async_copy(emb_ref, rows, in_sem)
    load.start()
    group = ids_ref[...] >> 1
    member = lax.broadcasted_iota(jnp.int32, (GROUPS, ROWS), 0) == group
    hot = jnp.where(member, 1.0, 0.0)
    earlier = jnp.where(
        lax.broadcasted_iota(jnp.int32, (SPAN, SPAN), 0) < lax.broadcasted_iota(jnp.int32, (SPAN, SPAN), 1), 1.0, 0.0
    ).astype(jnp.bfloat16)
    before = jnp.zeros((GROUPS, 1), jnp.float32)
    ranks = []
    for n in range(ROWS // SPAN):
        here = hot[:, n * SPAN : (n + 1) * SPAN]
        count = jnp.dot(here.astype(jnp.bfloat16), earlier, preferred_element_type=jnp.float32) + before
        ranks.append(jnp.sum(here * count, axis=0, keepdims=True))
        before = before + jnp.sum(here, axis=1, keepdims=True)
    rank = jnp.concatenate(ranks, axis=1).astype(jnp.int32)
    which = lax.broadcasted_iota(jnp.int32, (8, ROWS), 0)
    info = jnp.where(which == 0, group, jnp.where(which == 1, rank, 0))
    info_ref[...] = info
    core = where_am_i()[3]
    slot = slots_of(info, core, True)
    high, low = key_tables(info, ids_ref[...], order_ref[...], core, True)
    load.wait()
    stores = []
    for n in range(PIECES):
        count = PIECE // CAP
        pick = onehot(slot, n * PIECE, PIECE)
        found = jnp.dot(pick, rows[...], preferred_element_type=jnp.float32)
        fill_cells(out, n * count, count, found, high, low)
        cells = pl.ds(n * count, count)
        stores.append(pltpu.make_async_copy(out.at[cells], box_ref.at[cells], out_sems.at[n]))
        stores[-1].start()
    for store in stores:
        store.wait()


def prep(embeddings, ids, order):
    return pl.pallas_call(
        prep_kernel,
        out_shape=(
            jax.ShapeDtypeStruct((SOURCES, CELL, 128), jnp.bfloat16),
            jax.ShapeDtypeStruct((8, ROWS), jnp.int32),
        ),
        in_specs=[pl.BlockSpec(memory_space=pl.ANY)] + [pl.BlockSpec(memory_space=pltpu.VMEM)] * 2,
        out_specs=(pl.BlockSpec(memory_space=pl.ANY), pl.BlockSpec(memory_space=pltpu.VMEM)),
        scratch_shapes=[
            pltpu.VMEM((ROWS, D), jnp.bfloat16),
            pltpu.VMEM((SOURCES, CELL, 128), jnp.bfloat16),
            pltpu.SemaphoreType.DMA,
            pltpu.SemaphoreType.DMA((PIECES,)),
        ],
        compiler_params=pltpu.CompilerParams(vmem_limit_bytes=FULL),
        cost_estimate=cost(2 * ROWS * ROWS * D, 4 * ROWS * D),
        name="prep",
    )(embeddings, ids, order)


def hand_kernel(emb_ref, info_ref, ids_ref, order_ref, box_ref):
    info, core = info_ref[...], where_am_i()[3]
    pick = onehot(slots_of(info, core, False), 0, ROWS)
    found = jnp.dot(pick, normalize(emb_ref[...]), preferred_element_type=jnp.float32)
    high, low = key_tables(info, ids_ref[...], order_ref[...], core, False)
    fill_cells(box_ref, 0, SOURCES, found, high, low)


def hand(embeddings, info, ids, order):
    return pl.pallas_call(
        hand_kernel,
        out_shape=jax.ShapeDtypeStruct((SOURCES, CELL, 128), jnp.bfloat16),
        in_specs=[pl.BlockSpec(memory_space=pltpu.VMEM)] * 4,
        out_specs=pl.BlockSpec(memory_space=pltpu.VMEM),
        compiler_params=pltpu.CompilerParams(vmem_limit_bytes=VMEM),
        cost_estimate=cost(2 * ROWS * ROWS * D, 4 * ROWS * D),
        name="hand",
    )(embeddings, info, ids, order)


def open_kernel(raw, cells_ref, p_ref, m_ref):
    count = SOURCES // 2
    sub = lax.broadcasted_iota(jnp.int32, (count, 8, 128), 1)
    slot = lax.broadcasted_iota(jnp.int32, (count, CAP, 128), 1) == lax.broadcasted_iota(
        jnp.int32, (count, CAP, 128), 2
    )
    row = lax.broadcasted_iota(jnp.int32, (EXTRA, 128), 0)
    for number, out_ref in enumerate((p_ref, m_ref)):
        first = number * count
        columns = [
            cells_ref[first : first + count, column * CAP : (column + 1) * CAP, :].reshape(HALF_ROWS, 128)
            for column in range(COLUMNS)
        ]
        if raw:
            wide = [column.astype(jnp.float32) for column in columns]
            total = sum(column * column for column in wide)
            scale = 1.0 / jnp.sqrt(jnp.sum(total, axis=1, keepdims=True) + 1e-06)
            columns = [(column * scale).astype(jnp.bfloat16) for column in wide]
        for column in range(COLUMNS):
            out_ref[:HALF_ROWS, column * 128 : (column + 1) * 128] = columns[column]
        tile = cells_ref[first : first + count, COLUMNS * CAP :, :].astype(jnp.float32)
        keys = jnp.zeros((EXTRA, HALF_ROWS), jnp.float32)
        for part in range(2):
            its = jnp.sum(jnp.where(sub == part, tile, 0.0), axis=1)
            its = jnp.where(slot, its[:, None, :], 0.0).reshape(HALF_ROWS, 128).astype(jnp.bfloat16)
            keys += across(jnp.where(row == part, 1.0, 0.0).astype(jnp.bfloat16), its)
        out_ref[HALF_ROWS:] = jnp.concatenate(
            [keys, jnp.zeros((EXTRA, D - HALF_ROWS), jnp.float32)], axis=1
        ).astype(jnp.bfloat16)


def open_cells(cells, raw):
    return pl.pallas_call(
        functools.partial(open_kernel, raw),
        out_shape=tuple([jax.ShapeDtypeStruct((HALF_ROWS + EXTRA, D), jnp.bfloat16)] * 2),
        in_specs=[pl.BlockSpec(memory_space=pltpu.VMEM)],
        out_specs=tuple([pl.BlockSpec(memory_space=pltpu.VMEM)] * 2),
        compiler_params=pltpu.CompilerParams(vmem_limit_bytes=VMEM),
        cost_estimate=cost(0, 4 * ROWS * D),
        name="settle" if raw else "split",
    )(cells)


BLOCKS = [(part, far, chunk) for far in range(3) for chunk in range(2) for part in "PM"]


def pair_lists():
    pairs = []

    def all_chunks(one, other):
        for c in range(2):
            for e in range(2):
                pairs.append((one + (c,), other + (e,)))

    for part in "PM":
        pairs.append(((part, 0, 0), (part, 0, 1)))
        all_chunks((part, 0), (part, 1))
        pairs.append(((part, 0, 1), (part, 2, 0)))
    all_chunks(("P", 0), ("M", 0))
    all_chunks(("P", 0), ("M", 1))
    all_chunks(("P", 1), ("M", 1))
    pairs.append((("P", 1, 0), ("M", 2, 0)))
    pairs.append((("P", 1, 1), ("M", 2, 0)))
    pairs.append((("P", 2, 0), ("M", 1, 1)))
    pairs.append((("P", 1, 1), ("M", 2, 1)))
    by_place = [
        ((("P", 0, 0), ("P", 2, 0)), (("M", 0, 0), ("M", 2, 0))),
        ((("M", 0, 1), ("M", 2, 1)), (("P", 0, 1), ("P", 2, 1))),
    ]
    return pairs, by_place


def stage_of(pair):
    if all(chunk == 0 and far < 2 for part, far, chunk in pair):
        return 0
    return 1 + max([far for part, far, chunk in pair if chunk == 1] + [0])


def three_parts(values):
    parts = []
    for piece in range(3):
        parts.append(values.astype(jnp.bfloat16))
        values = values - parts[-1].astype(jnp.float32)
    return parts


def similar_kernel(blocks, n_tasks, n_before, *refs):
    n_blocks = len(blocks)
    tasks_ref, refs = refs[0], refs[1:]
    arrays, refs = refs[:n_blocks], refs[n_blocks:]
    befores, refs = refs[:n_before], refs[n_before:]
    out_ref, rows, kcol, ccol, krow, crow, best_row, best_col, s0, s1, sems = refs

    copies = [pltpu.make_async_copy(array, rows.at[slot], sems.at[slot]) for slot, array in enumerate(arrays)]
    for copy in copies:
        copy.start()
    for slot in range(n_blocks):
        best_row[slot] = jnp.full((HALF_ROWS, 128), -1.0, jnp.float32)
        best_col[slot] = jnp.full((8, HALF_ROWS), -1.0, jnp.float32)

    def cluster(key):
        return jnp.where(key >= ORDERS + 128, 2.0, jnp.where(key > 0, 1.0, 0.0))

    for slot, copy in enumerate(copies):
        copy.wait()
        parts = rows[slot, HALF_ROWS:, :HALF_ROWS].astype(jnp.float32)
        key = 128.0 * parts[0:1] + parts[1:2]
        krow[slot] = jnp.broadcast_to(key, (8, HALF_ROWS))
        crow[slot] = cluster(krow[slot])
        key = jnp.transpose(jnp.broadcast_to(key, (128, HALF_ROWS)))
        kcol[slot] = key
        ccol[slot] = cluster(key)

    def multiply(task, s):
        a, b = tasks_ref[3 * task], tasks_ref[3 * task + 1]
        s[...] = across(rows[a, :HALF_ROWS], rows[b, :HALF_ROWS])

    step = 16

    def reduce(task, s):
        a, b, sink = tasks_ref[3 * task], tasks_ref[3 * task + 1], tasks_ref[3 * task + 2]
        kb, cb = krow[b], crow[b]
        for row in range(0, HALF_ROWS, step):
            ka = kcol[a, row : row + step].reshape(step // 8, 8, 128)
            ca = ccol[a, row : row + step].reshape(step // 8, 8, 128)
            best = best_row[a, row : row + step]
            for at in range(0, HALF_ROWS, 128):
                found = s[row : row + step, at : at + 128].reshape(step // 8, 8, 128)
                same = jnp.where(ca == cb[None, :, at : at + 128], found, -1.0)
                later = kb[None, :, at : at + 128] < ka
                best = jnp.maximum(best, jnp.where(later, same, -1.0).reshape(step, 128))
                other = jnp.max(jnp.where(later, -1.0, same), axis=0)
                best_col[sink, :, at : at + 128] = jnp.maximum(best_col[sink, :, at : at + 128], other)
            best_row[a, row : row + step] = best

    def two(turn, carry):
        multiply(2 * turn + 1, s1)
        reduce(2 * turn, s0)
        multiply(2 * turn + 2, s0)
        reduce(2 * turn + 1, s1)
        return carry

    turns = (n_tasks - 1) // 2
    multiply(0, s0)
    if turns:
        lax.fori_loop(0, turns, two, 0)
    if n_tasks % 2 == 0:
        multiply(n_tasks - 1, s1)
    reduce(2 * turns, s0)
    if n_tasks % 2 == 0:
        reduce(n_tasks - 1, s1)

    empty = jnp.full((CAP, HALF_ROWS), -1.0, jnp.float32)
    diagonal = lax.broadcasted_iota(jnp.int32, (CAP, HALF_ROWS), 0) == (
        lax.broadcasted_iota(jnp.int32, (CAP, HALF_ROWS), 1) & (CAP - 1)
    )
    values = {}
    for number, part in enumerate("PM"):
        for level in range(2):
            tiles = [empty] * 4
            for slot, (its, far, chunk) in enumerate(blocks):
                if its == part and far // 2 == level:
                    by_row = jnp.max(jnp.transpose(best_row[slot]), axis=0, keepdims=True)
                    by_col = jnp.max(best_col[slot], axis=0, keepdims=True)
                    tiles[2 * (far & 1) + chunk] = jnp.where(diagonal, jnp.maximum(by_row, by_col), -1.0)
            if all(tile is empty for tile in tiles):
                value = jnp.full((HALF_ROWS // CAP, 128), -1.0, jnp.float32)
            else:
                value = jnp.transpose(jnp.concatenate(tiles, axis=0)).reshape(HALF_ROWS // CAP, CAP, 128)
                value = jnp.max(value, axis=1)
            at = pl.ds(level * SOURCES + number * (SOURCES // 2), SOURCES // 2)
            for before in befores:
                value = jnp.maximum(value, before[at, :])
            values[level, number] = value
    values = jnp.concatenate([values[level, number] for level in range(2) for number in range(2)], axis=0)
    if not befores:
        out_ref[...] = values
        return
    x, y, z, core = where_am_i()
    here = jnp.where(core == 0, x, y)
    row = lax.broadcasted_iota(jnp.int32, (CHIPS, 2 * SOURCES), 0)
    column = lax.broadcasted_iota(jnp.int32, (CHIPS, 2 * SOURCES), 1)
    source = row & (SOURCES - 1)
    far = (here - (row >> 5)) * jnp.where(source < SOURCES // 2, 1, -1) & 3
    wanted = (column == source) & (far < 2) | (column == source + SOURCES) & (far == 2)
    pick = jnp.where(wanted, 1.0, 0.0).astype(jnp.bfloat16)
    out_ref[...] = jnp.dot(
        jnp.concatenate([pick] * 3, axis=1),
        jnp.concatenate(three_parts(values), axis=0),
        preferred_element_type=jnp.float32,
    )


def similar(hold, low, high, ring_place, befores, name):
    blocks = [block for block in BLOCKS if any(block in pair for pair in low + high)]
    place = {block: number for number, block in enumerate(blocks)}
    spare = n = len(blocks)

    def table(pairs):
        return np.array(
            [(place[a], place[b], spare if a == b else place[b]) for a, b in pairs], np.int32
        ).reshape(-1)

    tasks = jnp.asarray(table(low))
    if low != high:
        tasks = jnp.where(ring_place < 2, tasks, jnp.asarray(table(high)))
    return pl.pallas_call(
        functools.partial(similar_kernel, blocks, len(low), len(befores)),
        out_shape=jax.ShapeDtypeStruct((CHIPS if befores else 2 * SOURCES, 128), jnp.float32),
        in_specs=[pl.BlockSpec(memory_space=pltpu.SMEM)]
        + [pl.BlockSpec(memory_space=pl.ANY)] * n
        + [pl.BlockSpec(memory_space=pltpu.VMEM)] * len(befores),
        out_specs=pl.BlockSpec(memory_space=pltpu.VMEM),
        scratch_shapes=[
            pltpu.VMEM((n, HALF_ROWS + EXTRA, D), jnp.bfloat16),
            pltpu.VMEM((n, HALF_ROWS, 128), jnp.float32),
            pltpu.VMEM((n, HALF_ROWS, 128), jnp.float32),
            pltpu.VMEM((n, 8, HALF_ROWS), jnp.float32),
            pltpu.VMEM((n, 8, HALF_ROWS), jnp.float32),
            pltpu.VMEM((n, HALF_ROWS, 128), jnp.float32),
            pltpu.VMEM((n + 1, 8, HALF_ROWS), jnp.float32),
            pltpu.VMEM((HALF_ROWS, HALF_ROWS), jnp.float32),
            pltpu.VMEM((HALF_ROWS, HALF_ROWS), jnp.float32),
            pltpu.SemaphoreType.DMA((n,)),
        ],
        compiler_params=pltpu.CompilerParams(vmem_limit_bytes=32 * 1024 * 1024),
        cost_estimate=cost(2 * D * HALF_ROWS * HALF_ROWS * len(low), 2 * n * HALF_ROWS * D),
        name=name,
    )(tasks, *[hold[block] for block in blocks], *befores)


def answer_kernel(away, info_ref, values_ref, *refs):
    info, out_ref = info_ref[...], refs[-1]
    group, rank = info[0:1], info[1:2]
    x, y, z, core = where_am_i()
    serving = (core + away) & 1
    here = (group >> 5) == serving
    ring_place, source = jnp.where(serving == 0, x, y), jnp.where(serving == 0, y, x)
    step = jnp.where(source < 2, 1, -1)
    place_of = lax.broadcasted_iota(jnp.int32, (SOURCES, ROWS), 0)
    pick = jnp.where(place_of == jnp.where(here, group & (HALF - 1), -1), 1.0, 0.0).astype(jnp.bfloat16)
    pick = jnp.concatenate([pick] * 3, axis=0)
    lane_of = lax.broadcasted_iota(jnp.int32, (128, ROWS), 0)
    best = refs[0][...] if away else jnp.full((1, ROWS), -1.0, jnp.float32)
    for far in range(3):
        holder = pl.multiple_of(((ring_place + far * step) & 3) * SOURCES, SOURCES)
        parts = jnp.concatenate(three_parts(values_ref[pl.ds(holder, SOURCES), :]), axis=0)
        found = lax.dot_general(parts, pick, (((0,), (0,)), ((), ())), preferred_element_type=jnp.float32)
        wanted = jnp.where(here, (far & 1) * 64 + away * CAP + rank, -1)
        found = jnp.max(jnp.where(lane_of == wanted, found, -1.0), axis=0, keepdims=True)
        best = jnp.maximum(best, found)
    out_ref[...] = best


def answer(away, info, values, *before):
    return pl.pallas_call(
        functools.partial(answer_kernel, away),
        out_shape=jax.ShapeDtypeStruct((1, ROWS), jnp.float32),
        in_specs=[pl.BlockSpec(memory_space=pltpu.VMEM)] * (2 + len(before)),
        out_specs=pl.BlockSpec(memory_space=pltpu.VMEM),
        compiler_params=pltpu.CompilerParams(vmem_limit_bytes=VMEM),
        cost_estimate=cost(2 * 3 * 3 * 128 * 128 * ROWS, 4 * 128 * 128),
        name="answer",
    )(info, values, *before)


def local(embeddings, cluster_ids, member_order):
    x, y, z, core = where_am_i()
    ring_place = jnp.where(core == 0, x, y)
    ids, order = cluster_ids.reshape(1, ROWS), member_order.reshape(1, ROWS)

    box, info = prep(embeddings, ids, order)
    chunk1 = exchange(box, ROUTES)
    handed = send(hand(embeddings, info, ids, order), SIBLING)
    chunk1, handed = lax.optimization_barrier((chunk1, handed))
    chunk2 = exchange(handed, ROUTES)

    hold = {}

    def ring_blocks(far, chunk, blocks):
        hold["P", far, chunk], hold["M", far, chunk] = blocks
        return blocks

    def onward(blocks):
        return send(blocks[0], ring(1)), send(blocks[1], ring(-1))

    pairs, by_place = pair_lists()
    pairs += [((part, 0, chunk),) * 2 for part in "PM" for chunk in range(2)]

    def run(stage, name, befores=()):
        low = [pair for pair in pairs if stage_of(pair) == stage]
        high = list(low)
        for one, other in by_place:
            if stage_of(one) == stage:
                low.append(one)
                high.append(other)
        return similar(hold, low, high, ring_place, befores, name)

    own1 = ring_blocks(0, 0, open_cells(chunk1, True))
    near1 = ring_blocks(1, 0, onward(own1))
    far1 = onward(near1)
    first = run(0, "first")
    chunk2, own1, near1, far1, first = lax.optimization_barrier((chunk2, own1, near1, far1, first))
    for far, blocks in enumerate((own1, near1, far1)):
        ring_blocks(far, 0, blocks)
    own2 = ring_blocks(0, 1, open_cells(chunk2, False))
    near2 = onward(own2)
    own = run(1, "own")
    near2, own = lax.optimization_barrier((near2, own))
    ring_blocks(1, 1, near2)
    ring_blocks(2, 1, onward(near2))
    near = run(2, "near")
    last = run(3, "far", (first, own, near))
    mine = exchange(last.reshape(CHIPS, 1, 128), RETURNS).reshape(CHIPS, 128)
    best = answer(0, info, mine)
    return answer(1, info, send(mine, SIBLING), best).reshape(ROWS)


def solution(mesh):
    return jax.shard_map(
        local,
        mesh=mesh,
        in_specs=(P(AXES, None), P(AXES), P(AXES)),
        out_specs=P(AXES),
        check_vma=False,
    )
```

```python
import functools

import jax
import jax.numpy as jnp
import numpy as np
from jax import lax
from jax.experimental import pallas as pl
from jax.experimental.pallas import tpu as pltpu
from jax.sharding import PartitionSpec as P

AXES = ("dp", "rep")
NX, NY, NZ = 4, 4, 8
CHIPS = NX * NY * NZ
GROUPS = 64
HALF = GROUPS // 2
SOURCES = 32
CAP = 32
ROWS = 1024
D = 768
EXTRA = 16
COLUMNS = D // 128
CELL = COLUMNS * 32 + 8
HALF_ROWS = 512
ORDERS = 4096
VMEM = 24 * 1024 * 1024
FULL = 58 * 1024 * 1024
PAIRS = 32 * 1024 * 1024
OWN = 121 * 512 * 1024
NEAR = 59 * 1024 * 1024


def device(x, y, z, core):
    return ((y * NZ + z) * 2 + core) * NX + x


ROUTES = [[device(x, y, z, 0) for y in range(NY) for z in range(NZ)] for x in range(NX)] + [
    [device(x, y, z, 1) for x in range(NX) for z in range(NZ)] for y in range(NY)
]
RETURNS = [
    [device(x, y, z, 0) for x in range(NX) for y in range(NY) for z in range(NZ)],
    [device(x, y, z, 1) for y in range(NY) for x in range(NX) for z in range(NZ)],
]


def ring(step):
    pairs = []
    for y in range(NY):
        for z in range(NZ):
            for x in range(NX):
                pairs.append((device(x, y, z, 0), device((x + step) % NX, y, z, 0)))
                pairs.append((device(x, y, z, 1), device(x, (y + step) % NY, z, 1)))
    return pairs


SIBLING = [(dp * NX + x, (dp ^ 1) * NX + x) for dp in range(NY * NZ * 2) for x in range(NX)]


def exchange(rows, groups):
    return lax.all_to_all(rows, AXES, split_axis=0, concat_axis=0, tiled=True, axis_index_groups=groups)


def send(rows, pairs):
    return lax.ppermute(rows, AXES, pairs)


def cost(flops, size):
    return pl.CostEstimate(flops=flops, bytes_accessed=size, transcendentals=0)


def across(one, other):
    return lax.dot_general(one, other, (((1,), (1,)), ((), ())), preferred_element_type=jnp.float32)


def key_tables(info, ids, order, core, mine):
    group, rank = info[0:1], info[1:2]
    key = (ids & 1) * ORDERS + order
    serving = group >> 5
    here = jnp.where((serving == core) if mine else (serving != core), group & (HALF - 1), -1)
    here = lax.broadcasted_iota(jnp.int32, (SOURCES, ROWS), 0) == here
    lanes = lax.broadcasted_iota(jnp.int32, (128, ROWS), 0) == rank
    lanes = jnp.where(lanes, 1.0, 0.0).astype(jnp.bfloat16)
    parts = ((key >> 7) + 1).astype(jnp.float32), (key & 127).astype(jnp.float32)
    return [across(jnp.where(here, part, 0.0).astype(jnp.bfloat16), lanes) for part in parts]


def fill_cells(out, first, count, rows, high, low):
    for column in range(COLUMNS):
        out[first : first + count, column * CAP : (column + 1) * CAP, :] = (
            rows[:, column * 128 : (column + 1) * 128].reshape(count, CAP, 128).astype(jnp.bfloat16)
        )
    sub = lax.broadcasted_iota(jnp.int32, (count, 8, 128), 1)
    high, low = high[first : first + count][:, None, :], low[first : first + count][:, None, :]
    tile = jnp.where(sub == 0, high, jnp.where(sub == 1, low, 0.0))
    out[first : first + count, COLUMNS * CAP :, :] = tile.astype(jnp.bfloat16)


def where_am_i():
    dp = lax.axis_index("dp")
    return lax.axis_index("rep"), dp >> 4, (dp >> 1) & (NZ - 1), dp & 1


def slots_of(info, core, mine):
    group, rank = info[0:1], info[1:2]
    serving = group >> 5
    slot = (group & (HALF - 1)) * CAP + rank
    return jnp.where((serving == core) if mine else (serving != core), slot, -1)


def onehot(slot, first, count):
    rows = lax.broadcasted_iota(jnp.int32, (count, ROWS), 0) + first
    return jnp.where(rows == slot, 1.0, 0.0).astype(jnp.bfloat16)


def normalize(rows):
    wide = rows.astype(jnp.float32)
    scale = 1.0 / jnp.sqrt(jnp.sum(wide * wide, axis=1, keepdims=True) + 1e-06)
    return (wide * scale).astype(jnp.bfloat16)


PIECE = 512
PIECES = ROWS // PIECE
SPAN = 256


def prep_kernel(emb_ref, ids_ref, order_ref, box_ref, info_ref, rows, out, in_sem, out_sems):
    load = pltpu.make_async_copy(emb_ref, rows, in_sem)
    load.start()
    group = ids_ref[...] >> 1
    member = lax.broadcasted_iota(jnp.int32, (GROUPS, ROWS), 0) == group
    hot = jnp.where(member, 1.0, 0.0)
    earlier = jnp.where(
        lax.broadcasted_iota(jnp.int32, (SPAN, SPAN), 0) < lax.broadcasted_iota(jnp.int32, (SPAN, SPAN), 1), 1.0, 0.0
    ).astype(jnp.bfloat16)
    before = jnp.zeros((GROUPS, 1), jnp.float32)
    ranks = []
    for n in range(ROWS // SPAN):
        here = hot[:, n * SPAN : (n + 1) * SPAN]
        count = jnp.dot(here.astype(jnp.bfloat16), earlier, preferred_element_type=jnp.float32) + before
        ranks.append(jnp.sum(here * count, axis=0, keepdims=True))
        before = before + jnp.sum(here, axis=1, keepdims=True)
    rank = jnp.concatenate(ranks, axis=1).astype(jnp.int32)
    which = lax.broadcasted_iota(jnp.int32, (8, ROWS), 0)
    info = jnp.where(which == 0, group, jnp.where(which == 1, rank, 0))
    info_ref[...] = info
    core = where_am_i()[3]
    slot = slots_of(info, core, True)
    high, low = key_tables(info, ids_ref[...], order_ref[...], core, True)
    load.wait()
    stores = []
    for n in range(PIECES):
        count = PIECE // CAP
        pick = onehot(slot, n * PIECE, PIECE)
        found = jnp.dot(pick, rows[...], preferred_element_type=jnp.float32)
        fill_cells(out, n * count, count, found, high, low)
        cells = pl.ds(n * count, count)
        stores.append(pltpu.make_async_copy(out.at[cells], box_ref.at[cells], out_sems.at[n]))
        stores[-1].start()
    for store in stores:
        store.wait()


def prep(embeddings, ids, order):
    return pl.pallas_call(
        prep_kernel,
        out_shape=(
            jax.ShapeDtypeStruct((SOURCES, CELL, 128), jnp.bfloat16),
            jax.ShapeDtypeStruct((8, ROWS), jnp.int32),
        ),
        in_specs=[pl.BlockSpec(memory_space=pl.ANY)] + [pl.BlockSpec(memory_space=pltpu.VMEM)] * 2,
        out_specs=(pl.BlockSpec(memory_space=pl.ANY), pl.BlockSpec(memory_space=pltpu.VMEM)),
        scratch_shapes=[
            pltpu.VMEM((ROWS, D), jnp.bfloat16),
            pltpu.VMEM((SOURCES, CELL, 128), jnp.bfloat16),
            pltpu.SemaphoreType.DMA,
            pltpu.SemaphoreType.DMA((PIECES,)),
        ],
        compiler_params=pltpu.CompilerParams(vmem_limit_bytes=FULL),
        cost_estimate=cost(2 * ROWS * ROWS * D, 4 * ROWS * D),
        name="prep",
    )(embeddings, ids, order)


def hand_kernel(emb_ref, info_ref, ids_ref, order_ref, box_ref):
    info, core = info_ref[...], where_am_i()[3]
    pick = onehot(slots_of(info, core, False), 0, ROWS)
    found = jnp.dot(pick, normalize(emb_ref[...]), preferred_element_type=jnp.float32)
    high, low = key_tables(info, ids_ref[...], order_ref[...], core, False)
    fill_cells(box_ref, 0, SOURCES, found, high, low)


def hand(embeddings, info, ids, order):
    return pl.pallas_call(
        hand_kernel,
        out_shape=jax.ShapeDtypeStruct((SOURCES, CELL, 128), jnp.bfloat16),
        in_specs=[pl.BlockSpec(memory_space=pltpu.VMEM)] * 4,
        out_specs=pl.BlockSpec(memory_space=pltpu.VMEM),
        compiler_params=pltpu.CompilerParams(vmem_limit_bytes=VMEM),
        cost_estimate=cost(2 * ROWS * ROWS * D, 4 * ROWS * D),
        name="hand",
    )(embeddings, info, ids, order)


def open_kernel(raw, cells_ref, p_ref, m_ref):
    count = SOURCES // 2
    sub = lax.broadcasted_iota(jnp.int32, (count, 8, 128), 1)
    slot = lax.broadcasted_iota(jnp.int32, (count, CAP, 128), 1) == lax.broadcasted_iota(
        jnp.int32, (count, CAP, 128), 2
    )
    row = lax.broadcasted_iota(jnp.int32, (EXTRA, 128), 0)
    for number, out_ref in enumerate((p_ref, m_ref)):
        first = number * count
        columns = [
            cells_ref[first : first + count, column * CAP : (column + 1) * CAP, :].reshape(HALF_ROWS, 128)
            for column in range(COLUMNS)
        ]
        if raw:
            wide = [column.astype(jnp.float32) for column in columns]
            total = sum(column * column for column in wide)
            scale = 1.0 / jnp.sqrt(jnp.sum(total, axis=1, keepdims=True) + 1e-06)
            columns = [(column * scale).astype(jnp.bfloat16) for column in wide]
        for column in range(COLUMNS):
            out_ref[:HALF_ROWS, column * 128 : (column + 1) * 128] = columns[column]
        tile = cells_ref[first : first + count, COLUMNS * CAP :, :].astype(jnp.float32)
        keys = jnp.zeros((EXTRA, HALF_ROWS), jnp.float32)
        for part in range(2):
            its = jnp.sum(jnp.where(sub == part, tile, 0.0), axis=1)
            its = jnp.where(slot, its[:, None, :], 0.0).reshape(HALF_ROWS, 128).astype(jnp.bfloat16)
            keys += across(jnp.where(row == part, 1.0, 0.0).astype(jnp.bfloat16), its)
        out_ref[HALF_ROWS:] = jnp.concatenate(
            [keys, jnp.zeros((EXTRA, D - HALF_ROWS), jnp.float32)], axis=1
        ).astype(jnp.bfloat16)


def open_cells(cells, raw):
    return pl.pallas_call(
        functools.partial(open_kernel, raw),
        out_shape=tuple([jax.ShapeDtypeStruct((HALF_ROWS + EXTRA, D), jnp.bfloat16)] * 2),
        in_specs=[pl.BlockSpec(memory_space=pltpu.VMEM)],
        out_specs=tuple([pl.BlockSpec(memory_space=pltpu.VMEM)] * 2),
        compiler_params=pltpu.CompilerParams(vmem_limit_bytes=VMEM),
        cost_estimate=cost(0, 4 * ROWS * D),
        name="settle" if raw else "split",
    )(cells)


BLOCKS = [(part, far, chunk) for far in range(3) for chunk in range(2) for part in "PM"]


def pair_lists():
    pairs = []

    def all_chunks(one, other):
        for c in range(2):
            for e in range(2):
                pairs.append((one + (c,), other + (e,)))

    for part in "PM":
        pairs.append(((part, 0, 0), (part, 0, 1)))
        all_chunks((part, 0), (part, 1))
        pairs.append(((part, 0, 1), (part, 2, 0)))
    all_chunks(("P", 0), ("M", 0))
    all_chunks(("P", 0), ("M", 1))
    all_chunks(("P", 1), ("M", 1))
    pairs.append((("P", 1, 0), ("M", 2, 0)))
    pairs.append((("P", 1, 1), ("M", 2, 0)))
    pairs.append((("P", 2, 0), ("M", 1, 1)))
    pairs.append((("P", 1, 1), ("M", 2, 1)))
    by_place = [
        ((("P", 0, 0), ("P", 2, 0)), (("M", 0, 0), ("M", 2, 0))),
        ((("M", 0, 1), ("M", 2, 1)), (("P", 0, 1), ("P", 2, 1))),
    ]
    return pairs, by_place


def stage_of(pair):
    if all(chunk == 0 and far < 2 for part, far, chunk in pair):
        return 0
    return 1 + max([far for part, far, chunk in pair if chunk == 1] + [0])


def three_parts(values):
    parts = []
    for piece in range(3):
        parts.append(values.astype(jnp.bfloat16))
        values = values - parts[-1].astype(jnp.float32)
    return parts


def similar_kernel(blocks, early, n_tasks, n_before, *refs):
    n_blocks = len(blocks)
    tasks_ref, refs = refs[0], refs[1:]
    arrays, refs = refs[:n_blocks], refs[n_blocks:]
    befores, refs = refs[:n_before], refs[n_before:]
    out_ref, rows, kcol, ccol, krow, crow, best_row, best_col, s0, s1, sems = refs

    copies = [pltpu.make_async_copy(array, rows.at[slot], sems.at[slot]) for slot, array in enumerate(arrays)]
    for copy in copies:
        copy.start()
    for slot in range(n_blocks):
        best_row[slot] = jnp.full((HALF_ROWS, 128), -1.0, jnp.float32)
        best_col[slot] = jnp.full((8, HALF_ROWS), -1.0, jnp.float32)

    def cluster(key):
        return jnp.where(key >= ORDERS + 128, 2.0, jnp.where(key > 0, 1.0, 0.0))

    def arrive(slots):
        for slot in slots:
            copies[slot].wait()
        for slot in slots:
            parts = rows[slot, HALF_ROWS:, :HALF_ROWS].astype(jnp.float32)
            key = 128.0 * parts[0:1] + parts[1:2]
            krow[slot] = jnp.broadcast_to(key, (8, HALF_ROWS))
            crow[slot] = cluster(krow[slot])
            key = jnp.transpose(jnp.broadcast_to(key, (128, HALF_ROWS)))
            kcol[slot] = key
            ccol[slot] = cluster(key)

    def multiply(task, s):
        a, b = tasks_ref[3 * task], tasks_ref[3 * task + 1]
        s[...] = across(rows[a, :HALF_ROWS], rows[b, :HALF_ROWS])

    step = 16

    def reduce(task, s):
        a, b, sink = tasks_ref[3 * task], tasks_ref[3 * task + 1], tasks_ref[3 * task + 2]
        kb, cb = krow[b], crow[b]
        for row in range(0, HALF_ROWS, step):
            ka = kcol[a, row : row + step].reshape(step // 8, 8, 128)
            ca = ccol[a, row : row + step].reshape(step // 8, 8, 128)
            best = best_row[a, row : row + step]
            for at in range(0, HALF_ROWS, 128):
                found = s[row : row + step, at : at + 128].reshape(step // 8, 8, 128)
                same = jnp.where(ca == cb[None, :, at : at + 128], found, -1.0)
                later = kb[None, :, at : at + 128] < ka
                best = jnp.maximum(best, jnp.where(later, same, -1.0).reshape(step, 128))
                other = jnp.max(jnp.where(later, -1.0, same), axis=0)
                best_col[sink, :, at : at + 128] = jnp.maximum(best_col[sink, :, at : at + 128], other)
            best_row[a, row : row + step] = best

    def two(turn, carry):
        multiply(2 * turn + 1, s1)
        reduce(2 * turn, s0)
        multiply(2 * turn + 2, s0)
        reduce(2 * turn + 1, s1)
        return carry

    turns = (n_tasks - 1) // 2
    start, early = early
    arrive(range(early))
    multiply(0, s0)
    if start:
        lax.fori_loop(0, start, two, 0)
    arrive(range(early, n_blocks))
    if turns > start:
        lax.fori_loop(start, turns, two, 0)
    if n_tasks % 2 == 0:
        multiply(n_tasks - 1, s1)
    reduce(2 * turns, s0)
    if n_tasks % 2 == 0:
        reduce(n_tasks - 1, s1)

    empty = jnp.full((CAP, HALF_ROWS), -1.0, jnp.float32)
    diagonal = lax.broadcasted_iota(jnp.int32, (CAP, HALF_ROWS), 0) == (
        lax.broadcasted_iota(jnp.int32, (CAP, HALF_ROWS), 1) & (CAP - 1)
    )
    values = {}
    for number, part in enumerate("PM"):
        for level in range(2):
            tiles = [empty] * 4
            for slot, (its, far, chunk) in enumerate(blocks):
                if its == part and far // 2 == level:
                    by_row = jnp.max(jnp.transpose(best_row[slot]), axis=0, keepdims=True)
                    by_col = jnp.max(best_col[slot], axis=0, keepdims=True)
                    tiles[2 * (far & 1) + chunk] = jnp.where(diagonal, jnp.maximum(by_row, by_col), -1.0)
            if all(tile is empty for tile in tiles):
                value = jnp.full((HALF_ROWS // CAP, 128), -1.0, jnp.float32)
            else:
                value = jnp.transpose(jnp.concatenate(tiles, axis=0)).reshape(HALF_ROWS // CAP, CAP, 128)
                value = jnp.max(value, axis=1)
            at = pl.ds(level * SOURCES + number * (SOURCES // 2), SOURCES // 2)
            for before in befores:
                value = jnp.maximum(value, before[at, :])
            values[level, number] = value
    values = jnp.concatenate([values[level, number] for level in range(2) for number in range(2)], axis=0)
    if not befores:
        out_ref[...] = values
        return
    x, y, z, core = where_am_i()
    here = jnp.where(core == 0, x, y)
    row = lax.broadcasted_iota(jnp.int32, (CHIPS, 2 * SOURCES), 0)
    column = lax.broadcasted_iota(jnp.int32, (CHIPS, 2 * SOURCES), 1)
    source = row & (SOURCES - 1)
    far = (here - (row >> 5)) * jnp.where(source < SOURCES // 2, 1, -1) & 3
    wanted = (column == source) & (far < 2) | (column == source + SOURCES) & (far == 2)
    pick = jnp.where(wanted, 1.0, 0.0).astype(jnp.bfloat16)
    out_ref[...] = jnp.dot(
        jnp.concatenate([pick] * 3, axis=1),
        jnp.concatenate(three_parts(values), axis=0),
        preferred_element_type=jnp.float32,
    )


def similar(hold, low, high, ring_place, befores, name, limit, start):
    first_use = {}
    for number, pairs in enumerate(zip(low, high)):
        for pair in pairs:
            for block in pair:
                first_use.setdefault(block, number)
    blocks = sorted(first_use, key=lambda block: (first_use[block], BLOCKS.index(block)))
    early = start, sum(first_use[block] <= 2 * start for block in blocks)
    place = {block: number for number, block in enumerate(blocks)}
    spare = n = len(blocks)

    def table(pairs):
        return np.array(
            [(place[a], place[b], spare if a == b else place[b]) for a, b in pairs], np.int32
        ).reshape(-1)

    tasks = jnp.asarray(table(low))
    if low != high:
        tasks = jnp.where(ring_place < 2, tasks, jnp.asarray(table(high)))
    return pl.pallas_call(
        functools.partial(similar_kernel, blocks, early, len(low), len(befores)),
        out_shape=jax.ShapeDtypeStruct((CHIPS if befores else 2 * SOURCES, 128), jnp.float32),
        in_specs=[pl.BlockSpec(memory_space=pltpu.SMEM)]
        + [pl.BlockSpec(memory_space=pl.ANY)] * n
        + [pl.BlockSpec(memory_space=pltpu.VMEM)] * len(befores),
        out_specs=pl.BlockSpec(memory_space=pltpu.VMEM),
        scratch_shapes=[
            pltpu.VMEM((n, HALF_ROWS + EXTRA, D), jnp.bfloat16),
            pltpu.VMEM((n, HALF_ROWS, 128), jnp.float32),
            pltpu.VMEM((n, HALF_ROWS, 128), jnp.float32),
            pltpu.VMEM((n, 8, HALF_ROWS), jnp.float32),
            pltpu.VMEM((n, 8, HALF_ROWS), jnp.float32),
            pltpu.VMEM((n, HALF_ROWS, 128), jnp.float32),
            pltpu.VMEM((n + 1, 8, HALF_ROWS), jnp.float32),
            pltpu.VMEM((HALF_ROWS, HALF_ROWS), jnp.float32),
            pltpu.VMEM((HALF_ROWS, HALF_ROWS), jnp.float32),
            pltpu.SemaphoreType.DMA((n,)),
        ],
        compiler_params=pltpu.CompilerParams(vmem_limit_bytes=limit),
        cost_estimate=cost(2 * D * HALF_ROWS * HALF_ROWS * len(low), 2 * n * HALF_ROWS * D),
        name=name,
    )(tasks, *[hold[block] for block in blocks], *befores)


def answer_kernel(away, info_ref, values_ref, *refs):
    info, out_ref = info_ref[...], refs[-1]
    group, rank = info[0:1], info[1:2]
    x, y, z, core = where_am_i()
    serving = (core + away) & 1
    here = (group >> 5) == serving
    ring_place, source = jnp.where(serving == 0, x, y), jnp.where(serving == 0, y, x)
    step = jnp.where(source < 2, 1, -1)
    place_of = lax.broadcasted_iota(jnp.int32, (SOURCES, ROWS), 0)
    pick = jnp.where(place_of == jnp.where(here, group & (HALF - 1), -1), 1.0, 0.0).astype(jnp.bfloat16)
    pick = jnp.concatenate([pick] * 3, axis=0)
    lane_of = lax.broadcasted_iota(jnp.int32, (128, ROWS), 0)
    best = refs[0][...] if away else jnp.full((1, ROWS), -1.0, jnp.float32)
    for far in range(3):
        holder = pl.multiple_of(((ring_place + far * step) & 3) * SOURCES, SOURCES)
        parts = jnp.concatenate(three_parts(values_ref[pl.ds(holder, SOURCES), :]), axis=0)
        found = lax.dot_general(parts, pick, (((0,), (0,)), ((), ())), preferred_element_type=jnp.float32)
        wanted = jnp.where(here, (far & 1) * 64 + away * CAP + rank, -1)
        found = jnp.max(jnp.where(lane_of == wanted, found, -1.0), axis=0, keepdims=True)
        best = jnp.maximum(best, found)
    out_ref[...] = best


def answer(away, info, values, *before):
    return pl.pallas_call(
        functools.partial(answer_kernel, away),
        out_shape=jax.ShapeDtypeStruct((1, ROWS), jnp.float32),
        in_specs=[pl.BlockSpec(memory_space=pltpu.VMEM)] * (2 + len(before)),
        out_specs=pl.BlockSpec(memory_space=pltpu.VMEM),
        compiler_params=pltpu.CompilerParams(vmem_limit_bytes=VMEM),
        cost_estimate=cost(2 * 3 * 3 * 128 * 128 * ROWS, 4 * 128 * 128),
        name="answer",
    )(info, values, *before)


def local(embeddings, cluster_ids, member_order):
    x, y, z, core = where_am_i()
    ring_place = jnp.where(core == 0, x, y)
    ids, order = cluster_ids.reshape(1, ROWS), member_order.reshape(1, ROWS)

    box, info = prep(embeddings, ids, order)
    chunk1 = exchange(box, ROUTES)
    handed = send(hand(embeddings, info, ids, order), SIBLING)
    chunk1, handed = lax.optimization_barrier((chunk1, handed))
    chunk2 = exchange(handed, ROUTES)

    hold = {}

    def ring_blocks(far, chunk, blocks):
        hold["P", far, chunk], hold["M", far, chunk] = blocks
        return blocks

    def onward(blocks):
        return send(blocks[0], ring(1)), send(blocks[1], ring(-1))

    pairs, by_place = pair_lists()
    pairs += [((part, 0, chunk),) * 2 for part in "PM" for chunk in range(2)]

    def run(stage, name, befores=()):
        low = [pair for pair in pairs if stage_of(pair) == stage]
        low.sort(key=lambda pair: sum(chunk == 0 for part, far, chunk in pair))
        high = list(low)
        for one, other in by_place:
            if stage_of(one) == stage:
                low.append(one)
                high.append(other)
        limit, start = ((PAIRS, 0), (OWN, 1), (NEAR, 1), (PAIRS, 0))[stage]
        return similar(hold, low, high, ring_place, befores, name, limit, start)

    own1 = ring_blocks(0, 0, open_cells(chunk1, True))
    near1 = ring_blocks(1, 0, onward(own1))
    far1 = onward(near1)
    first = run(0, "first")
    chunk2, own1, near1, far1, first = lax.optimization_barrier((chunk2, own1, near1, far1, first))
    for far, blocks in enumerate((own1, near1, far1)):
        ring_blocks(far, 0, blocks)
    own2 = ring_blocks(0, 1, open_cells(chunk2, False))
    near2 = onward(own2)
    own = run(1, "own")
    near2, own = lax.optimization_barrier((near2, own))
    ring_blocks(1, 1, near2)
    ring_blocks(2, 1, onward(near2))
    near = run(2, "near")
    last = run(3, "far", (first, own, near))
    mine = exchange(last.reshape(CHIPS, 1, 128), RETURNS).reshape(CHIPS, 128)
    best = answer(0, info, mine)
    return answer(1, info, send(mine, SIBLING), best).reshape(ROWS)


def solution(mesh):
    return jax.shard_map(
        local,
        mesh=mesh,
        in_specs=(P(AXES, None), P(AXES), P(AXES)),
        out_specs=P(AXES),
        check_vma=False,
    )
```

```python
import functools

import jax
import jax.numpy as jnp
import numpy as np
from jax import lax
from jax.experimental import pallas as pl
from jax.experimental.pallas import tpu as pltpu
from jax.sharding import PartitionSpec as P

AXES = ("dp", "rep")
NX, NY, NZ = 4, 4, 8
CHIPS = NX * NY * NZ
GROUPS = 64
HALF = GROUPS // 2
SOURCES = 32
CAP = 32
ROWS = 1024
D = 768
EXTRA = 16
COLUMNS = D // 128
CELL = COLUMNS * 32 + 8
HALF_ROWS = 512
ORDERS = 4096
VMEM = 24 * 1024 * 1024
FULL = 62 * 1024 * 1024
PAIRS = 32 * 1024 * 1024
OWN = 121 * 512 * 1024
NEAR = 233 * 256 * 1024


def device(x, y, z, core):
    return ((y * NZ + z) * 2 + core) * NX + x


ROUTES = [[device(x, y, z, 0) for y in range(NY) for z in range(NZ)] for x in range(NX)] + [
    [device(x, y, z, 1) for x in range(NX) for z in range(NZ)] for y in range(NY)
]
RETURNS = [
    [device(x, y, z, 0) for x in range(NX) for y in range(NY) for z in range(NZ)],
    [device(x, y, z, 1) for y in range(NY) for x in range(NX) for z in range(NZ)],
]


def ring(step):
    pairs = []
    for y in range(NY):
        for z in range(NZ):
            for x in range(NX):
                pairs.append((device(x, y, z, 0), device((x + step) % NX, y, z, 0)))
                pairs.append((device(x, y, z, 1), device(x, (y + step) % NY, z, 1)))
    return pairs


SIBLING = [(dp * NX + x, (dp ^ 1) * NX + x) for dp in range(NY * NZ * 2) for x in range(NX)]


def exchange(rows, groups):
    return lax.all_to_all(rows, AXES, split_axis=0, concat_axis=0, tiled=True, axis_index_groups=groups)


def send(rows, pairs):
    return lax.ppermute(rows, AXES, pairs)


def cost(flops, size):
    return pl.CostEstimate(flops=flops, bytes_accessed=size, transcendentals=0)


def across(one, other):
    return lax.dot_general(one, other, (((1,), (1,)), ((), ())), preferred_element_type=jnp.float32)


def key_tables(info, ids, order, core, mine):
    group, rank = info[0:1], info[1:2]
    key = (ids & 1) * ORDERS + order
    serving = group >> 5
    here = jnp.where((serving == core) if mine else (serving != core), group & (HALF - 1), -1)
    here = lax.broadcasted_iota(jnp.int32, (SOURCES, ROWS), 0) == here
    lanes = lax.broadcasted_iota(jnp.int32, (128, ROWS), 0) == rank
    lanes = jnp.where(lanes, 1.0, 0.0).astype(jnp.bfloat16)
    parts = ((key >> 7) + 1).astype(jnp.float32), (key & 127).astype(jnp.float32)
    return [across(jnp.where(here, part, 0.0).astype(jnp.bfloat16), lanes) for part in parts]


def fill_cells(out, first, count, rows, high, low):
    for column in range(COLUMNS):
        out[first : first + count, column * CAP : (column + 1) * CAP, :] = (
            rows[:, column * 128 : (column + 1) * 128].reshape(count, CAP, 128).astype(jnp.bfloat16)
        )
    sub = lax.broadcasted_iota(jnp.int32, (count, 8, 128), 1)
    high, low = high[first : first + count][:, None, :], low[first : first + count][:, None, :]
    tile = jnp.where(sub == 0, high, jnp.where(sub == 1, low, 0.0))
    out[first : first + count, COLUMNS * CAP :, :] = tile.astype(jnp.bfloat16)


def where_am_i():
    dp = lax.axis_index("dp")
    return lax.axis_index("rep"), dp >> 4, (dp >> 1) & (NZ - 1), dp & 1


def slots_of(info, core, mine):
    group, rank = info[0:1], info[1:2]
    serving = group >> 5
    slot = (group & (HALF - 1)) * CAP + rank
    return jnp.where((serving == core) if mine else (serving != core), slot, -1)


def onehot(slot, first, count):
    rows = lax.broadcasted_iota(jnp.int32, (count, ROWS), 0) + first
    return jnp.where(rows == slot, 1.0, 0.0).astype(jnp.bfloat16)


def normalize(rows):
    wide = rows.astype(jnp.float32)
    scale = 1.0 / jnp.sqrt(jnp.sum(wide * wide, axis=1, keepdims=True) + 1e-06)
    return (wide * scale).astype(jnp.bfloat16)


PIECE = 512
PIECES = ROWS // PIECE
SPAN = 256


def prep_kernel(emb_ref, ids_ref, order_ref, box_ref, info_ref, rows, in_sem):
    load = pltpu.make_async_copy(emb_ref, rows, in_sem)
    load.start()
    group = ids_ref[...] >> 1
    member = lax.broadcasted_iota(jnp.int32, (GROUPS, ROWS), 0) == group
    hot = jnp.where(member, 1.0, 0.0)
    earlier = jnp.where(
        lax.broadcasted_iota(jnp.int32, (SPAN, SPAN), 0) < lax.broadcasted_iota(jnp.int32, (SPAN, SPAN), 1), 1.0, 0.0
    ).astype(jnp.bfloat16)
    before = jnp.zeros((GROUPS, 1), jnp.float32)
    ranks = []
    for n in range(ROWS // SPAN):
        here = hot[:, n * SPAN : (n + 1) * SPAN]
        count = jnp.dot(here.astype(jnp.bfloat16), earlier, preferred_element_type=jnp.float32) + before
        ranks.append(jnp.sum(here * count, axis=0, keepdims=True))
        before = before + jnp.sum(here, axis=1, keepdims=True)
    rank = jnp.concatenate(ranks, axis=1).astype(jnp.int32)
    which = lax.broadcasted_iota(jnp.int32, (8, ROWS), 0)
    info = jnp.where(which == 0, group, jnp.where(which == 1, rank, 0))
    info_ref[...] = info
    core = where_am_i()[3]
    slot = slots_of(info, core, True)
    high, low = key_tables(info, ids_ref[...], order_ref[...], core, True)
    load.wait()
    for n in range(PIECES):
        count = PIECE // CAP
        pick = onehot(slot, n * PIECE, PIECE)
        found = jnp.dot(pick, rows[...], preferred_element_type=jnp.float32)
        fill_cells(box_ref, n * count, count, found, high, low)


def prep(embeddings, ids, order):
    return pl.pallas_call(
        prep_kernel,
        out_shape=(
            jax.ShapeDtypeStruct((SOURCES, CELL, 128), jnp.bfloat16),
            jax.ShapeDtypeStruct((8, ROWS), jnp.int32),
        ),
        in_specs=[pl.BlockSpec(memory_space=pl.ANY)] + [pl.BlockSpec(memory_space=pltpu.VMEM)] * 2,
        out_specs=tuple([pl.BlockSpec(memory_space=pltpu.VMEM)] * 2),
        scratch_shapes=[pltpu.VMEM((ROWS, D), jnp.bfloat16), pltpu.SemaphoreType.DMA],
        compiler_params=pltpu.CompilerParams(vmem_limit_bytes=FULL),
        cost_estimate=cost(2 * ROWS * ROWS * D, 4 * ROWS * D),
        name="prep",
    )(embeddings, ids, order)


def hand_kernel(emb_ref, info_ref, ids_ref, order_ref, box_ref):
    info, core = info_ref[...], where_am_i()[3]
    pick = onehot(slots_of(info, core, False), 0, ROWS)
    found = jnp.dot(pick, normalize(emb_ref[...]), preferred_element_type=jnp.float32)
    high, low = key_tables(info, ids_ref[...], order_ref[...], core, False)
    fill_cells(box_ref, 0, SOURCES, found, high, low)


def hand(embeddings, info, ids, order):
    return pl.pallas_call(
        hand_kernel,
        out_shape=jax.ShapeDtypeStruct((SOURCES, CELL, 128), jnp.bfloat16),
        in_specs=[pl.BlockSpec(memory_space=pltpu.VMEM)] * 4,
        out_specs=pl.BlockSpec(memory_space=pltpu.VMEM),
        compiler_params=pltpu.CompilerParams(vmem_limit_bytes=VMEM),
        cost_estimate=cost(2 * ROWS * ROWS * D, 4 * ROWS * D),
        name="hand",
    )(embeddings, info, ids, order)


def open_kernel(raw, cells_ref, p_ref, m_ref):
    count = SOURCES // 2
    sub = lax.broadcasted_iota(jnp.int32, (count, 8, 128), 1)
    slot = lax.broadcasted_iota(jnp.int32, (count, CAP, 128), 1) == lax.broadcasted_iota(
        jnp.int32, (count, CAP, 128), 2
    )
    row = lax.broadcasted_iota(jnp.int32, (EXTRA, 128), 0)
    for number, out_ref in enumerate((p_ref, m_ref)):
        first = number * count
        columns = [
            cells_ref[first : first + count, column * CAP : (column + 1) * CAP, :].reshape(HALF_ROWS, 128)
            for column in range(COLUMNS)
        ]
        if raw:
            wide = [column.astype(jnp.float32) for column in columns]
            total = sum(column * column for column in wide)
            scale = 1.0 / jnp.sqrt(jnp.sum(total, axis=1, keepdims=True) + 1e-06)
            columns = [(column * scale).astype(jnp.bfloat16) for column in wide]
        for column in range(COLUMNS):
            out_ref[:HALF_ROWS, column * 128 : (column + 1) * 128] = columns[column]
        tile = cells_ref[first : first + count, COLUMNS * CAP :, :].astype(jnp.float32)
        keys = jnp.zeros((EXTRA, HALF_ROWS), jnp.float32)
        for part in range(2):
            its = jnp.sum(jnp.where(sub == part, tile, 0.0), axis=1)
            its = jnp.where(slot, its[:, None, :], 0.0).reshape(HALF_ROWS, 128).astype(jnp.bfloat16)
            keys += across(jnp.where(row == part, 1.0, 0.0).astype(jnp.bfloat16), its)
        out_ref[HALF_ROWS:] = jnp.concatenate(
            [keys, jnp.zeros((EXTRA, D - HALF_ROWS), jnp.float32)], axis=1
        ).astype(jnp.bfloat16)


def open_cells(cells, raw):
    return pl.pallas_call(
        functools.partial(open_kernel, raw),
        out_shape=tuple([jax.ShapeDtypeStruct((HALF_ROWS + EXTRA, D), jnp.bfloat16)] * 2),
        in_specs=[pl.BlockSpec(memory_space=pltpu.VMEM)],
        out_specs=tuple([pl.BlockSpec(memory_space=pltpu.VMEM)] * 2),
        compiler_params=pltpu.CompilerParams(vmem_limit_bytes=VMEM),
        cost_estimate=cost(0, 4 * ROWS * D),
        name="settle" if raw else "split",
    )(cells)


BLOCKS = [(part, far, chunk) for far in range(3) for chunk in range(2) for part in "PM"]


def pair_lists():
    pairs = []

    def all_chunks(one, other):
        for c in range(2):
            for e in range(2):
                pairs.append((one + (c,), other + (e,)))

    for part in "PM":
        pairs.append(((part, 0, 0), (part, 0, 1)))
        all_chunks((part, 0), (part, 1))
        pairs.append(((part, 0, 1), (part, 2, 0)))
    all_chunks(("P", 0), ("M", 0))
    all_chunks(("P", 0), ("M", 1))
    all_chunks(("P", 1), ("M", 1))
    pairs.append((("P", 1, 0), ("M", 2, 0)))
    pairs.append((("P", 1, 1), ("M", 2, 0)))
    pairs.append((("P", 2, 0), ("M", 1, 1)))
    pairs.append((("P", 1, 1), ("M", 2, 1)))
    by_place = [
        ((("P", 0, 0), ("P", 2, 0)), (("M", 0, 0), ("M", 2, 0))),
        ((("M", 0, 1), ("M", 2, 1)), (("P", 0, 1), ("P", 2, 1))),
    ]
    return pairs, by_place


def stage_of(pair):
    if all(chunk == 0 for part, far, chunk in pair):
        return 0 if all(far < 2 for part, far, chunk in pair) else 2
    return 1 + max(far for part, far, chunk in pair if chunk == 1)


def three_parts(values):
    parts = []
    for piece in range(3):
        parts.append(values.astype(jnp.bfloat16))
        values = values - parts[-1].astype(jnp.float32)
    return parts


def similar_kernel(blocks, early, n_tasks, n_before, *refs):
    n_blocks = len(blocks)
    tasks_ref, refs = refs[0], refs[1:]
    arrays, refs = refs[:n_blocks], refs[n_blocks:]
    befores, refs = refs[:n_before], refs[n_before:]
    out_ref, rows, kcol, ccol, krow, crow, best_row, best_col, s0, s1, sems = refs

    copies = [pltpu.make_async_copy(array, rows.at[slot], sems.at[slot]) for slot, array in enumerate(arrays)]
    for copy in copies:
        copy.start()
    for slot in range(n_blocks):
        best_row[slot] = jnp.full((HALF_ROWS, 128), -1.0, jnp.float32)
        best_col[slot] = jnp.full((8, HALF_ROWS), -1.0, jnp.float32)

    def cluster(key):
        return jnp.where(key >= ORDERS + 128, 2.0, jnp.where(key > 0, 1.0, 0.0))

    def arrive(slots):
        for slot in slots:
            copies[slot].wait()
        for slot in slots:
            parts = rows[slot, HALF_ROWS:, :HALF_ROWS].astype(jnp.float32)
            key = 128.0 * parts[0:1] + parts[1:2]
            krow[slot] = jnp.broadcast_to(key, (8, HALF_ROWS))
            crow[slot] = cluster(krow[slot])
            key = jnp.transpose(jnp.broadcast_to(key, (128, HALF_ROWS)))
            kcol[slot] = key
            ccol[slot] = cluster(key)

    x, y, z, core = where_am_i()
    here = jnp.where(core == 0, x, y)
    table = jnp.where(here < 2, 0, 3 * n_tasks)

    def multiply(task, s):
        a, b = tasks_ref[table + 3 * task], tasks_ref[table + 3 * task + 1]
        s[...] = across(rows[a, :HALF_ROWS], rows[b, :HALF_ROWS])

    step = 16

    def reduce(task, s):
        a, b, sink = [tasks_ref[table + 3 * task + n] for n in range(3)]
        kb, cb = krow[b], crow[b]
        for row in range(0, HALF_ROWS, step):
            ka = kcol[a, row : row + step].reshape(step // 8, 8, 128)
            ca = ccol[a, row : row + step].reshape(step // 8, 8, 128)
            best = best_row[a, row : row + step]
            for at in range(0, HALF_ROWS, 128):
                found = s[row : row + step, at : at + 128].reshape(step // 8, 8, 128)
                same = jnp.where(ca == cb[None, :, at : at + 128], found, -1.0)
                later = kb[None, :, at : at + 128] < ka
                best = jnp.maximum(best, jnp.where(later, same, -1.0).reshape(step, 128))
                other = jnp.max(jnp.where(later, -1.0, same), axis=0)
                best_col[sink, :, at : at + 128] = jnp.maximum(best_col[sink, :, at : at + 128], other)
            best_row[a, row : row + step] = best

    def two(turn, carry):
        multiply(2 * turn + 1, s1)
        reduce(2 * turn, s0)
        multiply(2 * turn + 2, s0)
        reduce(2 * turn + 1, s1)
        return carry

    turns = (n_tasks - 1) // 2
    start, early = early
    arrive(range(early))
    multiply(0, s0)
    if start:
        lax.fori_loop(0, start, two, 0)
    arrive(range(early, n_blocks))
    if turns > start:
        lax.fori_loop(start, turns, two, 0)
    if n_tasks % 2 == 0:
        multiply(n_tasks - 1, s1)
    reduce(2 * turns, s0)
    if n_tasks % 2 == 0:
        reduce(n_tasks - 1, s1)

    empty = jnp.full((CAP, HALF_ROWS), -1.0, jnp.float32)
    diagonal = lax.broadcasted_iota(jnp.int32, (CAP, HALF_ROWS), 0) == (
        lax.broadcasted_iota(jnp.int32, (CAP, HALF_ROWS), 1) & (CAP - 1)
    )
    values = {}
    for number, part in enumerate("PM"):
        for level in range(2):
            tiles = [empty] * 4
            for slot, (its, far, chunk) in enumerate(blocks):
                if its == part and far // 2 == level:
                    by_row = jnp.max(jnp.transpose(best_row[slot]), axis=0, keepdims=True)
                    by_col = jnp.max(best_col[slot], axis=0, keepdims=True)
                    tiles[2 * (far & 1) + chunk] = jnp.where(diagonal, jnp.maximum(by_row, by_col), -1.0)
            if all(tile is empty for tile in tiles):
                value = jnp.full((HALF_ROWS // CAP, 128), -1.0, jnp.float32)
            else:
                value = jnp.transpose(jnp.concatenate(tiles, axis=0)).reshape(HALF_ROWS // CAP, CAP, 128)
                value = jnp.max(value, axis=1)
            at = pl.ds(level * SOURCES + number * (SOURCES // 2), SOURCES // 2)
            for before in befores:
                value = jnp.maximum(value, before[at, :])
            values[level, number] = value
    values = jnp.concatenate([values[level, number] for level in range(2) for number in range(2)], axis=0)
    if not befores:
        out_ref[...] = values
        return
    row = lax.broadcasted_iota(jnp.int32, (CHIPS, 2 * SOURCES), 0)
    column = lax.broadcasted_iota(jnp.int32, (CHIPS, 2 * SOURCES), 1)
    source = row & (SOURCES - 1)
    far = (here - (row >> 5)) * jnp.where(source < SOURCES // 2, 1, -1) & 3
    wanted = (column == source) & (far < 2) | (column == source + SOURCES) & (far == 2)
    pick = jnp.where(wanted, 1.0, 0.0).astype(jnp.bfloat16)
    out_ref[...] = jnp.dot(
        jnp.concatenate([pick] * 3, axis=1),
        jnp.concatenate(three_parts(values), axis=0),
        preferred_element_type=jnp.float32,
    )


def similar(hold, low, high, befores, name, limit, start):
    first_use = {}
    for number, pairs in enumerate(zip(low, high)):
        for pair in pairs:
            for block in pair:
                first_use.setdefault(block, number)
    blocks = sorted(first_use, key=lambda block: (first_use[block], BLOCKS.index(block)))
    early = start, sum(first_use[block] <= 2 * start for block in blocks)
    place = {block: number for number, block in enumerate(blocks)}
    spare = n = len(blocks)

    def table(pairs):
        return np.array(
            [(place[a], place[b], spare if a == b else place[b]) for a, b in pairs], np.int32
        ).reshape(-1)

    tasks = jnp.asarray(np.concatenate([table(low), table(high)]))
    return pl.pallas_call(
        functools.partial(similar_kernel, blocks, early, len(low), len(befores)),
        out_shape=jax.ShapeDtypeStruct((CHIPS if befores else 2 * SOURCES, 128), jnp.float32),
        in_specs=[pl.BlockSpec(memory_space=pltpu.SMEM)]
        + [pl.BlockSpec(memory_space=pl.ANY)] * n
        + [pl.BlockSpec(memory_space=pltpu.VMEM)] * len(befores),
        out_specs=pl.BlockSpec(memory_space=pltpu.VMEM),
        scratch_shapes=[
            pltpu.VMEM((n, HALF_ROWS + EXTRA, D), jnp.bfloat16),
            pltpu.VMEM((n, HALF_ROWS, 128), jnp.float32),
            pltpu.VMEM((n, HALF_ROWS, 128), jnp.float32),
            pltpu.VMEM((n, 8, HALF_ROWS), jnp.float32),
            pltpu.VMEM((n, 8, HALF_ROWS), jnp.float32),
            pltpu.VMEM((n, HALF_ROWS, 128), jnp.float32),
            pltpu.VMEM((n + 1, 8, HALF_ROWS), jnp.float32),
            pltpu.VMEM((HALF_ROWS, HALF_ROWS), jnp.float32),
            pltpu.VMEM((HALF_ROWS, HALF_ROWS), jnp.float32),
            pltpu.SemaphoreType.DMA((n,)),
        ],
        compiler_params=pltpu.CompilerParams(vmem_limit_bytes=limit),
        cost_estimate=cost(2 * D * HALF_ROWS * HALF_ROWS * len(low), 2 * n * HALF_ROWS * D),
        name=name,
    )(tasks, *[hold[block] for block in blocks], *befores)


def answer_kernel(away, info_ref, values_ref, *refs):
    info, out_ref = info_ref[...], refs[-1]
    group, rank = info[0:1], info[1:2]
    x, y, z, core = where_am_i()
    serving = (core + away) & 1
    here = (group >> 5) == serving
    ring_place, source = jnp.where(serving == 0, x, y), jnp.where(serving == 0, y, x)
    step = jnp.where(source < 2, 1, -1)
    place_of = lax.broadcasted_iota(jnp.int32, (SOURCES, ROWS), 0)
    pick = jnp.where(place_of == jnp.where(here, group & (HALF - 1), -1), 1.0, 0.0).astype(jnp.bfloat16)
    pick = jnp.concatenate([pick] * 3, axis=0)
    lane_of = lax.broadcasted_iota(jnp.int32, (128, ROWS), 0)
    best = refs[0][...] if away else jnp.full((1, ROWS), -1.0, jnp.float32)
    for far in range(3):
        holder = pl.multiple_of(((ring_place + far * step) & 3) * SOURCES, SOURCES)
        parts = jnp.concatenate(three_parts(values_ref[pl.ds(holder, SOURCES), :]), axis=0)
        found = lax.dot_general(parts, pick, (((0,), (0,)), ((), ())), preferred_element_type=jnp.float32)
        wanted = jnp.where(here, (far & 1) * 64 + away * CAP + rank, -1)
        found = jnp.max(jnp.where(lane_of == wanted, found, -1.0), axis=0, keepdims=True)
        best = jnp.maximum(best, found)
    out_ref[...] = best


def answer(away, info, values, *before):
    return pl.pallas_call(
        functools.partial(answer_kernel, away),
        out_shape=jax.ShapeDtypeStruct((1, ROWS), jnp.float32),
        in_specs=[pl.BlockSpec(memory_space=pltpu.VMEM)] * (2 + len(before)),
        out_specs=pl.BlockSpec(memory_space=pltpu.VMEM),
        compiler_params=pltpu.CompilerParams(vmem_limit_bytes=VMEM),
        cost_estimate=cost(2 * 3 * 3 * 128 * 128 * ROWS, 4 * 128 * 128),
        name="answer",
    )(info, values, *before)


def local(embeddings, cluster_ids, member_order):
    ids, order = cluster_ids.reshape(1, ROWS), member_order.reshape(1, ROWS)

    box, info = prep(embeddings, ids, order)
    chunk1 = exchange(box, ROUTES)
    handed = send(hand(embeddings, info, ids, order), SIBLING)
    chunk1, handed = lax.optimization_barrier((chunk1, handed))
    chunk2 = exchange(handed, ROUTES)

    hold = {}

    def ring_blocks(far, chunk, blocks):
        hold["P", far, chunk], hold["M", far, chunk] = blocks
        return blocks

    def onward(blocks):
        return send(blocks[0], ring(1)), send(blocks[1], ring(-1))

    pairs, by_place = pair_lists()
    pairs += [((part, 0, chunk),) * 2 for part in "PM" for chunk in range(2)]

    def run(stage, name, befores=()):
        low = [pair for pair in pairs if stage_of(pair) == stage]
        low.sort(key=lambda pair: sum(chunk == 0 for part, far, chunk in pair))
        high = list(low)
        for one, other in by_place:
            if stage_of(one) == stage:
                low.append(one)
                high.append(other)
        limit, start = ((PAIRS, 0), (OWN, 1), (NEAR, 1), (PAIRS, 0))[stage]
        return similar(hold, low, high, befores, name, limit, start)

    own1 = ring_blocks(0, 0, open_cells(chunk1, True))
    near1 = ring_blocks(1, 0, onward(own1))
    far1 = onward(near1)
    first = run(0, "first")
    chunk2, own1, near1, far1, first = lax.optimization_barrier((chunk2, own1, near1, far1, first))
    for far, blocks in enumerate((own1, near1, far1)):
        ring_blocks(far, 0, blocks)
    own2 = ring_blocks(0, 1, open_cells(chunk2, False))
    near2 = onward(own2)
    own = run(1, "own")
    near2, own = lax.optimization_barrier((near2, own))
    ring_blocks(1, 1, near2)
    ring_blocks(2, 1, onward(near2))
    near = run(2, "near")
    last = run(3, "far", (first, own, near))
    mine = exchange(last.reshape(CHIPS, 1, 128), RETURNS).reshape(CHIPS, 128)
    best = answer(0, info, mine)
    return answer(1, info, send(mine, SIBLING), best).reshape(ROWS)


def solution(mesh):
    return jax.shard_map(
        local,
        mesh=mesh,
        in_specs=(P(AXES, None), P(AXES), P(AXES)),
        out_specs=P(AXES),
        check_vma=False,
    )
```

```python
import functools

import jax
import jax.numpy as jnp
import numpy as np
from jax import lax
from jax.experimental import pallas as pl
from jax.experimental.pallas import tpu as pltpu
from jax.sharding import PartitionSpec as P

AXES = ("dp", "rep")
NX, NY, NZ = 4, 4, 8
CHIPS = NX * NY * NZ
GROUPS = 64
HALF = GROUPS // 2
SOURCES = 32
CAP = 32
ROWS = 1024
D = 768
EXTRA = 16
COLUMNS = D // 128
CELL = COLUMNS * 32 + 8
HALF_ROWS = 512
ORDERS = 4096
VMEM = 24 * 1024 * 1024
FULL = 62 * 1024 * 1024
PAIRS = 32 * 1024 * 1024
OWN = 121 * 512 * 1024
NEAR = 233 * 256 * 1024


def device(x, y, z, core):
    return ((y * NZ + z) * 2 + core) * NX + x


ROUTES = [[device(x, y, z, 0) for y in range(NY) for z in range(NZ)] for x in range(NX)] + [
    [device(x, y, z, 1) for x in range(NX) for z in range(NZ)] for y in range(NY)
]
RETURNS = [
    [device(x, y, z, 0) for x in range(NX) for y in range(NY) for z in range(NZ)],
    [device(x, y, z, 1) for y in range(NY) for x in range(NX) for z in range(NZ)],
]


def ring(step):
    pairs = []
    for y in range(NY):
        for z in range(NZ):
            for x in range(NX):
                pairs.append((device(x, y, z, 0), device((x + step) % NX, y, z, 0)))
                pairs.append((device(x, y, z, 1), device(x, (y + step) % NY, z, 1)))
    return pairs


SIBLING = [(dp * NX + x, (dp ^ 1) * NX + x) for dp in range(NY * NZ * 2) for x in range(NX)]


def exchange(rows, groups):
    return lax.all_to_all(rows, AXES, split_axis=0, concat_axis=0, tiled=True, axis_index_groups=groups)


def send(rows, pairs):
    return lax.ppermute(rows, AXES, pairs)


def cost(flops, size):
    return pl.CostEstimate(flops=flops, bytes_accessed=size, transcendentals=0)


def across(one, other):
    return lax.dot_general(one, other, (((1,), (1,)), ((), ())), preferred_element_type=jnp.float32)


def key_tables(info, ids, order, core, mine):
    group, rank = info[0:1], info[1:2]
    key = (ids & 1) * ORDERS + order
    serving = group >> 5
    here = jnp.where((serving == core) if mine else (serving != core), group & (HALF - 1), -1)
    here = lax.broadcasted_iota(jnp.int32, (SOURCES, ROWS), 0) == here
    lanes = lax.broadcasted_iota(jnp.int32, (128, ROWS), 0) == rank
    lanes = jnp.where(lanes, 1.0, 0.0).astype(jnp.bfloat16)
    parts = ((key >> 7) + 1).astype(jnp.float32), (key & 127).astype(jnp.float32)
    return [across(jnp.where(here, part, 0.0).astype(jnp.bfloat16), lanes) for part in parts]


def fill_cells(out, first, count, rows, high, low):
    for column in range(COLUMNS):
        out[first : first + count, column * CAP : (column + 1) * CAP, :] = (
            rows[:, column * 128 : (column + 1) * 128].reshape(count, CAP, 128).astype(jnp.bfloat16)
        )
    sub = lax.broadcasted_iota(jnp.int32, (count, 8, 128), 1)
    high, low = high[first : first + count][:, None, :], low[first : first + count][:, None, :]
    tile = jnp.where(sub == 0, high, jnp.where(sub == 1, low, 0.0))
    out[first : first + count, COLUMNS * CAP :, :] = tile.astype(jnp.bfloat16)


def where_am_i():
    dp = lax.axis_index("dp")
    return lax.axis_index("rep"), dp >> 4, (dp >> 1) & (NZ - 1), dp & 1


def slots_of(info, core, mine):
    group, rank = info[0:1], info[1:2]
    serving = group >> 5
    slot = (group & (HALF - 1)) * CAP + rank
    return jnp.where((serving == core) if mine else (serving != core), slot, -1)


def onehot(slot, first, count):
    rows = lax.broadcasted_iota(jnp.int32, (count, ROWS), 0) + first
    return jnp.where(rows == slot, 1.0, 0.0).astype(jnp.bfloat16)


def normalize(rows):
    wide = rows.astype(jnp.float32)
    scale = 1.0 / jnp.sqrt(jnp.sum(wide * wide, axis=1, keepdims=True) + 1e-06)
    return (wide * scale).astype(jnp.bfloat16)


PIECE = 512
PIECES = ROWS // PIECE
SPAN = 256


def prep_kernel(emb_ref, ids_ref, order_ref, box_ref, info_ref, rows, in_sem):
    load = pltpu.make_async_copy(emb_ref, rows, in_sem)
    load.start()
    group = ids_ref[...] >> 1
    member = lax.broadcasted_iota(jnp.int32, (GROUPS, ROWS), 0) == group
    hot = jnp.where(member, 1.0, 0.0)
    earlier = jnp.where(
        lax.broadcasted_iota(jnp.int32, (SPAN, SPAN), 0) < lax.broadcasted_iota(jnp.int32, (SPAN, SPAN), 1), 1.0, 0.0
    ).astype(jnp.bfloat16)
    before = jnp.zeros((GROUPS, 1), jnp.float32)
    ranks = []
    for n in range(ROWS // SPAN):
        here = hot[:, n * SPAN : (n + 1) * SPAN]
        count = jnp.dot(here.astype(jnp.bfloat16), earlier, preferred_element_type=jnp.float32) + before
        ranks.append(jnp.sum(here * count, axis=0, keepdims=True))
        before = before + jnp.sum(here, axis=1, keepdims=True)
    rank = jnp.concatenate(ranks, axis=1).astype(jnp.int32)
    which = lax.broadcasted_iota(jnp.int32, (8, ROWS), 0)
    info = jnp.where(which == 0, group, jnp.where(which == 1, rank, 0))
    info_ref[...] = info
    core = where_am_i()[3]
    slot = slots_of(info, core, True)
    high, low = key_tables(info, ids_ref[...], order_ref[...], core, True)
    load.wait()
    for n in range(PIECES):
        count = PIECE // CAP
        pick = onehot(slot, n * PIECE, PIECE)
        found = jnp.dot(pick, rows[...], preferred_element_type=jnp.float32)
        fill_cells(box_ref, n * count, count, found, high, low)


def prep(embeddings, ids, order):
    return pl.pallas_call(
        prep_kernel,
        out_shape=(
            jax.ShapeDtypeStruct((SOURCES, CELL, 128), jnp.bfloat16),
            jax.ShapeDtypeStruct((8, ROWS), jnp.int32),
        ),
        in_specs=[pl.BlockSpec(memory_space=pl.ANY)] + [pl.BlockSpec(memory_space=pltpu.VMEM)] * 2,
        out_specs=tuple([pl.BlockSpec(memory_space=pltpu.VMEM)] * 2),
        scratch_shapes=[pltpu.VMEM((ROWS, D), jnp.bfloat16), pltpu.SemaphoreType.DMA],
        compiler_params=pltpu.CompilerParams(vmem_limit_bytes=FULL),
        cost_estimate=cost(2 * ROWS * ROWS * D, 4 * ROWS * D),
        name="prep",
    )(embeddings, ids, order)


def hand_kernel(emb_ref, info_ref, ids_ref, order_ref, box_ref):
    info, core = info_ref[...], where_am_i()[3]
    pick = onehot(slots_of(info, core, False), 0, ROWS)
    found = jnp.dot(pick, normalize(emb_ref[...]), preferred_element_type=jnp.float32)
    high, low = key_tables(info, ids_ref[...], order_ref[...], core, False)
    fill_cells(box_ref, 0, SOURCES, found, high, low)


def hand(embeddings, info, ids, order):
    return pl.pallas_call(
        hand_kernel,
        out_shape=jax.ShapeDtypeStruct((SOURCES, CELL, 128), jnp.bfloat16),
        in_specs=[pl.BlockSpec(memory_space=pltpu.VMEM)] * 4,
        out_specs=pl.BlockSpec(memory_space=pltpu.VMEM),
        compiler_params=pltpu.CompilerParams(vmem_limit_bytes=VMEM),
        cost_estimate=cost(2 * ROWS * ROWS * D, 4 * ROWS * D),
        name="hand",
    )(embeddings, info, ids, order)


def open_kernel(raw, cells_ref, p_ref, m_ref):
    count = SOURCES // 2
    sub = lax.broadcasted_iota(jnp.int32, (count, 8, 128), 1)
    slot = lax.broadcasted_iota(jnp.int32, (count, CAP, 128), 1) == lax.broadcasted_iota(
        jnp.int32, (count, CAP, 128), 2
    )
    row = lax.broadcasted_iota(jnp.int32, (EXTRA, 128), 0)
    for number, out_ref in enumerate((p_ref, m_ref)):
        first = number * count
        columns = [
            cells_ref[first : first + count, column * CAP : (column + 1) * CAP, :].reshape(HALF_ROWS, 128)
            for column in range(COLUMNS)
        ]
        if raw:
            wide = [column.astype(jnp.float32) for column in columns]
            total = sum(column * column for column in wide)
            scale = 1.0 / jnp.sqrt(jnp.sum(total, axis=1, keepdims=True) + 1e-06)
            columns = [(column * scale).astype(jnp.bfloat16) for column in wide]
        for column in range(COLUMNS):
            out_ref[:HALF_ROWS, column * 128 : (column + 1) * 128] = columns[column]
        tile = cells_ref[first : first + count, COLUMNS * CAP :, :].astype(jnp.float32)
        keys = jnp.zeros((EXTRA, HALF_ROWS), jnp.float32)
        for part in range(2):
            its = jnp.sum(jnp.where(sub == part, tile, 0.0), axis=1)
            its = jnp.where(slot, its[:, None, :], 0.0).reshape(HALF_ROWS, 128).astype(jnp.bfloat16)
            keys += across(jnp.where(row == part, 1.0, 0.0).astype(jnp.bfloat16), its)
        out_ref[HALF_ROWS:] = jnp.concatenate(
            [keys, jnp.zeros((EXTRA, D - HALF_ROWS), jnp.float32)], axis=1
        ).astype(jnp.bfloat16)


def open_cells(cells, raw):
    return pl.pallas_call(
        functools.partial(open_kernel, raw),
        out_shape=tuple([jax.ShapeDtypeStruct((HALF_ROWS + EXTRA, D), jnp.bfloat16)] * 2),
        in_specs=[pl.BlockSpec(memory_space=pltpu.VMEM)],
        out_specs=tuple([pl.BlockSpec(memory_space=pltpu.VMEM)] * 2),
        compiler_params=pltpu.CompilerParams(vmem_limit_bytes=VMEM),
        cost_estimate=cost(0, 4 * ROWS * D),
        name="settle" if raw else "split",
    )(cells)


BLOCKS = [(part, far, chunk) for far in range(3) for chunk in range(2) for part in "PM"]


def pair_lists():
    pairs = []

    def all_chunks(one, other):
        for c in range(2):
            for e in range(2):
                pairs.append((one + (c,), other + (e,)))

    for part in "PM":
        pairs.append(((part, 0, 0), (part, 0, 1)))
        all_chunks((part, 0), (part, 1))
        pairs.append(((part, 0, 1), (part, 2, 0)))
    all_chunks(("P", 0), ("M", 0))
    all_chunks(("P", 0), ("M", 1))
    all_chunks(("P", 1), ("M", 1))
    pairs.append((("P", 1, 0), ("M", 2, 0)))
    pairs.append((("P", 1, 1), ("M", 2, 0)))
    pairs.append((("P", 2, 0), ("M", 1, 1)))
    pairs.append((("P", 2, 1), ("M", 1, 1)))
    by_place = [
        ((("P", 0, 0), ("P", 2, 0)), (("M", 0, 0), ("M", 2, 0))),
        ((("M", 0, 1), ("M", 2, 1)), (("P", 0, 1), ("P", 2, 1))),
    ]
    return pairs, by_place


def stage_of(pair):
    if all(chunk == 0 for part, far, chunk in pair):
        return 0 if all(far < 2 for part, far, chunk in pair) else 2
    return 1 + max(far for part, far, chunk in pair if chunk == 1)


def three_parts(values):
    parts = []
    for piece in range(3):
        parts.append(values.astype(jnp.bfloat16))
        values = values - parts[-1].astype(jnp.float32)
    return parts


def similar_kernel(blocks, early, n_tasks, n_before, *refs):
    n_blocks = len(blocks)
    tasks_ref, refs = refs[0], refs[1:]
    arrays, refs = refs[:n_blocks], refs[n_blocks:]
    befores, refs = refs[:n_before], refs[n_before:]
    out_ref, rows, kcol, ccol, krow, crow, best_row, best_col, s0, s1, sems = refs

    copies = [pltpu.make_async_copy(array, rows.at[slot], sems.at[slot]) for slot, array in enumerate(arrays)]
    for copy in copies:
        copy.start()
    for slot in range(n_blocks):
        best_row[slot] = jnp.full((HALF_ROWS, 128), -1.0, jnp.float32)
        best_col[slot] = jnp.full((8, HALF_ROWS), -1.0, jnp.float32)

    def cluster(key):
        return jnp.where(key >= ORDERS + 128, 2.0, jnp.where(key > 0, 1.0, 0.0))

    def arrive(slots):
        for slot in slots:
            copies[slot].wait()

    def make_keys(slots):
        for slot in slots:
            parts = rows[slot, HALF_ROWS:, :HALF_ROWS].astype(jnp.float32)
            key = 128.0 * parts[0:1] + parts[1:2]
            krow[slot] = jnp.broadcast_to(key, (8, HALF_ROWS))
            crow[slot] = cluster(krow[slot])
            key = jnp.transpose(jnp.broadcast_to(key, (128, HALF_ROWS)))
            kcol[slot] = key
            ccol[slot] = cluster(key)

    x, y, z, core = where_am_i()
    here = jnp.where(core == 0, x, y)
    table = jnp.where(here < 2, 0, 3 * n_tasks)

    def multiply(task, s):
        a, b = tasks_ref[table + 3 * task], tasks_ref[table + 3 * task + 1]
        s[...] = across(rows[a, :HALF_ROWS], rows[b, :HALF_ROWS])

    step = 8

    def reduce(task, s):
        a, b, sink = [tasks_ref[table + 3 * task + n] for n in range(3)]
        kb, cb = krow[b], crow[b]
        for row in range(0, HALF_ROWS, step):
            ka = kcol[a, row : row + step].reshape(step // 8, 8, 128)
            ca = ccol[a, row : row + step].reshape(step // 8, 8, 128)
            best = best_row[a, row : row + step]
            for at in range(0, HALF_ROWS, 128):
                found = s[row : row + step, at : at + 128].reshape(step // 8, 8, 128)
                same = jnp.where(ca == cb[None, :, at : at + 128], found, -1.0)
                later = kb[None, :, at : at + 128] < ka
                best = jnp.maximum(best, jnp.where(later, same, -1.0).reshape(step, 128))
                other = jnp.max(jnp.where(later, -1.0, same), axis=0)
                best_col[sink, :, at : at + 128] = jnp.maximum(best_col[sink, :, at : at + 128], other)
            best_row[a, row : row + step] = best

    def two(turn, carry):
        multiply(2 * turn + 1, s1)
        reduce(2 * turn, s0)
        multiply(2 * turn + 2, s0)
        reduce(2 * turn + 1, s1)
        return carry

    turns = (n_tasks - 1) // 2
    start, early = early
    arrive(range(early))
    multiply(0, s0)
    make_keys(range(early))
    if start:
        lax.fori_loop(0, start, two, 0)
    arrive(range(early, n_blocks))
    if turns > start:
        make_keys(range(early, n_blocks))
        lax.fori_loop(start, turns, two, 0)
    if n_tasks % 2 == 0:
        multiply(n_tasks - 1, s1)
    if turns == start:
        make_keys(range(early, n_blocks))
    reduce(2 * turns, s0)
    if n_tasks % 2 == 0:
        reduce(n_tasks - 1, s1)

    empty = jnp.full((CAP, HALF_ROWS), -1.0, jnp.float32)
    diagonal = lax.broadcasted_iota(jnp.int32, (CAP, HALF_ROWS), 0) == (
        lax.broadcasted_iota(jnp.int32, (CAP, HALF_ROWS), 1) & (CAP - 1)
    )
    values = {}
    for number, part in enumerate("PM"):
        for level in range(2):
            tiles = [empty] * 4
            for slot, (its, far, chunk) in enumerate(blocks):
                if its == part and far // 2 == level:
                    by_row = jnp.max(jnp.transpose(best_row[slot]), axis=0, keepdims=True)
                    by_col = jnp.max(best_col[slot], axis=0, keepdims=True)
                    tiles[2 * (far & 1) + chunk] = jnp.where(diagonal, jnp.maximum(by_row, by_col), -1.0)
            if all(tile is empty for tile in tiles):
                value = jnp.full((HALF_ROWS // CAP, 128), -1.0, jnp.float32)
            else:
                value = jnp.transpose(jnp.concatenate(tiles, axis=0)).reshape(HALF_ROWS // CAP, CAP, 128)
                value = jnp.max(value, axis=1)
            at = pl.ds(level * SOURCES + number * (SOURCES // 2), SOURCES // 2)
            for before in befores:
                value = jnp.maximum(value, before[at, :])
            values[level, number] = value
    values = jnp.concatenate([values[level, number] for level in range(2) for number in range(2)], axis=0)
    if not befores:
        out_ref[...] = values
        return
    row = lax.broadcasted_iota(jnp.int32, (CHIPS, 2 * SOURCES), 0)
    column = lax.broadcasted_iota(jnp.int32, (CHIPS, 2 * SOURCES), 1)
    source = row & (SOURCES - 1)
    far = (here - (row >> 5)) * jnp.where(source < SOURCES // 2, 1, -1) & 3
    wanted = (column == source) & (far < 2) | (column == source + SOURCES) & (far == 2)
    pick = jnp.where(wanted, 1.0, 0.0).astype(jnp.bfloat16)
    out_ref[...] = jnp.dot(
        jnp.concatenate([pick] * 3, axis=1),
        jnp.concatenate(three_parts(values), axis=0),
        preferred_element_type=jnp.float32,
    )


def similar(hold, low, high, befores, name, limit, start):
    first_use = {}
    for number, pairs in enumerate(zip(low, high)):
        for pair in pairs:
            for block in pair:
                first_use.setdefault(block, number)
    blocks = sorted(first_use, key=lambda block: (first_use[block], BLOCKS.index(block)))
    early = start, sum(first_use[block] <= 2 * start for block in blocks)
    place = {block: number for number, block in enumerate(blocks)}
    spare = n = len(blocks)

    def table(pairs):
        return np.array(
            [(place[a], place[b], spare if a == b else place[b]) for a, b in pairs], np.int32
        ).reshape(-1)

    tasks = jnp.asarray(np.concatenate([table(low), table(high)]))
    return pl.pallas_call(
        functools.partial(similar_kernel, blocks, early, len(low), len(befores)),
        out_shape=jax.ShapeDtypeStruct((CHIPS if befores else 2 * SOURCES, 128), jnp.float32),
        in_specs=[pl.BlockSpec(memory_space=pltpu.SMEM)]
        + [pl.BlockSpec(memory_space=pl.ANY)] * n
        + [pl.BlockSpec(memory_space=pltpu.VMEM)] * len(befores),
        out_specs=pl.BlockSpec(memory_space=pltpu.VMEM),
        scratch_shapes=[
            pltpu.VMEM((n, HALF_ROWS + EXTRA, D), jnp.bfloat16),
            pltpu.VMEM((n, HALF_ROWS, 128), jnp.float32),
            pltpu.VMEM((n, HALF_ROWS, 128), jnp.float32),
            pltpu.VMEM((n, 8, HALF_ROWS), jnp.float32),
            pltpu.VMEM((n, 8, HALF_ROWS), jnp.float32),
            pltpu.VMEM((n, HALF_ROWS, 128), jnp.float32),
            pltpu.VMEM((n + 1, 8, HALF_ROWS), jnp.float32),
            pltpu.VMEM((HALF_ROWS, HALF_ROWS), jnp.float32),
            pltpu.VMEM((HALF_ROWS, HALF_ROWS), jnp.float32),
            pltpu.SemaphoreType.DMA((n,)),
        ],
        compiler_params=pltpu.CompilerParams(vmem_limit_bytes=limit),
        cost_estimate=cost(2 * D * HALF_ROWS * HALF_ROWS * len(low), 2 * n * HALF_ROWS * D),
        name=name,
    )(tasks, *[hold[block] for block in blocks], *befores)


def answer_kernel(away, info_ref, values_ref, *refs):
    info, out_ref = info_ref[...], refs[-1]
    group, rank = info[0:1], info[1:2]
    x, y, z, core = where_am_i()
    serving = (core + away) & 1
    here = (group >> 5) == serving
    ring_place, source = jnp.where(serving == 0, x, y), jnp.where(serving == 0, y, x)
    step = jnp.where(source < 2, 1, -1)
    place_of = lax.broadcasted_iota(jnp.int32, (SOURCES, ROWS), 0)
    pick = jnp.where(place_of == jnp.where(here, group & (HALF - 1), -1), 1.0, 0.0).astype(jnp.bfloat16)
    pick = jnp.concatenate([pick] * 3, axis=0)
    lane_of = lax.broadcasted_iota(jnp.int32, (128, ROWS), 0)
    best = refs[0][...] if away else jnp.full((1, ROWS), -1.0, jnp.float32)
    for far in range(3):
        holder = pl.multiple_of(((ring_place + far * step) & 3) * SOURCES, SOURCES)
        parts = jnp.concatenate(three_parts(values_ref[pl.ds(holder, SOURCES), :]), axis=0)
        found = lax.dot_general(parts, pick, (((0,), (0,)), ((), ())), preferred_element_type=jnp.float32)
        wanted = jnp.where(here, (far & 1) * 64 + away * CAP + rank, -1)
        found = jnp.max(jnp.where(lane_of == wanted, found, -1.0), axis=0, keepdims=True)
        best = jnp.maximum(best, found)
    out_ref[...] = best


def answer(away, info, values, *before):
    return pl.pallas_call(
        functools.partial(answer_kernel, away),
        out_shape=jax.ShapeDtypeStruct((1, ROWS), jnp.float32),
        in_specs=[pl.BlockSpec(memory_space=pltpu.VMEM)] * (2 + len(before)),
        out_specs=pl.BlockSpec(memory_space=pltpu.VMEM),
        compiler_params=pltpu.CompilerParams(vmem_limit_bytes=VMEM),
        cost_estimate=cost(2 * 3 * 3 * 128 * 128 * ROWS, 4 * 128 * 128),
        name="answer",
    )(info, values, *before)


def local(embeddings, cluster_ids, member_order):
    ids, order = cluster_ids.reshape(1, ROWS), member_order.reshape(1, ROWS)

    box, info = prep(embeddings, ids, order)
    chunk1 = exchange(box, ROUTES)
    handed = send(hand(embeddings, info, ids, order), SIBLING)
    chunk1, handed = lax.optimization_barrier((chunk1, handed))
    chunk2 = exchange(handed, ROUTES)

    hold = {}

    def ring_blocks(far, chunk, blocks):
        hold["P", far, chunk], hold["M", far, chunk] = blocks
        return blocks

    def onward(blocks):
        return send(blocks[0], ring(1)), send(blocks[1], ring(-1))

    pairs, by_place = pair_lists()
    pairs += [((part, 0, chunk),) * 2 for part in "PM" for chunk in range(2)]

    def run(stage, name, befores=()):
        low = [pair for pair in pairs if stage_of(pair) == stage]
        low.sort(key=lambda pair: sum(chunk == 0 for part, far, chunk in pair))
        high = list(low)
        for one, other in by_place:
            if stage_of(one) == stage:
                low.append(one)
                high.append(other)
        limit, start = ((PAIRS, 0), (OWN, 1), (NEAR, 1), (PAIRS, 0))[stage]
        return similar(hold, low, high, befores, name, limit, start)

    own1 = ring_blocks(0, 0, open_cells(chunk1, True))
    near1 = ring_blocks(1, 0, onward(own1))
    far1 = onward(near1)
    first = run(0, "first")
    chunk2, own1, near1, far1, first = lax.optimization_barrier((chunk2, own1, near1, far1, first))
    for far, blocks in enumerate((own1, near1, far1)):
        ring_blocks(far, 0, blocks)
    own2 = ring_blocks(0, 1, open_cells(chunk2, False))
    near2 = onward(own2)
    own = run(1, "own")
    near2, own = lax.optimization_barrier((near2, own))
    ring_blocks(1, 1, near2)
    ring_blocks(2, 1, onward(near2))
    near = run(2, "near")
    last = run(3, "far", (first, own, near))
    mine = exchange(last.reshape(CHIPS, 1, 128), RETURNS).reshape(CHIPS, 128)
    best = answer(0, info, mine)
    return answer(1, info, send(mine, SIBLING), best).reshape(ROWS)


def solution(mesh):
    return jax.shard_map(
        local,
        mesh=mesh,
        in_specs=(P(AXES, None), P(AXES), P(AXES)),
        out_specs=P(AXES),
        check_vma=False,
    )
```
